512 devices in a mesh: seq: 64 (over y, z_lo, core), head: 8 (over x, z_hi).
Axes of the slice: x: 4, y: 8, z: 8 (z_hi: 2, z_lo: 4; z = z_hi * 4 + z_lo), core: 2. Of those that a mesh axis runs over, the one named last changes fastest.
Arguments:
- query_pre: bfloat16 [16384, 5120], P('seq', 'head'), may hold values from -250 to 250
- key_pre: bfloat16 [16384, 5120], P('seq', 'head'), may hold values from -250 to 250
- value: bfloat16 [16384, 5120], P('seq', 'head'), may hold values from -6 to 6
- d_out: bfloat16 [16384, 5120], P('seq', 'head'), may hold values from -96 to 96
- gain_q: bfloat16 [5120], P('head'), may hold values from 0.25 to 1.75
- gain_k: bfloat16 [5120], P('head'), may hold values from 0.25 to 1.75
- head_class: int32 [40], P('head'), may hold values from 0 to 1, as said below
- head_band: int32 [40], P('head'), may hold values from 0 to 1, as said below
Outputs:
- d_query: bfloat16 [16384, 5120], P('seq', 'head')
- d_key: bfloat16 [16384, 5120], P('seq', 'head')
- d_value: bfloat16 [16384, 5120], P('seq', 'head')
The draws below stay inside these ranges and needn't reach their ends.
Inputs may be any that keep to these rules, and one draw needn't show every extreme that they name: `head_class`: each group of 5 consecutive heads holds exactly 3 spatial heads (0) and 2 temporal heads (1). `head_band`: temporal heads hold 0; each group of 5 consecutive heads has a spatial head with 0 and one with 1.
All inputs are finite; a program needn't handle non-finite values.
Results may differ from the reference program's by a relative error of at most 0.0095.
The reference program's roundings to bfloat16 on the way count: a program that leaves them out, or rounds other values in their place, can miss the bound.
Values may be sent and summed in bfloat16 or wider, within the bound.
No kernel may reach another device: no remote copies, remote signals or barrier semaphores. Data moves between devices by JAX's collectives and lax.ppermute only.
A program may use at most 64 MiB of HBM per device.

```python
import math
import jax
import jax.numpy as jnp
from jax import lax

HD = 128
SPAT_DEV = 3
H_DEV = 5
HEADS = 40
D = 5120
TILE = 4
FRAMES = 64
TOKF = 256
TOKENS = 16384


def head_plan(key):
    group_count = HEADS // H_DEV
    subkeys = jax.random.split(key, 2)
    ranking = jax.random.randint(subkeys[0], (group_count, H_DEV), 0, 1 << 20) * H_DEV + jnp.arange(H_DEV, dtype=jnp.int32)[None, :]
    ranks = jnp.argsort(jnp.argsort(ranking, axis=1, stable=True), axis=1, stable=True).astype(jnp.int32)
    head_kind = (ranks >= SPAT_DEV).astype(jnp.int32)
    picked = jax.random.randint(subkeys[1], (group_count, H_DEV), 0, 2)
    widths = jnp.where(ranks == 0, 0, jnp.where(ranks == 1, 1, picked)) * (1 - head_kind)
    return (head_kind.reshape(-1), widths.astype(jnp.int32).reshape(-1))


def draw_head_class(key, part):
    head_kind, widths = head_plan(key)
    return head_kind


def draw_head_band(key, part):
    head_kind, widths = head_plan(key)
    return widths


def feature_scales(key):
    columns = HEADS * HD
    group_of = (jnp.arange(columns) // (H_DEV * HD)).astype(jnp.float32)
    ramp_up = jnp.sqrt(3.0 ** (group_of / max(HEADS // H_DEV - 1, 1)))
    spread = jax.random.uniform(key, (columns,), minval=-1.15, maxval=1.15)
    return ramp_up * jnp.exp(spread)


def draw_query_pre(key, part):
    key = jax.random.fold_in(key, 21)
    subkeys = jax.random.split(key, 3)
    columns = HEADS * HD
    raw_draw = jnp.clip(jax.random.normal(subkeys[0], (TOKENS, columns)), -4.0, 4.0)
    row_scale = jnp.exp(jax.random.uniform(subkeys[1], (TOKENS, 1), minval=0.0, maxval=1.15))
    return (raw_draw * row_scale * feature_scales(subkeys[2])[None, :]).astype(jnp.bfloat16)


def draw_key_pre(key, part):
    key = jax.random.fold_in(key, 22)
    subkeys = jax.random.split(key, 3)
    columns = HEADS * HD
    raw_draw = jnp.clip(jax.random.normal(subkeys[0], (TOKENS, columns)), -4.0, 4.0)
    row_scale = jnp.exp(jax.random.uniform(subkeys[1], (TOKENS, 1), minval=0.0, maxval=1.15))
    return (raw_draw * row_scale * feature_scales(subkeys[2])[None, :]).astype(jnp.bfloat16)


def block_scale(key, extent, pieces, least, high):
    def one(axis_at, shards_of):
        heights = jax.random.uniform(jax.random.fold_in(jax.random.fold_in(key, 6), axis_at), (shards_of,), jnp.float32, least / len(pieces), high / len(pieces))
        return jnp.repeat(jnp.exp(heights), extent[axis_at] // shards_of).reshape((-1,) + (1,) * (len(extent) - axis_at - 1))

    factor_of = one(*pieces[0])
    for cut in pieces[1:]:
        factor_of = factor_of * one(*cut)
    return factor_of


def bell_draw(rng, extent, scale, limit, pieces=(), held_as=jnp.bfloat16):
    level = block_scale(rng, extent, pieces, -0.22, 0.18) if pieces else 1.0
    entries = jax.random.normal(rng, extent, jnp.float32) * scale * level
    return jnp.minimum(jnp.maximum(entries, -limit), limit).astype(held_as)


def setup_inputs(seed: int = 0) -> dict:
    arg_keys = jax.random.split(jax.random.key(seed), 9)
    query_pre = draw_query_pre(jax.random.fold_in(arg_keys[8], 71), 0)
    key_pre = draw_key_pre(jax.random.fold_in(arg_keys[8], 71), 0)
    value = bell_draw(arg_keys[2], (TOKENS, D), 1.0, 6.0, ((0, 64), (1, 8)))
    d_out = bell_draw(arg_keys[3], (TOKENS, D), 16.0, 96.0, ((0, 64), (1, 8)))
    gain_q = jnp.clip(1.0 + 0.15 * jax.random.normal(arg_keys[4], (D,), jnp.float32), 0.25, 1.75).astype(jnp.bfloat16)
    gain_k = jnp.clip(1.0 + 0.15 * jax.random.normal(arg_keys[5], (D,), jnp.float32), 0.25, 1.75).astype(jnp.bfloat16)
    head_class = draw_head_class(jax.random.fold_in(arg_keys[8], 71), 0)
    head_band = draw_head_band(jax.random.fold_in(arg_keys[8], 71), 0)
    return dict(query_pre=query_pre, key_pre=key_pre, value=value, d_out=d_out, gain_q=gain_q, gain_k=gain_k, head_class=head_class, head_band=head_band)


EPSILON = 1e-06

def normalize(inputs, gain):
    wide_in = inputs.astype(jnp.float32)
    inverse = lax.rsqrt(lax.optimization_barrier(jnp.mean(wide_in * wide_in, axis=-1, keepdims=True)) + EPSILON)
    return ((wide_in * inverse * gain.astype(jnp.float32)).astype(jnp.bfloat16), inverse)

def normalize_grad(inputs, gain, inverse, upstream):
    wide_in = inputs.astype(jnp.float32)
    gain_f = gain.astype(jnp.float32)
    grad_f = upstream.astype(jnp.float32)
    inner_sums = lax.optimization_barrier(jnp.sum(gain_f * grad_f * wide_in, axis=-1, keepdims=True))
    cubed = inverse * inverse * inverse
    return (inverse * gain_f * grad_f - wide_in * cubed * inner_sums / wide_in.shape[-1]).astype(jnp.bfloat16)

def block_grads(q_rows, k_rows, v_rows, g_rows, allowed):
    scaling = 1.0 / math.sqrt(HD)
    scores = jnp.dot(q_rows, k_rows.T, preferred_element_type=jnp.float32) * scaling
    scores = jnp.where(allowed, scores, -1e+30)
    largest = lax.optimization_barrier(jnp.max(scores, axis=-1, keepdims=True))
    powers = jnp.where(allowed, jnp.exp(scores - largest), 0.0)
    attention = powers / lax.optimization_barrier(jnp.sum(powers, axis=-1, keepdims=True))
    d_attention = jnp.dot(g_rows, v_rows.T, preferred_element_type=jnp.float32)
    deltas = lax.optimization_barrier(jnp.sum(attention * d_attention, axis=-1, keepdims=True))
    d_scores = (attention * (d_attention - deltas)).astype(jnp.bfloat16)
    attention_b = attention.astype(jnp.bfloat16)
    d_q = jnp.dot(d_scores, k_rows, preferred_element_type=jnp.float32) * scaling
    d_k = jnp.dot(d_scores.T, q_rows, preferred_element_type=jnp.float32) * scaling
    d_v = jnp.dot(attention_b.T, g_rows, preferred_element_type=jnp.float32)
    return (d_q, d_k, d_v)

def gather_frames(partial_value):
    zeros_row = jnp.zeros((1, TOKF, HD), dtype=partial_value.dtype)
    from_below = jnp.concatenate([partial_value[1:, 0], zeros_row], axis=0)
    from_above = jnp.concatenate([zeros_row, partial_value[:-1, 2]], axis=0)
    return partial_value[:, 1] + from_below + from_above

def spatial_head(q_rows, k_rows, v_rows, g_rows, band_width):
    k_pad = jnp.pad(k_rows, ((1, 1), (0, 0), (0, 0)))
    v_pad = jnp.pad(v_rows, ((1, 1), (0, 0), (0, 0)))
    offsets = jnp.arange(3 * TOKF, dtype=jnp.int32) // TOKF - 1

    def one_frame(frame_at):
        k_win = lax.dynamic_slice_in_dim(k_pad, frame_at, 3, 0).reshape(3 * TOKF, HD)
        v_win = lax.dynamic_slice_in_dim(v_pad, frame_at, 3, 0).reshape(3 * TOKF, HD)
        target = frame_at + offsets
        allowed = ((jnp.abs(offsets) <= band_width) & (target >= 0) & (target < FRAMES))[None, :]
        q_here = lax.dynamic_index_in_dim(q_rows, frame_at, 0, keepdims=False)
        g_here = lax.dynamic_index_in_dim(g_rows, frame_at, 0, keepdims=False)
        d_q, d_k, d_v = block_grads(q_here, k_win, v_win, g_here, allowed)
        return (d_q, d_k.reshape(3, TOKF, HD), d_v.reshape(3, TOKF, HD))
    d_q, d_k, d_v = lax.map(one_frame, jnp.arange(FRAMES, dtype=jnp.int32))
    return (d_q.astype(jnp.bfloat16), gather_frames(d_k).astype(jnp.bfloat16), gather_frames(d_v).astype(jnp.bfloat16))

def temporal_head(q_rows, k_rows, v_rows, g_rows, band_width):
    tile_count = TOKF // TILE

    def to_tiles(values):
        return values.reshape(FRAMES, tile_count, TILE, HD).transpose(1, 0, 2, 3).reshape(tile_count, FRAMES * TILE, HD)

    def from_tiles(values):
        return values.reshape(tile_count, FRAMES, TILE, HD).transpose(1, 0, 2, 3).reshape(FRAMES, TOKF, HD)
    allowed = jnp.ones((1, FRAMES * TILE), dtype=bool)

    def one_tile(blocks):
        return block_grads(blocks[0], blocks[1], blocks[2], blocks[3], allowed)
    d_q, d_k, d_v = lax.map(one_tile, (to_tiles(q_rows), to_tiles(k_rows), to_tiles(v_rows), to_tiles(g_rows)))
    return (from_tiles(d_q).astype(jnp.bfloat16), from_tiles(d_k).astype(jnp.bfloat16), from_tiles(d_v).astype(jnp.bfloat16))

def reference(query_pre, key_pre, value, d_out, gain_q, gain_k, head_class, head_band):
    q_norm, q_inverse = normalize(query_pre, gain_q)
    k_norm, k_inverse = normalize(key_pre, gain_k)

    def split_heads(values):
        return values.reshape(FRAMES, TOKF, HEADS, HD).transpose(2, 0, 1, 3)

    def one_head(blocks):
        q_rows, k_rows, v_rows, g_rows, head_kind, band_width = blocks
        return lax.switch(head_kind, [spatial_head, temporal_head], q_rows, k_rows, v_rows, g_rows, band_width)
    d_q, d_k, d_v = lax.map(one_head, (split_heads(q_norm), split_heads(k_norm), split_heads(value), split_heads(d_out), head_class, head_band))

    def join_heads(values):
        return values.transpose(1, 2, 0, 3).reshape(TOKENS, HEADS * HD)
    return (normalize_grad(query_pre, gain_q, q_inverse, join_heads(d_q)), normalize_grad(key_pre, gain_k, k_inverse, join_heads(d_k)), join_heads(d_v))
```

```python
import functools
import math

import jax
import jax.numpy as jnp
from jax import lax
from jax.experimental import pallas as pl
from jax.experimental.pallas import tpu as pltpu
from jax.sharding import PartitionSpec as P

HD = 128
TOK = 256
HEADS_DEV = 5
FRAMES = 64
WIDTH = HEADS_DEV * HD
FULL = 5120
EPSILON = 1e-06
SCALE = 1.0 / math.sqrt(HD)
NEG = -1e30

BF = jnp.bfloat16
F32 = jnp.float32
VM = pl.BlockSpec(memory_space=pltpu.VMEM)
SM = pl.BlockSpec(memory_space=pltpu.SMEM)


def shape(dims, dtype):
    return jax.ShapeDtypeStruct(dims, dtype)


def call(body, outs, specs, name, micros, mib=24):
    return pl.pallas_call(
        body,
        out_shape=outs,
        in_specs=specs,
        out_specs=jax.tree.map(lambda _: VM, outs),
        name=name,
        compiler_params=pltpu.CompilerParams(vmem_limit_bytes=mib << 20),
        cost_estimate=pl.CostEstimate(
            flops=int(micros * 1e9), bytes_accessed=int(micros * 1e6), transcendentals=0
        ),
    )


def head_slots(cls_ref, band_ref):
    kinds = [cls_ref[i] for i in range(HEADS_DEV)]
    bands = [band_ref[i] for i in range(HEADS_DEV)]
    zero = jnp.int32(0)
    first = zero
    for i in reversed(range(HEADS_DEV)):
        first = jnp.where((kinds[i] == 0) & (bands[i] == 0), i, first)
    second, third, band_2, band_3, temp_0, temp_1 = zero, zero, zero, zero, zero, zero
    for i in reversed(range(HEADS_DEV)):
        other = (kinds[i] == 0) & (first != i)
        second = jnp.where(other, i, second)
        band_2 = jnp.where(other, bands[i], band_2)
        temp_0 = jnp.where(kinds[i] != 0, i, temp_0)
    for i in range(HEADS_DEV):
        other = (kinds[i] == 0) & (first != i)
        third = jnp.where(other, i, third)
        band_3 = jnp.where(other, bands[i], band_3)
        temp_1 = jnp.where(kinds[i] != 0, i, temp_1)
    return (first, second, third, temp_0, temp_1), (band_2, band_3)


def columns(slot):
    return pl.ds(pl.multiple_of(slot * HD, HD), HD)


def dot_nt(a, b, precision=None):
    return lax.dot_general(
        a, b, (((1,), (1,)), ((), ())), preferred_element_type=F32, precision=precision
    )


def dot_tn(a, b):
    return lax.dot_general(a, b, (((0,), (0,)), ((), ())), preferred_element_type=F32)


def dot_nn(a, b):
    return lax.dot_general(a, b, (((1,), (0,)), ((), ())), preferred_element_type=F32)


def rows_of(q_row, k_row):
    at = lax.broadcasted_iota(jnp.int32, (8, HD), 0)
    return jnp.where(
        at == 0,
        q_row[:, :HD],
        jnp.where(at == 1, q_row[:, HD:], jnp.where(at == 2, k_row[:, :HD], k_row[:, HD:])),
    )


def spread(rows, at):
    low = jnp.broadcast_to(rows[at : at + 1], (HD, HD)).T
    high = jnp.broadcast_to(rows[at + 1 : at + 2], (HD, HD)).T
    return jnp.concatenate([low, high], axis=0)


def lane_sums(values):
    return dot_nt(jnp.ones((8, HD), F32), values, lax.Precision.HIGHEST)


def inverses(sums_ref):
    return lax.rsqrt(jnp.sum(sums_ref[...], axis=0) / FULL + EPSILON)


def squares_body(q_ref, k_ref, out_ref):
    sums = []
    for ref in (q_ref, k_ref):
        total = jnp.zeros((TOK, HD), F32)
        for head in range(HEADS_DEV):
            wide = ref[:, head * HD : (head + 1) * HD].astype(F32)
            total += wide * wide
        sums.append(lane_sums(total))
    out_ref[...] = jnp.broadcast_to(rows_of(*sums)[None], (8, 8, HD))


def norm_body(
    cls_ref, band_ref, sums_ref, gain_ref, q_ref, k_ref, v_ref, g_ref, send_ref, halo_ref, qs_ref, ks_ref
):
    slots, _ = head_slots(cls_ref, band_ref)
    inv = inverses(sums_ref)
    q_inv, k_inv = spread(inv, 0), spread(inv, 2)

    def normed(ref, inverse, which, slot):
        gain = gain_ref[which, pl.ds(slot, 1), :]
        return (ref[:, columns(slot)].astype(F32) * inverse * gain).astype(BF)

    for s in range(2):
        slot = slots[3 + s]
        parts = (
            normed(q_ref, q_inv, 0, slot),
            normed(k_ref, k_inv, 1, slot),
            v_ref[:, columns(slot)],
            g_ref[:, columns(slot)],
        )
        for a, part in enumerate(parts):
            send_ref[s * 32 : (s + 1) * 32, a] = part.reshape(32, 8, HD)
    for s in range(3):
        slot = slots[s]
        qs_ref[s] = normed(q_ref, q_inv, 0, slot)
        k_norm = normed(k_ref, k_inv, 1, slot)
        if s == 0:
            ks_ref[...] = k_norm
        else:
            halo_ref[2 * s - 2] = k_norm
            halo_ref[2 * s - 1] = v_ref[:, columns(slot)]


def attend(q, g, keys, values, allowed):
    scores = []
    for key, ok in zip(keys, allowed):
        score = dot_nt(key, q) * SCALE
        scores.append(score if ok is None else jnp.where(ok, score, NEG))
    largest = functools.reduce(
        jnp.maximum, [jnp.max(score, axis=0, keepdims=True) for score in scores]
    )
    powers = [jnp.exp(score - largest) for score in scores]
    totals = sum(jnp.sum(power, axis=0, keepdims=True) for power in powers)
    inverse = 1.0 / totals
    probs = [power * inverse for power in powers]
    d_probs = [dot_nt(value, g) for value in values]
    deltas = sum(jnp.sum(p * d, axis=0, keepdims=True) for p, d in zip(probs, d_probs))
    d_scores = [(p * (d - deltas)).astype(BF) for p, d in zip(probs, d_probs)]
    d_q = sum(dot_tn(d, key) for d, key in zip(d_scores, keys)) * SCALE
    d_keys = [dot_nn(d, q) * SCALE for d in d_scores]
    d_values = [dot_nn(p.astype(BF), g) for p in probs]
    return d_q, d_keys, d_values


def spatial_body(
    cls_ref,
    band_ref,
    frame_ref,
    qs_ref,
    ks_ref,
    halo_ref,
    low_ref,
    high_ref,
    v_ref,
    g_ref,
    dq_ref,
    fin_ref,
    own_ref,
    to_low_ref,
    to_high_ref,
):
    slots, bands = head_slots(cls_ref, band_ref)
    frame = frame_ref[0]
    d_q, d_k, d_v = attend(
        qs_ref[0], g_ref[:, columns(slots[0])], [ks_ref[...]], [v_ref[:, columns(slots[0])]], [None]
    )
    dq_ref[0] = d_q.astype(BF)
    fin_ref[0] = d_k[0].astype(BF)
    fin_ref[1] = d_v[0].astype(BF)
    for s in (1, 2):
        at = 2 * s - 2
        wide = bands[s - 1] > 0
        g = g_ref[:, columns(slots[s])]
        keys = [low_ref[at], halo_ref[at], high_ref[at]]
        values = [low_ref[at + 1], halo_ref[at + 1], high_ref[at + 1]]
        allowed = [wide & (frame > 0), None, wide & (frame < FRAMES - 1)]
        d_q, d_k, d_v = attend(qs_ref[s], g, keys, values, allowed)
        dq_ref[s] = d_q.astype(BF)
        to_low_ref[at] = d_k[0].astype(BF)
        to_low_ref[at + 1] = d_v[0].astype(BF)
        own_ref[at] = d_k[1]
        own_ref[at + 1] = d_v[1]
        to_high_ref[at] = d_k[2].astype(BF)
        to_high_ref[at + 1] = d_v[2].astype(BF)


def temporal_body(in_ref, out_ref):
    rows = FRAMES * 8
    q, k, v, g = (in_ref[:, a].reshape(rows, HD) for a in range(4))
    d_k = jnp.zeros((rows, HD), F32)
    d_v = jnp.zeros((rows, HD), F32)
    step = 256
    for part in range(rows // step):
        q_part, g_part = q[part * step : (part + 1) * step], g[part * step : (part + 1) * step]
        key_tile = lax.broadcasted_iota(jnp.int32, (rows, step), 0) & 4
        query_tile = lax.broadcasted_iota(jnp.int32, (rows, step), 1) & 4
        d_q, d_keys, d_values = attend(q_part, g_part, [k], [v], [key_tile == query_tile])
        frames = step // 8
        out_ref[part * frames : (part + 1) * frames, 0] = d_q.astype(BF).reshape(frames, 8, HD)
        d_k += d_keys[0]
        d_v += d_values[0]
    out_ref[:, 1] = d_k.astype(BF).reshape(FRAMES, 8, HD)
    out_ref[:, 2] = d_v.astype(BF).reshape(FRAMES, 8, HD)


def product(gain_ref, which, slot, grad, ref):
    gain = gain_ref[which, pl.ds(slot, 1), :]
    return gain * grad.astype(F32) * ref[:, columns(slot)].astype(F32)


def spatial_sums_body(
    cls_ref, band_ref, gain_ref, q_ref, k_ref, dq_ref, fin_ref, own_ref, low_ref, high_ref, grad_ref, part_ref
):
    slots, _ = head_slots(cls_ref, band_ref)
    q_total = product(gain_ref, 0, slots[0], dq_ref[0], q_ref)
    k_total = product(gain_ref, 1, slots[0], fin_ref[0], k_ref)
    for s in (1, 2):
        for b in range(2):
            at = 2 * s - 2 + b
            grad_ref[at] = (
                own_ref[at] + low_ref[at].astype(F32) + high_ref[at].astype(F32)
            ).astype(BF)
        q_total += product(gain_ref, 0, slots[s], dq_ref[s], q_ref)
        k_total += product(gain_ref, 1, slots[s], grad_ref[2 * s - 2], k_ref)
    part_ref[0] = q_total
    part_ref[1] = k_total


def inner_body(cls_ref, band_ref, gain_ref, q_ref, k_ref, back_ref, part_ref, out_ref):
    slots, _ = head_slots(cls_ref, band_ref)
    sums = []
    for which, ref in enumerate((q_ref, k_ref)):
        total = part_ref[which]
        for s in range(2):
            grad = back_ref[s * 32 : (s + 1) * 32, which].reshape(TOK, HD)
            total += product(gain_ref, which, slots[3 + s], grad, ref)
        sums.append(lane_sums(total))
    out_ref[...] = jnp.broadcast_to(rows_of(*sums)[None], (8, 8, HD))


def final_body(
    cls_ref,
    band_ref,
    gain_ref,
    sums_ref,
    inner_ref,
    q_ref,
    k_ref,
    back_ref,
    dq_ref,
    fin_ref,
    grad_ref,
    out_q_ref,
    out_k_ref,
    out_v_ref,
):
    slots, _ = head_slots(cls_ref, band_ref)
    inv = inverses(sums_ref)
    pull = inv * inv * inv * jnp.sum(inner_ref[...], axis=0) / FULL
    for which, (ref, out) in enumerate(((q_ref, out_q_ref), (k_ref, out_k_ref))):
        inverse, pulled = spread(inv, 2 * which), spread(pull, 2 * which)
        for s in range(HEADS_DEV):
            if s >= 3:
                grad = back_ref[(s - 3) * 32 : (s - 2) * 32, which].reshape(TOK, HD)
            elif which == 0:
                grad = dq_ref[s]
            else:
                grad = fin_ref[0] if s == 0 else grad_ref[2 * s - 2]
            gain = gain_ref[which, pl.ds(slots[s], 1), :]
            at = columns(slots[s])
            out[:, at] = (
                inverse * gain * grad.astype(F32) - ref[:, at].astype(F32) * pulled
            ).astype(BF)
    out_v_ref[:, columns(slots[0])] = fin_ref[1]
    for s in (1, 2):
        out_v_ref[:, columns(slots[s])] = grad_ref[2 * s - 1]
    for s in range(2):
        out_v_ref[:, columns(slots[3 + s])] = back_ref[s * 32 : (s + 1) * 32, 2].reshape(TOK, HD)


def per_device(query_pre, key_pre, value, d_out, gain_q, gain_k, head_class, head_band):
    gains = jnp.stack([gain_q, gain_k]).astype(F32).reshape(2, HEADS_DEV, HD)
    frame = lax.axis_index("seq").astype(jnp.int32).reshape(1)
    up = [(i, i + 1) for i in range(FRAMES - 1)]
    down = [(i + 1, i) for i in range(FRAMES - 1)]
    block = (4, TOK, HD)

    sums = call(squares_body, shape((8, 8, HD), F32), [VM] * 2, "squares", 2)(query_pre, key_pre)
    sums = lax.all_to_all(sums, "head", 0, 0, tiled=True)
    send, halo, qs, ks = call(
        norm_body,
        (
            shape((FRAMES, 4, 8, HD), BF),
            shape(block, BF),
            shape((3, TOK, HD), BF),
            shape((TOK, HD), BF),
        ),
        [SM, SM] + [VM] * 6,
        "norm",
        3,
    )(head_class, head_band, sums, gains, query_pre, key_pre, value, d_out)
    held = lax.all_to_all(send, "seq", 0, 0, tiled=True)
    low = lax.ppermute(halo, "seq", up)
    high = lax.ppermute(halo, "seq", down)
    dq, fin, own, to_low, to_high = call(
        spatial_body,
        (
            shape((3, TOK, HD), BF),
            shape((2, TOK, HD), BF),
            shape(block, F32),
            shape(block, BF),
            shape(block, BF),
        ),
        [SM] * 3 + [VM] * 7,
        "spatial",
        6,
    )(head_class, head_band, frame, qs, ks, halo, low, high, value, d_out)
    from_low = lax.ppermute(to_high, "seq", up)
    from_high = lax.ppermute(to_low, "seq", down)
    grads = call(temporal_body, shape((FRAMES, 3, 8, HD), BF), [VM], "temporal", 3)(held)
    back = lax.all_to_all(grads, "seq", 0, 0, tiled=True)
    grad, part = call(
        spatial_sums_body,
        (shape(block, BF), shape((2, TOK, HD), F32)),
        [SM, SM] + [VM] * 8,
        "spatial_sums",
        3,
    )(head_class, head_band, gains, query_pre, key_pre, dq, fin, own, from_low, from_high)
    inner = call(
        inner_body, shape((8, 8, HD), F32), [SM, SM] + [VM] * 5, "inner", 2
    )(head_class, head_band, gains, query_pre, key_pre, back, part)
    inner = lax.all_to_all(inner, "head", 0, 0, tiled=True)
    return call(
        final_body,
        (shape((TOK, WIDTH), BF),) * 3,
        [SM, SM] + [VM] * 9,
        "final",
        3,
    )(head_class, head_band, gains, sums, inner, query_pre, key_pre, back, dq, fin, grad)


def solution(mesh):
    whole = P("seq", "head")
    return jax.shard_map(
        per_device,
        mesh=mesh,
        in_specs=(whole,) * 4 + (P("head"),) * 4,
        out_specs=(whole,) * 3,
        check_vma=False,
    )
```

```python
import functools
import math

import jax
import jax.numpy as jnp
from jax import lax
from jax.experimental import pallas as pl
from jax.experimental.pallas import tpu as pltpu
from jax.sharding import PartitionSpec as P

HD = 128
TOK = 256
HEADS_DEV = 5
FRAMES = 64
WIDTH = HEADS_DEV * HD
FULL = 5120
EPSILON = 1e-06
SCALE = 1.0 / math.sqrt(HD)
NEG = -1e30
LOG2E = math.log2(math.e)

BF = jnp.bfloat16
F32 = jnp.float32
VM = pl.BlockSpec(memory_space=pltpu.VMEM)
SM = pl.BlockSpec(memory_space=pltpu.SMEM)
ANY = pl.BlockSpec(memory_space=pl.ANY)


def shape(dims, dtype):
    return jax.ShapeDtypeStruct(dims, dtype)


def call(body, outs, specs, name, micros, mib=24):
    return pl.pallas_call(
        body,
        out_shape=outs,
        in_specs=specs,
        out_specs=jax.tree.map(lambda _: VM, outs),
        name=name,
        compiler_params=pltpu.CompilerParams(vmem_limit_bytes=mib << 20),
        cost_estimate=pl.CostEstimate(
            flops=int(micros * 1e9), bytes_accessed=int(micros * 1e6), transcendentals=0
        ),
    )


def head_slots(cls_ref, band_ref):
    kinds = [cls_ref[i] for i in range(HEADS_DEV)]
    bands = [band_ref[i] for i in range(HEADS_DEV)]
    zero = jnp.int32(0)
    first = zero
    for i in reversed(range(HEADS_DEV)):
        first = jnp.where((kinds[i] == 0) & (bands[i] == 0), i, first)
    second, third, band_2, band_3, temp_0, temp_1 = zero, zero, zero, zero, zero, zero
    for i in reversed(range(HEADS_DEV)):
        other = (kinds[i] == 0) & (first != i)
        second = jnp.where(other, i, second)
        band_2 = jnp.where(other, bands[i], band_2)
        temp_0 = jnp.where(kinds[i] != 0, i, temp_0)
    for i in range(HEADS_DEV):
        other = (kinds[i] == 0) & (first != i)
        third = jnp.where(other, i, third)
        band_3 = jnp.where(other, bands[i], band_3)
        temp_1 = jnp.where(kinds[i] != 0, i, temp_1)
    return (first, second, third, temp_0, temp_1), (band_2, band_3)


def columns(slot):
    return pl.ds(pl.multiple_of(slot * HD, HD), HD)


def dot_nt(a, b, precision=None):
    return lax.dot_general(
        a, b, (((1,), (1,)), ((), ())), preferred_element_type=F32, precision=precision
    )


def dot_tn(a, b):
    return lax.dot_general(a, b, (((0,), (0,)), ((), ())), preferred_element_type=F32)


def dot_nn(a, b):
    return lax.dot_general(a, b, (((1,), (0,)), ((), ())), preferred_element_type=F32)


def rows_of(q_row, k_row):
    at = lax.broadcasted_iota(jnp.int32, (8, HD), 0)
    return jnp.where(
        at == 0,
        q_row[:, :HD],
        jnp.where(at == 1, q_row[:, HD:], jnp.where(at == 2, k_row[:, :HD], k_row[:, HD:])),
    )


def spread(rows, at):
    low = jnp.broadcast_to(rows[at : at + 1], (HD, HD)).T
    high = jnp.broadcast_to(rows[at + 1 : at + 2], (HD, HD)).T
    return jnp.concatenate([low, high], axis=0)


def lane_sums(values):
    return dot_nt(jnp.ones((8, HD), F32), values, lax.Precision.HIGHEST)


def inverses(sums_ref):
    return lax.rsqrt(jnp.sum(sums_ref[...], axis=0) / FULL + EPSILON)


def squares_body(cls_ref, band_ref, q_hbm, k_hbm, v_hbm, out_ref, halo_ref, q_ref, k_ref, v_ref, sems):
    copies = [
        pltpu.make_async_copy(source, target, sems.at[i])
        for i, (source, target) in enumerate(((q_hbm, q_ref), (k_hbm, k_ref), (v_hbm, v_ref)))
    ]
    for copy in copies:
        copy.start()
    slots, _ = head_slots(cls_ref, band_ref)
    sums = []
    for copy, ref in zip(copies, (q_ref, k_ref)):
        copy.wait()
        total = jnp.zeros((TOK, HD), F32)
        for head in range(HEADS_DEV):
            wide = ref[:, head * HD : (head + 1) * HD].astype(F32)
            total += wide * wide
        sums.append(lane_sums(total))
    out_ref[...] = jnp.broadcast_to(rows_of(*sums)[None], (8, 8, HD))
    copies[2].wait()
    for s in (1, 2):
        halo_ref[2 * s - 2] = k_ref[:, columns(slots[s])]
        halo_ref[2 * s - 1] = v_ref[:, columns(slots[s])]


def gains_body(q_ref, k_ref, after_ref, g_ref, out_ref):
    out_ref[0] = q_ref[...].astype(F32)
    out_ref[1] = k_ref[...].astype(F32)


def normed(values, inverse, gain):
    return (values.astype(F32) * inverse * gain).astype(BF)


def norm_body(
    cls_ref, band_ref, sums_ref, gain_ref, q_ref, k_ref, v_ref, g_ref, after_ref, send_ref, inv_ref
):
    slots, _ = head_slots(cls_ref, band_ref)
    inv = inverses(sums_ref)
    inv_ref[...] = inv
    q_inv, k_inv = spread(inv, 0), spread(inv, 2)
    for s in range(2):
        slot = slots[3 + s]
        at = columns(slot)
        parts = (
            normed(q_ref[:, at], q_inv, gain_ref[0, pl.ds(slot, 1), :]),
            normed(k_ref[:, at], k_inv, gain_ref[1, pl.ds(slot, 1), :]),
            v_ref[:, at],
            g_ref[:, at],
        )
        for a, part in enumerate(parts):
            send_ref[s * 32 : (s + 1) * 32, a] = part.reshape(32, 8, HD)


def attend(q, g, keys, values, allowed):
    scores = []
    for key, ok in zip(keys, allowed):
        score = dot_nt(key, q)
        scores.append(score if ok is None else jnp.where(ok, score, NEG))
    largest = functools.reduce(
        jnp.maximum, [jnp.max(score, axis=0, keepdims=True) for score in scores]
    )
    powers = [jnp.exp2((score - largest) * (SCALE * LOG2E)) for score in scores]
    totals = sum(jnp.sum(power, axis=0, keepdims=True) for power in powers)
    inverse = 1.0 / totals
    probs = [power * inverse for power in powers]
    d_probs = [dot_nt(value, g) for value in values]
    deltas = sum(jnp.sum(p * d, axis=0, keepdims=True) for p, d in zip(probs, d_probs))
    d_scores = [(p * (d - deltas)).astype(BF) for p, d in zip(probs, d_probs)]
    d_q = sum(dot_tn(d, key) for d, key in zip(d_scores, keys)) * SCALE
    d_keys = [dot_nn(d, q) * SCALE for d in d_scores]
    d_values = [dot_nn(p.astype(BF), g) for p in probs]
    return d_q, d_keys, d_values


def spatial_body(
    cls_ref,
    band_ref,
    frame_ref,
    gain_ref,
    inv_ref,
    inv_near_ref,
    inv_far_ref,
    q_ref,
    k_ref,
    v_ref,
    g_ref,
    near_ref,
    far_ref,
    dq_ref,
    fin_ref,
    own_ref,
    to_near_ref,
    to_far_ref,
    done_ref,
):
    done_ref[...] = inv_ref[...]
    slots, bands = head_slots(cls_ref, band_ref)
    frame = frame_ref[0]
    inv = inv_ref[...]
    q_inv, k_inv = spread(inv, 0), spread(inv, 2)
    near_inv, far_inv = spread(inv_near_ref[...], 2), spread(inv_far_ref[...], 2)
    for s in range(3):
        slot = slots[s]
        cols = columns(slot)
        k_gain = gain_ref[1, pl.ds(slot, 1), :]
        q = normed(q_ref[:, cols], q_inv, gain_ref[0, pl.ds(slot, 1), :])
        k = normed(k_ref[:, cols], k_inv, k_gain)
        v, g = v_ref[:, cols], g_ref[:, cols]
        if s == 0:
            d_q, d_k, d_v = attend(q, g, [k], [v], [None])
            fin_ref[0] = d_k[0].astype(BF)
            fin_ref[1] = d_v[0].astype(BF)
        else:
            at = 2 * s - 2
            wide = bands[s - 1] > 0
            keys = [normed(near_ref[at], near_inv, k_gain), k, normed(far_ref[at], far_inv, k_gain)]
            values = [near_ref[at + 1], v, far_ref[at + 1]]
            allowed = [wide, None, wide & (frame > 0) & (frame < FRAMES - 1)]
            d_q, d_k, d_v = attend(q, g, keys, values, allowed)
            to_near_ref[at] = d_k[0].astype(BF)
            to_near_ref[at + 1] = d_v[0].astype(BF)
            own_ref[at] = d_k[1]
            own_ref[at + 1] = d_v[1]
            to_far_ref[at] = d_k[2].astype(BF)
            to_far_ref[at + 1] = d_v[2].astype(BF)
        dq_ref[s] = d_q.astype(BF)


def temporal_body(in_ref, after_ref, out_ref):
    rows = FRAMES * 8
    q, k, v, g = (in_ref[:, a].reshape(rows, HD) for a in range(4))
    d_k = jnp.zeros((rows, HD), F32)
    d_v = jnp.zeros((rows, HD), F32)
    step = 256
    for part in range(rows // step):
        q_part, g_part = q[part * step : (part + 1) * step], g[part * step : (part + 1) * step]
        key_tile = lax.broadcasted_iota(jnp.int32, (rows, step), 0) & 4
        query_tile = lax.broadcasted_iota(jnp.int32, (rows, step), 1) & 4
        d_q, d_keys, d_values = attend(q_part, g_part, [k], [v], [key_tile == query_tile])
        frames = step // 8
        out_ref[part * frames : (part + 1) * frames, 0] = d_q.astype(BF).reshape(frames, 8, HD)
        d_k += d_keys[0]
        d_v += d_values[0]
    out_ref[:, 1] = d_k.astype(BF).reshape(FRAMES, 8, HD)
    out_ref[:, 2] = d_v.astype(BF).reshape(FRAMES, 8, HD)


def product(gain_ref, which, slot, grad, ref):
    gain = gain_ref[which, pl.ds(slot, 1), :]
    return gain * grad.astype(F32) * ref[:, columns(slot)].astype(F32)


def spatial_sums_body(
    cls_ref, band_ref, gain_ref, q_ref, k_ref, dq_ref, fin_ref, own_ref, near_ref, far_ref, grad_ref, part_ref
):
    slots, _ = head_slots(cls_ref, band_ref)
    q_total = product(gain_ref, 0, slots[0], dq_ref[0], q_ref)
    k_total = product(gain_ref, 1, slots[0], fin_ref[0], k_ref)
    for s in (1, 2):
        for b in range(2):
            at = 2 * s - 2 + b
            grad_ref[at] = (
                own_ref[at] + near_ref[at].astype(F32) + far_ref[at].astype(F32)
            ).astype(BF)
        q_total += product(gain_ref, 0, slots[s], dq_ref[s], q_ref)
        k_total += product(gain_ref, 1, slots[s], grad_ref[2 * s - 2], k_ref)
    part_ref[0] = q_total
    part_ref[1] = k_total


def inner_body(cls_ref, band_ref, gain_ref, q_ref, k_ref, back_ref, part_ref, out_ref):
    slots, _ = head_slots(cls_ref, band_ref)
    sums = []
    for which, ref in enumerate((q_ref, k_ref)):
        total = part_ref[which]
        for s in range(2):
            grad = back_ref[s * 32 : (s + 1) * 32, which].reshape(TOK, HD)
            total += product(gain_ref, which, slots[3 + s], grad, ref)
        sums.append(lane_sums(total))
    out_ref[...] = jnp.broadcast_to(rows_of(*sums)[None], (8, 8, HD))


def value_body(cls_ref, band_ref, back_ref, fin_ref, grad_ref, out_ref):
    slots, _ = head_slots(cls_ref, band_ref)
    out_ref[:, columns(slots[0])] = fin_ref[1]
    for s in (1, 2):
        out_ref[:, columns(slots[s])] = grad_ref[2 * s - 1]
    for s in range(2):
        out_ref[:, columns(slots[3 + s])] = back_ref[s * 32 : (s + 1) * 32, 2].reshape(TOK, HD)


def final_body(
    cls_ref,
    band_ref,
    gain_ref,
    inv_ref,
    inner_ref,
    q_ref,
    k_ref,
    back_ref,
    dq_ref,
    fin_ref,
    grad_ref,
    out_q_ref,
    out_k_ref,
):
    slots, _ = head_slots(cls_ref, band_ref)
    inv = inv_ref[...]
    pull = inv * inv * inv * jnp.sum(inner_ref[...], axis=0) / FULL
    for which, (ref, out) in enumerate(((q_ref, out_q_ref), (k_ref, out_k_ref))):
        inverse, pulled = spread(inv, 2 * which), spread(pull, 2 * which)
        for s in range(HEADS_DEV):
            if s >= 3:
                grad = back_ref[(s - 3) * 32 : (s - 2) * 32, which].reshape(TOK, HD)
            elif which == 0:
                grad = dq_ref[s]
            else:
                grad = fin_ref[0] if s == 0 else grad_ref[2 * s - 2]
            gain = gain_ref[which, pl.ds(slots[s], 1), :]
            at = columns(slots[s])
            out[:, at] = (
                inverse * gain * grad.astype(F32) - ref[:, at].astype(F32) * pulled
            ).astype(BF)


def per_device(query_pre, key_pre, value, d_out, gain_q, gain_k, head_class, head_band):
    frame = lax.axis_index("seq").astype(jnp.int32).reshape(1)
    core = [(i, i ^ 1) for i in range(FRAMES)]
    chip = [(i, ((i - 1) ^ 1) + 1) for i in range(1, FRAMES - 1)]
    block = (4, TOK, HD)

    sums, halo = pl.pallas_call(
        squares_body,
        out_shape=(shape((8, 8, HD), F32), shape(block, BF)),
        in_specs=[SM, SM] + [ANY] * 3,
        out_specs=(VM,) * 2,
        scratch_shapes=[pltpu.VMEM((TOK, WIDTH), BF)] * 3 + [pltpu.SemaphoreType.DMA((3,))],
        name="squares",
        compiler_params=pltpu.CompilerParams(vmem_limit_bytes=56 << 20),
    )(head_class, head_band, query_pre, key_pre, value)
    gains = call(gains_body, shape((2, HEADS_DEV, HD), F32), [VM, VM, ANY, VM], "gains", 1)(
        gain_q.reshape(HEADS_DEV, HD), gain_k.reshape(HEADS_DEV, HD), sums, d_out
    )
    near = lax.ppermute(halo, "seq", core)
    far = lax.ppermute(halo, "seq", chip)
    sums = lax.all_to_all(sums, "head", 0, 0, tiled=True)
    send, inv = call(
        norm_body,
        (shape((FRAMES, 4, 8, HD), BF), shape((8, HD), F32)),
        [SM, SM] + [VM] * 6 + [ANY],
        "norm",
        2,
    )(head_class, head_band, sums, gains, query_pre, key_pre, value, d_out, far)
    held = lax.all_to_all(send, "seq", 0, 0, tiled=True)
    inv_near = lax.ppermute(inv, "seq", core)
    inv_far = lax.ppermute(inv, "seq", chip)
    dq, fin, own, to_near, to_far, done = call(
        spatial_body,
        (
            shape((3, TOK, HD), BF),
            shape((2, TOK, HD), BF),
            shape(block, F32),
            shape(block, BF),
            shape(block, BF),
            shape((8, HD), F32),
        ),
        [SM] * 3 + [VM] * 10,
        "spatial",
        4,
    )(
        head_class,
        head_band,
        frame,
        gains,
        inv,
        inv_near,
        inv_far,
        query_pre,
        key_pre,
        value,
        d_out,
        near,
        far,
    )
    from_near = lax.ppermute(to_near, "seq", core)
    from_far = lax.ppermute(to_far, "seq", chip)
    grads = call(temporal_body, shape((FRAMES, 3, 8, HD), BF), [VM, ANY], "temporal", 3)(held, done)
    back = lax.all_to_all(grads, "seq", 0, 0, tiled=True)
    grad, part = call(
        spatial_sums_body,
        (shape(block, BF), shape((2, TOK, HD), F32)),
        [SM, SM] + [VM] * 8,
        "spatial_sums",
        3,
    )(head_class, head_band, gains, query_pre, key_pre, dq, fin, own, from_near, from_far)
    inner = call(inner_body, shape((8, 8, HD), F32), [SM, SM] + [VM] * 5, "inner", 2)(
        head_class, head_band, gains, query_pre, key_pre, back, part
    )
    inner = lax.all_to_all(inner, "head", 0, 0, tiled=True)
    d_value = call(value_body, shape((TOK, WIDTH), BF), [SM, SM] + [VM] * 3, "value", 2)(
        head_class, head_band, back, fin, grad
    )
    d_query, d_key = call(
        final_body, (shape((TOK, WIDTH), BF),) * 2, [SM, SM] + [VM] * 9, "final", 3
    )(head_class, head_band, gains, inv, inner, query_pre, key_pre, back, dq, fin, grad)
    return d_query, d_key, d_value


def solution(mesh):
    whole = P("seq", "head")
    return jax.shard_map(
        per_device,
        mesh=mesh,
        in_specs=(whole,) * 4 + (P("head"),) * 4,
        out_specs=(whole,) * 3,
        check_vma=False,
    )
```

```python
import functools
import math

import jax
import jax.numpy as jnp
from jax import lax
from jax.experimental import pallas as pl
from jax.experimental.pallas import tpu as pltpu
from jax.sharding import PartitionSpec as P

HD = 128
TOK = 256
HEADS_DEV = 5
FRAMES = 64
WIDTH = HEADS_DEV * HD
FULL = 5120
EPSILON = 1e-06
SCALE = 1.0 / math.sqrt(HD)
NEG = -1e30
LOG2E = math.log2(math.e)

BF = jnp.bfloat16
F32 = jnp.float32
VM = pl.BlockSpec(memory_space=pltpu.VMEM)
SM = pl.BlockSpec(memory_space=pltpu.SMEM)
ANY = pl.BlockSpec(memory_space=pl.ANY)


def shape(dims, dtype):
    return jax.ShapeDtypeStruct(dims, dtype)


def call(body, outs, specs, name, micros, mib=24):
    return pl.pallas_call(
        body,
        out_shape=outs,
        in_specs=specs,
        out_specs=jax.tree.map(lambda _: VM, outs),
        name=name,
        compiler_params=pltpu.CompilerParams(vmem_limit_bytes=mib << 20),
        cost_estimate=pl.CostEstimate(
            flops=int(micros * 1e9), bytes_accessed=int(micros * 1e6), transcendentals=0
        ),
    )


def head_slots(cls_ref, band_ref):
    kinds = [cls_ref[i] for i in range(HEADS_DEV)]
    bands = [band_ref[i] for i in range(HEADS_DEV)]
    zero = jnp.int32(0)
    first = zero
    for i in reversed(range(HEADS_DEV)):
        first = jnp.where((kinds[i] == 0) & (bands[i] == 0), i, first)
    second, third, band_2, band_3, temp_0, temp_1 = zero, zero, zero, zero, zero, zero
    for i in reversed(range(HEADS_DEV)):
        other = (kinds[i] == 0) & (first != i)
        second = jnp.where(other, i, second)
        band_2 = jnp.where(other, bands[i], band_2)
        temp_0 = jnp.where(kinds[i] != 0, i, temp_0)
    for i in range(HEADS_DEV):
        other = (kinds[i] == 0) & (first != i)
        third = jnp.where(other, i, third)
        band_3 = jnp.where(other, bands[i], band_3)
        temp_1 = jnp.where(kinds[i] != 0, i, temp_1)
    return (first, second, third, temp_0, temp_1), (band_2, band_3)


def columns(slot):
    return pl.ds(pl.multiple_of(slot * HD, HD), HD)


def dot_nt(a, b, precision=None):
    return lax.dot_general(
        a, b, (((1,), (1,)), ((), ())), preferred_element_type=F32, precision=precision
    )


def dot_tn(a, b):
    return lax.dot_general(a, b, (((0,), (0,)), ((), ())), preferred_element_type=F32)


def dot_nn(a, b):
    return lax.dot_general(a, b, (((1,), (0,)), ((), ())), preferred_element_type=F32)


def rows_of(q_row, k_row):
    at = lax.broadcasted_iota(jnp.int32, (8, HD), 0)
    return jnp.where(
        at == 0,
        q_row[:, :HD],
        jnp.where(at == 1, q_row[:, HD:], jnp.where(at == 2, k_row[:, :HD], k_row[:, HD:])),
    )


def spread(rows, at):
    low = jnp.broadcast_to(rows[at : at + 1], (HD, HD)).T
    high = jnp.broadcast_to(rows[at + 1 : at + 2], (HD, HD)).T
    return jnp.concatenate([low, high], axis=0)


def lane_sums(values):
    return dot_nt(jnp.ones((8, HD), F32), values, lax.Precision.HIGHEST)


def inverses(sums_ref):
    return lax.rsqrt(jnp.sum(sums_ref[...], axis=0) / FULL + EPSILON)


def squares_body(q_hbm, k_hbm, out_ref, q_ref, k_ref, sems):
    copies = [
        pltpu.make_async_copy(source, target, sems.at[i])
        for i, (source, target) in enumerate(((q_hbm, q_ref), (k_hbm, k_ref)))
    ]
    for copy in copies:
        copy.start()
    sums = []
    for copy, ref in zip(copies, (q_ref, k_ref)):
        copy.wait()
        total = jnp.zeros((TOK, HD), F32)
        for head in range(HEADS_DEV):
            wide = ref[:, head * HD : (head + 1) * HD].astype(F32)
            total += wide * wide
        sums.append(lane_sums(total))
    out_ref[...] = jnp.broadcast_to(rows_of(*sums)[None], (8, 8, HD))


def halo_body(cls_ref, band_ref, after_ref, q_ref, k_ref, v_ref, g_ref, halo_ref):
    slots, _ = head_slots(cls_ref, band_ref)
    for s in (1, 2):
        halo_ref[2 * s - 2] = k_ref[:, columns(slots[s])]
        halo_ref[2 * s - 1] = v_ref[:, columns(slots[s])]


def gains_body(q_ref, k_ref, after_ref, out_ref):
    out_ref[0] = q_ref[...].astype(F32)
    out_ref[1] = k_ref[...].astype(F32)


def normed(values, inverse, gain):
    return (values.astype(F32) * inverse * gain).astype(BF)


def norm_body(
    cls_ref, band_ref, sums_ref, gain_ref, q_ref, k_ref, v_ref, g_ref, after_ref, send_ref, inv_ref
):
    slots, _ = head_slots(cls_ref, band_ref)
    inv = inverses(sums_ref)
    inv_ref[...] = inv
    q_inv, k_inv = spread(inv, 0), spread(inv, 2)
    for s in range(2):
        slot = slots[3 + s]
        at = columns(slot)
        parts = (
            normed(q_ref[:, at], q_inv, gain_ref[0, pl.ds(slot, 1), :]),
            normed(k_ref[:, at], k_inv, gain_ref[1, pl.ds(slot, 1), :]),
            v_ref[:, at],
            g_ref[:, at],
        )
        for a, part in enumerate(parts):
            send_ref[s * 32 : (s + 1) * 32, a] = part.reshape(32, 8, HD)


def attend(q, g, keys, values, allowed):
    scores = []
    for key, ok in zip(keys, allowed):
        score = dot_nt(key, q)
        scores.append(score if ok is None else jnp.where(ok, score, NEG))
    largest = functools.reduce(
        jnp.maximum, [jnp.max(score, axis=0, keepdims=True) for score in scores]
    )
    powers = [jnp.exp2((score - largest) * (SCALE * LOG2E)) for score in scores]
    totals = sum(jnp.sum(power, axis=0, keepdims=True) for power in powers)
    inverse = 1.0 / totals
    probs = [power * inverse for power in powers]
    d_probs = [dot_nt(value, g) for value in values]
    deltas = sum(jnp.sum(p * d, axis=0, keepdims=True) for p, d in zip(probs, d_probs))
    d_scores = [(p * (d - deltas)).astype(BF) for p, d in zip(probs, d_probs)]
    d_q = sum(dot_tn(d, key) for d, key in zip(d_scores, keys)) * SCALE
    d_keys = [dot_nn(d, q) * SCALE for d in d_scores]
    d_values = [dot_nn(p.astype(BF), g) for p in probs]
    return d_q, d_keys, d_values


def spatial_body(
    cls_ref,
    band_ref,
    frame_ref,
    gain_ref,
    inv_ref,
    inv_near_ref,
    inv_far_ref,
    q_ref,
    k_ref,
    v_ref,
    g_ref,
    near_ref,
    far_ref,
    dq_ref,
    fin_ref,
    own_ref,
    to_near_ref,
    to_far_ref,
):
    slots, bands = head_slots(cls_ref, band_ref)
    frame = frame_ref[0]
    inv = inv_ref[...]
    q_inv, k_inv = spread(inv, 0), spread(inv, 2)
    near_inv, far_inv = spread(inv_near_ref[...], 2), spread(inv_far_ref[...], 2)
    for s in range(3):
        slot = slots[s]
        cols = columns(slot)
        k_gain = gain_ref[1, pl.ds(slot, 1), :]
        q = normed(q_ref[:, cols], q_inv, gain_ref[0, pl.ds(slot, 1), :])
        k = normed(k_ref[:, cols], k_inv, k_gain)
        v, g = v_ref[:, cols], g_ref[:, cols]
        if s == 0:
            d_q, d_k, d_v = attend(q, g, [k], [v], [None])
            fin_ref[0] = d_k[0].astype(BF)
            fin_ref[1] = d_v[0].astype(BF)
        else:
            at = 2 * s - 2
            wide = bands[s - 1] > 0
            keys = [normed(near_ref[at], near_inv, k_gain), k, normed(far_ref[at], far_inv, k_gain)]
            values = [near_ref[at + 1], v, far_ref[at + 1]]
            allowed = [wide, None, wide & (frame > 0) & (frame < FRAMES - 1)]
            d_q, d_k, d_v = attend(q, g, keys, values, allowed)
            to_near_ref[at] = d_k[0].astype(BF)
            to_near_ref[at + 1] = d_v[0].astype(BF)
            own_ref[at] = d_k[1]
            own_ref[at + 1] = d_v[1]
            to_far_ref[at] = d_k[2].astype(BF)
            to_far_ref[at + 1] = d_v[2].astype(BF)
        dq_ref[s] = d_q.astype(BF)


def temporal_body(in_ref, out_ref):
    rows = FRAMES * 8
    q, k, v, g = (in_ref[:, a].reshape(rows, HD) for a in range(4))
    d_k = jnp.zeros((rows, HD), F32)
    d_v = jnp.zeros((rows, HD), F32)
    step = 256
    for part in range(rows // step):
        q_part, g_part = q[part * step : (part + 1) * step], g[part * step : (part + 1) * step]
        key_tile = lax.broadcasted_iota(jnp.int32, (rows, step), 0) & 4
        query_tile = lax.broadcasted_iota(jnp.int32, (rows, step), 1) & 4
        d_q, d_keys, d_values = attend(q_part, g_part, [k], [v], [key_tile == query_tile])
        frames = step // 8
        out_ref[part * frames : (part + 1) * frames, 0] = d_q.astype(BF).reshape(frames, 8, HD)
        d_k += d_keys[0]
        d_v += d_values[0]
    out_ref[:, 1] = d_k.astype(BF).reshape(FRAMES, 8, HD)
    out_ref[:, 2] = d_v.astype(BF).reshape(FRAMES, 8, HD)


def product(gain_ref, which, slot, grad, ref):
    gain = gain_ref[which, pl.ds(slot, 1), :]
    return gain * grad.astype(F32) * ref[:, columns(slot)].astype(F32)


def spatial_sums_body(
    cls_ref, band_ref, gain_ref, q_ref, k_ref, dq_ref, fin_ref, own_ref, near_ref, far_ref, grad_ref, part_ref
):
    slots, _ = head_slots(cls_ref, band_ref)
    q_total = product(gain_ref, 0, slots[0], dq_ref[0], q_ref)
    k_total = product(gain_ref, 1, slots[0], fin_ref[0], k_ref)
    for s in (1, 2):
        for b in range(2):
            at = 2 * s - 2 + b
            grad_ref[at] = (
                own_ref[at] + near_ref[at].astype(F32) + far_ref[at].astype(F32)
            ).astype(BF)
        q_total += product(gain_ref, 0, slots[s], dq_ref[s], q_ref)
        k_total += product(gain_ref, 1, slots[s], grad_ref[2 * s - 2], k_ref)
    part_ref[0] = q_total
    part_ref[1] = k_total


def inner_body(cls_ref, band_ref, gain_ref, q_ref, k_ref, back_ref, part_ref, out_ref):
    slots, _ = head_slots(cls_ref, band_ref)
    sums = []
    for which, ref in enumerate((q_ref, k_ref)):
        total = part_ref[which]
        for s in range(2):
            grad = back_ref[s * 32 : (s + 1) * 32, which].reshape(TOK, HD)
            total += product(gain_ref, which, slots[3 + s], grad, ref)
        sums.append(lane_sums(total))
    out_ref[...] = jnp.broadcast_to(rows_of(*sums)[None], (8, 8, HD))


def value_body(cls_ref, band_ref, back_ref, fin_ref, grad_ref, out_ref):
    slots, _ = head_slots(cls_ref, band_ref)
    out_ref[:, columns(slots[0])] = fin_ref[1]
    for s in (1, 2):
        out_ref[:, columns(slots[s])] = grad_ref[2 * s - 1]
    for s in range(2):
        out_ref[:, columns(slots[3 + s])] = back_ref[s * 32 : (s + 1) * 32, 2].reshape(TOK, HD)


def final_body(
    cls_ref,
    band_ref,
    gain_ref,
    inv_ref,
    inner_ref,
    q_ref,
    k_ref,
    back_ref,
    dq_ref,
    fin_ref,
    grad_ref,
    out_q_ref,
    out_k_ref,
):
    slots, _ = head_slots(cls_ref, band_ref)
    inv = inv_ref[...]
    pull = inv * inv * inv * jnp.sum(inner_ref[...], axis=0) / FULL
    for which, (ref, out) in enumerate(((q_ref, out_q_ref), (k_ref, out_k_ref))):
        inverse, pulled = spread(inv, 2 * which), spread(pull, 2 * which)
        for s in range(HEADS_DEV):
            if s >= 3:
                grad = back_ref[(s - 3) * 32 : (s - 2) * 32, which].reshape(TOK, HD)
            elif which == 0:
                grad = dq_ref[s]
            else:
                grad = fin_ref[0] if s == 0 else grad_ref[2 * s - 2]
            gain = gain_ref[which, pl.ds(slots[s], 1), :]
            at = columns(slots[s])
            out[:, at] = (
                inverse * gain * grad.astype(F32) - ref[:, at].astype(F32) * pulled
            ).astype(BF)


def per_device(query_pre, key_pre, value, d_out, gain_q, gain_k, head_class, head_band):
    frame = lax.axis_index("seq").astype(jnp.int32).reshape(1)
    core = [(i, i ^ 1) for i in range(FRAMES)]
    chip = [(i, ((i - 1) ^ 1) + 1) for i in range(1, FRAMES - 1)]
    block = (4, TOK, HD)

    sums = pl.pallas_call(
        squares_body,
        out_shape=shape((8, 8, HD), F32),
        in_specs=[ANY] * 2,
        out_specs=VM,
        scratch_shapes=[pltpu.VMEM((TOK, WIDTH), BF)] * 2 + [pltpu.SemaphoreType.DMA((2,))],
        name="squares",
        compiler_params=pltpu.CompilerParams(vmem_limit_bytes=56 << 20),
    )(query_pre, key_pre)
    halo = call(halo_body, shape(block, BF), [SM, SM, ANY] + [VM] * 4, "halo", 2)(
        head_class, head_band, sums, query_pre, key_pre, value, d_out
    )
    gains = call(gains_body, shape((2, HEADS_DEV, HD), F32), [VM, VM, ANY], "gains", 8)(
        gain_q.reshape(HEADS_DEV, HD), gain_k.reshape(HEADS_DEV, HD), sums
    )
    near = lax.ppermute(halo, "seq", core)
    far = lax.ppermute(halo, "seq", chip)
    sums = lax.all_to_all(sums, "head", 0, 0, tiled=True)
    send, inv = call(
        norm_body,
        (shape((FRAMES, 4, 8, HD), BF), shape((8, HD), F32)),
        [SM, SM] + [VM] * 6 + [ANY],
        "norm",
        2,
    )(head_class, head_band, sums, gains, query_pre, key_pre, value, d_out, far)
    held = lax.all_to_all(send, "seq", 0, 0, tiled=True)
    inv_near = lax.ppermute(inv, "seq", core)
    inv_far = lax.ppermute(inv, "seq", chip)
    dq, fin, own, to_near, to_far = call(
        spatial_body,
        (
            shape((3, TOK, HD), BF),
            shape((2, TOK, HD), BF),
            shape(block, F32),
            shape(block, BF),
            shape(block, BF),
        ),
        [SM] * 3 + [VM] * 10,
        "spatial",
        4,
    )(
        head_class,
        head_band,
        frame,
        gains,
        inv,
        inv_near,
        inv_far,
        query_pre,
        key_pre,
        value,
        d_out,
        near,
        far,
    )
    from_near = lax.ppermute(to_near, "seq", core)
    from_far = lax.ppermute(to_far, "seq", chip)
    grads = call(temporal_body, shape((FRAMES, 3, 8, HD), BF), [VM], "temporal", 3)(held)
    back = lax.all_to_all(grads, "seq", 0, 0, tiled=True)
    grad, part = call(
        spatial_sums_body,
        (shape(block, BF), shape((2, TOK, HD), F32)),
        [SM, SM] + [VM] * 8,
        "spatial_sums",
        3,
    )(head_class, head_band, gains, query_pre, key_pre, dq, fin, own, from_near, from_far)
    inner = call(inner_body, shape((8, 8, HD), F32), [SM, SM] + [VM] * 5, "inner", 2)(
        head_class, head_band, gains, query_pre, key_pre, back, part
    )
    inner = lax.all_to_all(inner, "head", 0, 0, tiled=True)
    d_value = call(value_body, shape((TOK, WIDTH), BF), [SM, SM] + [VM] * 3, "value", 2)(
        head_class, head_band, back, fin, grad
    )
    d_query, d_key = call(
        final_body, (shape((TOK, WIDTH), BF),) * 2, [SM, SM] + [VM] * 9, "final", 3
    )(head_class, head_band, gains, inv, inner, query_pre, key_pre, back, dq, fin, grad)
    return d_query, d_key, d_value


def solution(mesh):
    whole = P("seq", "head")
    return jax.shard_map(
        per_device,
        mesh=mesh,
        in_specs=(whole,) * 4 + (P("head"),) * 4,
        out_specs=(whole,) * 3,
        check_vma=False,
    )
```

```python
import functools
import math

import jax
import jax.numpy as jnp
from jax import lax
from jax.experimental import pallas as pl
from jax.experimental.pallas import tpu as pltpu
from jax.sharding import PartitionSpec as P

HD = 128
TOK = 256
HEADS_DEV = 5
FRAMES = 64
WIDTH = HEADS_DEV * HD
FULL = 5120
EPSILON = 1e-06
SCALE = 1.0 / math.sqrt(HD)
NEG = -1e30
LOG2E = math.log2(math.e)

BF = jnp.bfloat16
F32 = jnp.float32
VM = pl.BlockSpec(memory_space=pltpu.VMEM)
SM = pl.BlockSpec(memory_space=pltpu.SMEM)
ANY = pl.BlockSpec(memory_space=pl.ANY)


def shape(dims, dtype):
    return jax.ShapeDtypeStruct(dims, dtype)


def call(body, outs, specs, name, micros, mib=24):
    return pl.pallas_call(
        body,
        out_shape=outs,
        in_specs=specs,
        out_specs=jax.tree.map(lambda _: VM, outs),
        name=name,
        compiler_params=pltpu.CompilerParams(vmem_limit_bytes=mib << 20),
        cost_estimate=pl.CostEstimate(
            flops=int(micros * 1e9), bytes_accessed=int(micros * 1e6), transcendentals=0
        ),
    )


def head_slots(cls_ref, band_ref):
    kinds = [cls_ref[i] for i in range(HEADS_DEV)]
    bands = [band_ref[i] for i in range(HEADS_DEV)]
    zero = jnp.int32(0)
    first = zero
    for i in reversed(range(HEADS_DEV)):
        first = jnp.where((kinds[i] == 0) & (bands[i] == 0), i, first)
    second, third, band_2, band_3, temp_0, temp_1 = zero, zero, zero, zero, zero, zero
    for i in reversed(range(HEADS_DEV)):
        other = (kinds[i] == 0) & (first != i)
        second = jnp.where(other, i, second)
        band_2 = jnp.where(other, bands[i], band_2)
        temp_0 = jnp.where(kinds[i] != 0, i, temp_0)
    for i in range(HEADS_DEV):
        other = (kinds[i] == 0) & (first != i)
        third = jnp.where(other, i, third)
        band_3 = jnp.where(other, bands[i], band_3)
        temp_1 = jnp.where(kinds[i] != 0, i, temp_1)
    return (first, second, third, temp_0, temp_1), (band_2, band_3)


def columns(slot):
    return pl.ds(pl.multiple_of(slot * HD, HD), HD)


def dot_nt(a, b, precision=None):
    return lax.dot_general(
        a, b, (((1,), (1,)), ((), ())), preferred_element_type=F32, precision=precision
    )


def dot_tn(a, b):
    return lax.dot_general(a, b, (((0,), (0,)), ((), ())), preferred_element_type=F32)


def dot_nn(a, b):
    return lax.dot_general(a, b, (((1,), (0,)), ((), ())), preferred_element_type=F32)


def rows_of(q_row, k_row):
    at = lax.broadcasted_iota(jnp.int32, (8, HD), 0)
    return jnp.where(
        at == 0,
        q_row[:, :HD],
        jnp.where(at == 1, q_row[:, HD:], jnp.where(at == 2, k_row[:, :HD], k_row[:, HD:])),
    )


def spread(rows, at):
    low = jnp.broadcast_to(rows[at : at + 1], (HD, HD)).T
    high = jnp.broadcast_to(rows[at + 1 : at + 2], (HD, HD)).T
    return jnp.concatenate([low, high], axis=0)


def lane_sums(values):
    return dot_nt(jnp.ones((8, HD), F32), values, lax.Precision.HIGHEST)


def inverses(sums_ref):
    return lax.rsqrt(jnp.sum(sums_ref[...], axis=0) / FULL + EPSILON)


def squares_body(q_hbm, k_hbm, out_ref, q_ref, k_ref, sems):
    copies = [
        pltpu.make_async_copy(source, target, sems.at[i])
        for i, (source, target) in enumerate(((q_hbm, q_ref), (k_hbm, k_ref)))
    ]
    for copy in copies:
        copy.start()
    sums = []
    for copy, ref in zip(copies, (q_ref, k_ref)):
        copy.wait()
        total = jnp.zeros((TOK, HD), F32)
        for head in range(HEADS_DEV):
            wide = ref[:, head * HD : (head + 1) * HD].astype(F32)
            total += wide * wide
        sums.append(lane_sums(total))
    out_ref[...] = jnp.broadcast_to(rows_of(*sums)[None], (8, 8, HD))


def halo_body(cls_ref, band_ref, after_ref, q_ref, k_ref, v_ref, g_ref, halo_ref):
    slots, _ = head_slots(cls_ref, band_ref)
    for s in (1, 2):
        for a, ref in enumerate((k_ref, v_ref, q_ref, g_ref)):
            halo_ref[4 * s - 4 + a] = ref[:, columns(slots[s])]


def gains_body(q_ref, k_ref, after_ref, out_ref):
    out_ref[0] = q_ref[...].astype(F32)
    out_ref[1] = k_ref[...].astype(F32)


def normed(values, inverse, gain):
    return (values.astype(F32) * inverse * gain).astype(BF)


def norm_body(
    cls_ref, band_ref, sums_ref, gain_ref, q_ref, k_ref, v_ref, g_ref, send_ref, inv_ref
):
    slots, _ = head_slots(cls_ref, band_ref)
    inv = inverses(sums_ref)
    inv_ref[...] = inv
    q_inv, k_inv = spread(inv, 0), spread(inv, 2)
    for s in range(2):
        slot = slots[3 + s]
        at = columns(slot)
        parts = (
            normed(q_ref[:, at], q_inv, gain_ref[0, pl.ds(slot, 1), :]),
            normed(k_ref[:, at], k_inv, gain_ref[1, pl.ds(slot, 1), :]),
            v_ref[:, at],
            g_ref[:, at],
        )
        for a, part in enumerate(parts):
            send_ref[s * 32 : (s + 1) * 32, a] = part.reshape(32, 8, HD)


def attend(q, g, keys, values, allowed):
    scores = []
    for key, ok in zip(keys, allowed):
        score = dot_nt(key, q)
        scores.append(score if ok is None else jnp.where(ok, score, NEG))
    largest = functools.reduce(
        jnp.maximum, [jnp.max(score, axis=0, keepdims=True) for score in scores]
    )
    powers = [jnp.exp2((score - largest) * (SCALE * LOG2E)) for score in scores]
    inverse = 1.0 / sum(jnp.sum(power, axis=0, keepdims=True) for power in powers)
    probs = [power * inverse for power in powers]
    d_probs = [dot_nt(value, g) for value in values]
    deltas = sum(jnp.sum(p * d, axis=0, keepdims=True) for p, d in zip(probs, d_probs))
    d_scores = [(p * (d - deltas)).astype(BF) for p, d in zip(probs, d_probs)]
    d_q = sum(dot_tn(d, key) for d, key in zip(d_scores, keys)) * SCALE
    return d_q, d_scores, probs, (largest, inverse, deltas)


def own_body(cls_ref, band_ref, gain_ref, inv_ref, q_ref, k_ref, v_ref, g_ref, out_ref):
    slots, _ = head_slots(cls_ref, band_ref)
    inv = inv_ref[...]
    cols = columns(slots[0])
    q = normed(q_ref[:, cols], spread(inv, 0), gain_ref[0, pl.ds(slots[0], 1), :])
    k = normed(k_ref[:, cols], spread(inv, 2), gain_ref[1, pl.ds(slots[0], 1), :])
    g = g_ref[:, cols]
    d_q, d_scores, probs, _ = attend(q, g, [k], [v_ref[:, cols]], [None])
    out_ref[0] = d_q.astype(BF)
    out_ref[1] = (dot_nn(d_scores[0], q) * SCALE).astype(BF)
    out_ref[2] = dot_nn(probs[0].astype(BF), g).astype(BF)


def reach(bands, s, frame):
    wide = bands[s - 1] > 0
    return wide, wide & (frame > 0) & (frame < FRAMES - 1)


def spatial_body(
    cls_ref,
    band_ref,
    frame_ref,
    gain_ref,
    inv_ref,
    inv_near_ref,
    inv_far_ref,
    q_ref,
    k_ref,
    v_ref,
    g_ref,
    near_ref,
    far_ref,
    dq_ref,
    part_ref,
    norm_ref,
    stat_ref,
):
    slots, bands = head_slots(cls_ref, band_ref)
    inv = inv_ref[...]
    q_inv, k_inv = spread(inv, 0), spread(inv, 2)
    near_inv, far_inv = spread(inv_near_ref[...], 2), spread(inv_far_ref[...], 2)
    stats = []
    for s in (1, 2):
        cols = columns(slots[s])
        k_gain = gain_ref[1, pl.ds(slots[s], 1), :]
        q = normed(q_ref[:, cols], q_inv, gain_ref[0, pl.ds(slots[s], 1), :])
        k = normed(k_ref[:, cols], k_inv, k_gain)
        g = g_ref[:, cols]
        at = 4 * s - 4
        near_ok, far_ok = reach(bands, s, frame_ref[0])
        keys = [k, normed(near_ref[at], near_inv, k_gain), normed(far_ref[at], far_inv, k_gain)]
        values = [v_ref[:, cols], near_ref[at + 1], far_ref[at + 1]]
        d_q, d_scores, probs, stat = attend(q, g, keys, values, [None, near_ok, far_ok])
        dq_ref[s - 1] = d_q.astype(BF)
        norm_ref[s - 1] = k
        part_ref[2 * s - 2] = dot_nn(d_scores[0], q)
        part_ref[2 * s - 1] = dot_nn(probs[0].astype(BF), g)
        stats.extend(stat)
    stat_ref[...] = jnp.concatenate(stats + stats[:2], axis=0)


def product(gain_ref, which, slot, grad, ref):
    gain = gain_ref[which, pl.ds(slot, 1), :]
    return gain * grad.astype(F32) * ref[:, columns(slot)].astype(F32)


def beside_body(
    cls_ref,
    band_ref,
    frame_ref,
    gain_ref,
    inv_near_ref,
    inv_far_ref,
    stat_near_ref,
    stat_far_ref,
    near_ref,
    far_ref,
    q_ref,
    k_ref,
    v_ref,
    norm_ref,
    own_ref,
    dq_ref,
    part_ref,
    grad_ref,
    sum_ref,
):
    slots, bands = head_slots(cls_ref, band_ref)
    q_invs = spread(inv_near_ref[...], 0), spread(inv_far_ref[...], 0)
    q_total = product(gain_ref, 0, slots[0], own_ref[0], q_ref)
    k_total = product(gain_ref, 1, slots[0], own_ref[1], k_ref)
    for s in (1, 2):
        slot = slots[s]
        q_gain = gain_ref[0, pl.ds(slot, 1), :]
        k, v = norm_ref[s - 1], v_ref[:, columns(slot)]
        d_k, d_v = part_ref[2 * s - 2], part_ref[2 * s - 1]
        at, row = 4 * s - 4, 3 * s - 3
        sides = zip((near_ref, far_ref), (stat_near_ref, stat_far_ref), q_invs, reach(bands, s, frame_ref[0]))
        for ref, stat, q_inv, ok in sides:
            q, g = normed(ref[at + 2], q_inv, q_gain), ref[at + 3]
            largest, inverse, delta = (stat[row + i : row + i + 1, :] for i in range(3))
            score = jnp.where(ok, dot_nt(k, q), NEG)
            prob = jnp.exp2((score - largest) * (SCALE * LOG2E)) * inverse
            d_score = (prob * (dot_nt(v, g) - delta)).astype(BF)
            d_k += dot_nn(d_score, q)
            d_v += dot_nn(prob.astype(BF), g)
        d_k = (d_k * SCALE).astype(BF)
        grad_ref[2 * s - 2] = d_k
        grad_ref[2 * s - 1] = d_v.astype(BF)
        q_total += product(gain_ref, 0, slot, dq_ref[s - 1], q_ref)
        k_total += product(gain_ref, 1, slot, d_k, k_ref)
    sum_ref[0] = q_total
    sum_ref[1] = k_total


def temporal_body(in_ref, after_ref, out_ref):
    rows = FRAMES * 8
    q, k, v, g = (in_ref[:, a].reshape(rows, HD) for a in range(4))
    d_k = jnp.zeros((rows, HD), F32)
    d_v = jnp.zeros((rows, HD), F32)
    step = 256
    for part in range(rows // step):
        q_part, g_part = q[part * step : (part + 1) * step], g[part * step : (part + 1) * step]
        key_tile = lax.broadcasted_iota(jnp.int32, (rows, step), 0) & 4
        query_tile = lax.broadcasted_iota(jnp.int32, (rows, step), 1) & 4
        d_q, d_scores, probs, _ = attend(q_part, g_part, [k], [v], [key_tile == query_tile])
        frames = step // 8
        out_ref[part * frames : (part + 1) * frames, 0] = d_q.astype(BF).reshape(frames, 8, HD)
        d_k += dot_nn(d_scores[0], q_part)
        d_v += dot_nn(probs[0].astype(BF), g_part)
    out_ref[:, 1] = (d_k * SCALE).astype(BF).reshape(FRAMES, 8, HD)
    out_ref[:, 2] = d_v.astype(BF).reshape(FRAMES, 8, HD)


def inner_body(cls_ref, band_ref, gain_ref, q_ref, k_ref, back_ref, part_ref, out_ref):
    slots, _ = head_slots(cls_ref, band_ref)
    sums = []
    for which, ref in enumerate((q_ref, k_ref)):
        total = part_ref[which]
        for s in range(2):
            grad = back_ref[s * 32 : (s + 1) * 32, which].reshape(TOK, HD)
            total += product(gain_ref, which, slots[3 + s], grad, ref)
        sums.append(lane_sums(total))
    out_ref[...] = jnp.broadcast_to(rows_of(*sums)[None], (8, 8, HD))


def value_body(cls_ref, band_ref, back_ref, own_ref, grad_ref, out_ref):
    slots, _ = head_slots(cls_ref, band_ref)
    out_ref[:, columns(slots[0])] = own_ref[2]
    for s in (1, 2):
        out_ref[:, columns(slots[s])] = grad_ref[2 * s - 1]
    for s in range(2):
        out_ref[:, columns(slots[3 + s])] = back_ref[s * 32 : (s + 1) * 32, 2].reshape(TOK, HD)


def final_body(
    cls_ref,
    band_ref,
    gain_ref,
    inv_ref,
    inner_ref,
    q_ref,
    k_ref,
    back_ref,
    own_ref,
    dq_ref,
    grad_ref,
    out_q_ref,
    out_k_ref,
):
    slots, _ = head_slots(cls_ref, band_ref)
    inv = inv_ref[...]
    pull = inv * inv * inv * jnp.sum(inner_ref[...], axis=0) / FULL
    for which, (ref, out) in enumerate(((q_ref, out_q_ref), (k_ref, out_k_ref))):
        inverse, pulled = spread(inv, 2 * which), spread(pull, 2 * which)
        for s in range(HEADS_DEV):
            if s >= 3:
                grad = back_ref[(s - 3) * 32 : (s - 2) * 32, which].reshape(TOK, HD)
            elif s == 0:
                grad = own_ref[which]
            else:
                grad = dq_ref[s - 1] if which == 0 else grad_ref[2 * s - 2]
            gain = gain_ref[which, pl.ds(slots[s], 1), :]
            at = columns(slots[s])
            out[:, at] = (
                inverse * gain * grad.astype(F32) - ref[:, at].astype(F32) * pulled
            ).astype(BF)


def per_device(query_pre, key_pre, value, d_out, gain_q, gain_k, head_class, head_band):
    frame = lax.axis_index("seq").astype(jnp.int32).reshape(1)
    core = [(i, i ^ 1) for i in range(FRAMES)]
    chip = [(i, ((i - 1) ^ 1) + 1) for i in range(1, FRAMES - 1)]

    sums = pl.pallas_call(
        squares_body,
        out_shape=shape((8, 8, HD), F32),
        in_specs=[ANY] * 2,
        out_specs=VM,
        scratch_shapes=[pltpu.VMEM((TOK, WIDTH), BF)] * 2 + [pltpu.SemaphoreType.DMA((2,))],
        name="squares",
        compiler_params=pltpu.CompilerParams(vmem_limit_bytes=56 << 20),
    )(query_pre, key_pre)
    halo = call(halo_body, shape((8, TOK, HD), BF), [SM, SM, ANY] + [VM] * 4, "halo", 2)(
        head_class, head_band, sums, query_pre, key_pre, value, d_out
    )
    gains = call(gains_body, shape((2, HEADS_DEV, HD), F32), [VM, VM, ANY], "gains", 8)(
        gain_q.reshape(HEADS_DEV, HD), gain_k.reshape(HEADS_DEV, HD), sums
    )
    near = lax.ppermute(halo, "seq", core)
    far = lax.ppermute(halo, "seq", chip)
    sums = lax.all_to_all(sums, "head", 0, 0, tiled=True)
    send, inv = call(
        norm_body,
        (shape((FRAMES, 4, 8, HD), BF), shape((8, HD), F32)),
        [SM, SM] + [VM] * 6,
        "norm",
        2,
    )(head_class, head_band, sums, gains, query_pre, key_pre, value, d_out)
    held = lax.all_to_all(send, "seq", 0, 0, tiled=True)
    inv_near = lax.ppermute(inv, "seq", core)
    inv_far = lax.ppermute(inv, "seq", chip)
    own = call(own_body, shape((3, TOK, HD), BF), [SM, SM] + [VM] * 6, "own", 2)(
        head_class, head_band, gains, inv, query_pre, key_pre, value, d_out
    )
    dq, part, k_norm, stat = call(
        spatial_body,
        (
            shape((2, TOK, HD), BF),
            shape((4, TOK, HD), F32),
            shape((2, TOK, HD), BF),
            shape((8, TOK), F32),
        ),
        [SM] * 3 + [VM] * 10,
        "spatial",
        8,
    )(
        head_class,
        head_band,
        frame,
        gains,
        inv,
        inv_near,
        inv_far,
        query_pre,
        key_pre,
        value,
        d_out,
        near,
        far,
    )
    grads = call(temporal_body, shape((FRAMES, 3, 8, HD), BF), [VM, ANY], "temporal", 3)(held, stat)
    stat_near = lax.ppermute(stat, "seq", core)
    stat_far = lax.ppermute(stat, "seq", chip)
    back = lax.all_to_all(grads, "seq", 0, 0, tiled=True)
    grad, part = call(
        beside_body,
        (shape((4, TOK, HD), BF), shape((2, TOK, HD), F32)),
        [SM] * 3 + [VM] * 14,
        "beside",
        3,
    )(
        head_class,
        head_band,
        frame,
        gains,
        inv_near,
        inv_far,
        stat_near,
        stat_far,
        near,
        far,
        query_pre,
        key_pre,
        value,
        k_norm,
        own,
        dq,
        part,
    )
    inner = call(inner_body, shape((8, 8, HD), F32), [SM, SM] + [VM] * 5, "inner", 2)(
        head_class, head_band, gains, query_pre, key_pre, back, part
    )
    inner = lax.all_to_all(inner, "head", 0, 0, tiled=True)
    d_value = call(value_body, shape((TOK, WIDTH), BF), [SM, SM] + [VM] * 3, "value", 2)(
        head_class, head_band, back, own, grad
    )
    d_query, d_key = call(
        final_body, (shape((TOK, WIDTH), BF),) * 2, [SM, SM] + [VM] * 9, "final", 3
    )(head_class, head_band, gains, inv, inner, query_pre, key_pre, back, own, dq, grad)
    return d_query, d_key, d_value


def solution(mesh):
    whole = P("seq", "head")
    return jax.shard_map(
        per_device,
        mesh=mesh,
        in_specs=(whole,) * 4 + (P("head"),) * 4,
        out_specs=(whole,) * 3,
        check_vma=False,
    )
```

```python
import functools
import math

import jax
import jax.numpy as jnp
from jax import lax
from jax.experimental import pallas as pl
from jax.experimental.pallas import tpu as pltpu
from jax.sharding import PartitionSpec as P

HD = 128
TOK = 256
HEADS_DEV = 5
FRAMES = 64
WIDTH = HEADS_DEV * HD
FULL = 5120
EPSILON = 1e-06
SCALE = 1.0 / math.sqrt(HD)
NEG = -1e30
LOG2E = math.log2(math.e)

BF = jnp.bfloat16
F32 = jnp.float32
VM = pl.BlockSpec(memory_space=pltpu.VMEM)
SM = pl.BlockSpec(memory_space=pltpu.SMEM)
ANY = pl.BlockSpec(memory_space=pl.ANY)


def shape(dims, dtype):
    return jax.ShapeDtypeStruct(dims, dtype)


def call(body, outs, specs, name, micros, mib=24):
    return pl.pallas_call(
        body,
        out_shape=outs,
        in_specs=specs,
        out_specs=jax.tree.map(lambda _: VM, outs),
        name=name,
        compiler_params=pltpu.CompilerParams(vmem_limit_bytes=mib << 20),
        cost_estimate=pl.CostEstimate(
            flops=int(micros * 1e9), bytes_accessed=int(micros * 1e6), transcendentals=0
        ),
    )


def head_slots(cls_ref, band_ref):
    kinds = [cls_ref[i] for i in range(HEADS_DEV)]
    bands = [band_ref[i] for i in range(HEADS_DEV)]
    zero = jnp.int32(0)
    first = zero
    for i in reversed(range(HEADS_DEV)):
        first = jnp.where((kinds[i] == 0) & (bands[i] == 0), i, first)
    second, third, band_2, band_3, temp_0, temp_1 = zero, zero, zero, zero, zero, zero
    for i in reversed(range(HEADS_DEV)):
        other = (kinds[i] == 0) & (first != i)
        second = jnp.where(other, i, second)
        band_2 = jnp.where(other, bands[i], band_2)
        temp_0 = jnp.where(kinds[i] != 0, i, temp_0)
    for i in range(HEADS_DEV):
        other = (kinds[i] == 0) & (first != i)
        third = jnp.where(other, i, third)
        band_3 = jnp.where(other, bands[i], band_3)
        temp_1 = jnp.where(kinds[i] != 0, i, temp_1)
    return (first, second, third, temp_0, temp_1), (band_2, band_3)


def columns(slot):
    return pl.ds(pl.multiple_of(slot * HD, HD), HD)


def dot_nt(a, b, precision=None):
    return lax.dot_general(
        a, b, (((1,), (1,)), ((), ())), preferred_element_type=F32, precision=precision
    )


def dot_tn(a, b):
    return lax.dot_general(a, b, (((0,), (0,)), ((), ())), preferred_element_type=F32)


def dot_nn(a, b):
    return lax.dot_general(a, b, (((1,), (0,)), ((), ())), preferred_element_type=F32)


def rows_of(q_row, k_row):
    at = lax.broadcasted_iota(jnp.int32, (8, HD), 0)
    return jnp.where(
        at == 0,
        q_row[:, :HD],
        jnp.where(at == 1, q_row[:, HD:], jnp.where(at == 2, k_row[:, :HD], k_row[:, HD:])),
    )


def spread(rows, at):
    low = jnp.broadcast_to(rows[at : at + 1], (HD, HD)).T
    high = jnp.broadcast_to(rows[at + 1 : at + 2], (HD, HD)).T
    return jnp.concatenate([low, high], axis=0)


def lane_sums(values):
    return dot_nt(jnp.ones((8, HD), F32), values, lax.Precision.HIGHEST)


def inverses(sums_ref):
    return lax.rsqrt(jnp.sum(sums_ref[...], axis=0) / FULL + EPSILON)


def squares_body(q_hbm, k_hbm, out_ref, q_ref, k_ref, sems):
    copies = [
        pltpu.make_async_copy(source, target, sems.at[i])
        for i, (source, target) in enumerate(((q_hbm, q_ref), (k_hbm, k_ref)))
    ]
    for copy in copies:
        copy.start()
    sums = []
    for copy, ref in zip(copies, (q_ref, k_ref)):
        copy.wait()
        total = jnp.zeros((TOK, HD), F32)
        for head in range(HEADS_DEV):
            wide = ref[:, head * HD : (head + 1) * HD].astype(F32)
            total += wide * wide
        sums.append(lane_sums(total))
    out_ref[...] = jnp.broadcast_to(rows_of(*sums)[None], (8, 8, HD))


def gains_body(q_ref, k_ref, after_ref, g_ref, out_ref):
    out_ref[0] = q_ref[...].astype(F32)
    out_ref[1] = k_ref[...].astype(F32)


def normed(values, inverse, gain):
    return (values.astype(F32) * inverse * gain).astype(BF)


def norm_body(
    cls_ref, band_ref, sums_ref, gain_ref, q_ref, k_ref, v_ref, g_ref, send_ref, halo_ref, inv_ref
):
    slots, _ = head_slots(cls_ref, band_ref)
    inv = inverses(sums_ref)
    inv_ref[...] = inv
    q_inv, k_inv = spread(inv, 0), spread(inv, 2)
    for s in range(2):
        slot = slots[3 + s]
        at = columns(slot)
        parts = (
            normed(q_ref[:, at], q_inv, gain_ref[0, pl.ds(slot, 1), :]),
            normed(k_ref[:, at], k_inv, gain_ref[1, pl.ds(slot, 1), :]),
            v_ref[:, at],
            g_ref[:, at],
        )
        for a, part in enumerate(parts):
            send_ref[s * 32 : (s + 1) * 32, a] = part.reshape(32, 8, HD)
    for s in (1, 2):
        at = columns(slots[s])
        halo_ref[2 * s - 2] = normed(k_ref[:, at], k_inv, gain_ref[1, pl.ds(slots[s], 1), :])
        halo_ref[2 * s - 1] = v_ref[:, at]


def attend(q, g, keys, values, allowed):
    scores = []
    for key, ok in zip(keys, allowed):
        score = dot_nt(key, q)
        scores.append(score if ok is None else jnp.where(ok, score, NEG))
    largest = functools.reduce(
        jnp.maximum, [jnp.max(score, axis=0, keepdims=True) for score in scores]
    )
    powers = [jnp.exp2((score - largest) * (SCALE * LOG2E)) for score in scores]
    totals = sum(jnp.sum(power, axis=0, keepdims=True) for power in powers)
    inverse = 1.0 / totals
    probs = [power * inverse for power in powers]
    d_probs = [dot_nt(value, g) for value in values]
    deltas = sum(jnp.sum(p * d, axis=0, keepdims=True) for p, d in zip(probs, d_probs))
    d_scores = [(p * (d - deltas)).astype(BF) for p, d in zip(probs, d_probs)]
    d_q = sum(dot_tn(d, key) for d, key in zip(d_scores, keys)) * SCALE
    d_keys = [dot_nn(d, q) * SCALE for d in d_scores]
    d_values = [dot_nn(p.astype(BF), g) for p in probs]
    return d_q, d_keys, d_values


def spatial_body(
    cls_ref,
    band_ref,
    frame_ref,
    gain_ref,
    inv_ref,
    q_ref,
    k_ref,
    v_ref,
    g_ref,
    halo_ref,
    near_ref,
    far_ref,
    dq_ref,
    fin_ref,
    own_ref,
    to_near_ref,
    to_far_ref,
):
    slots, bands = head_slots(cls_ref, band_ref)
    frame = frame_ref[0]
    inv = inv_ref[...]
    q_inv = spread(inv, 0)
    for s in range(3):
        cols = columns(slots[s])
        q = normed(q_ref[:, cols], q_inv, gain_ref[0, pl.ds(slots[s], 1), :])
        g = g_ref[:, cols]
        if s == 0:
            k = normed(k_ref[:, cols], spread(inv, 2), gain_ref[1, pl.ds(slots[s], 1), :])
            d_q, d_k, d_v = attend(q, g, [k], [v_ref[:, cols]], [None])
            fin_ref[0] = d_k[0].astype(BF)
            fin_ref[1] = d_v[0].astype(BF)
        else:
            at = 2 * s - 2
            wide = bands[s - 1] > 0
            keys = [near_ref[at], halo_ref[at], far_ref[at]]
            values = [near_ref[at + 1], halo_ref[at + 1], far_ref[at + 1]]
            allowed = [wide, None, wide & (frame > 0) & (frame < FRAMES - 1)]
            d_q, d_k, d_v = attend(q, g, keys, values, allowed)
            to_near_ref[at] = d_k[0].astype(BF)
            to_near_ref[at + 1] = d_v[0].astype(BF)
            own_ref[at] = d_k[1]
            own_ref[at + 1] = d_v[1]
            to_far_ref[at] = d_k[2].astype(BF)
            to_far_ref[at + 1] = d_v[2].astype(BF)
        dq_ref[s] = d_q.astype(BF)


def temporal_body(in_ref, out_ref):
    rows = FRAMES * 8
    q, k, v, g = (in_ref[:, a].reshape(rows, HD) for a in range(4))
    d_k = jnp.zeros((rows, HD), F32)
    d_v = jnp.zeros((rows, HD), F32)
    step = 256
    for part in range(rows // step):
        q_part, g_part = q[part * step : (part + 1) * step], g[part * step : (part + 1) * step]
        key_tile = lax.broadcasted_iota(jnp.int32, (rows, step), 0) & 4
        query_tile = lax.broadcasted_iota(jnp.int32, (rows, step), 1) & 4
        d_q, d_keys, d_values = attend(q_part, g_part, [k], [v], [key_tile == query_tile])
        frames = step // 8
        out_ref[part * frames : (part + 1) * frames, 0] = d_q.astype(BF).reshape(frames, 8, HD)
        d_k += d_keys[0]
        d_v += d_values[0]
    out_ref[:, 1] = d_k.astype(BF).reshape(FRAMES, 8, HD)
    out_ref[:, 2] = d_v.astype(BF).reshape(FRAMES, 8, HD)


def product(gain_ref, which, slot, grad, ref):
    gain = gain_ref[which, pl.ds(slot, 1), :]
    return gain * grad.astype(F32) * ref[:, columns(slot)].astype(F32)


def spatial_sums_body(
    cls_ref, band_ref, gain_ref, q_ref, k_ref, dq_ref, fin_ref, own_ref, near_ref, far_ref, grad_ref, part_ref
):
    slots, _ = head_slots(cls_ref, band_ref)
    q_total = product(gain_ref, 0, slots[0], dq_ref[0], q_ref)
    k_total = product(gain_ref, 1, slots[0], fin_ref[0], k_ref)
    for s in (1, 2):
        for b in range(2):
            at = 2 * s - 2 + b
            grad_ref[at] = (
                own_ref[at] + near_ref[at].astype(F32) + far_ref[at].astype(F32)
            ).astype(BF)
        q_total += product(gain_ref, 0, slots[s], dq_ref[s], q_ref)
        k_total += product(gain_ref, 1, slots[s], grad_ref[2 * s - 2], k_ref)
    part_ref[0] = q_total
    part_ref[1] = k_total


def inner_body(cls_ref, band_ref, gain_ref, q_ref, k_ref, back_ref, part_ref, out_ref):
    slots, _ = head_slots(cls_ref, band_ref)
    sums = []
    for which, ref in enumerate((q_ref, k_ref)):
        total = part_ref[which]
        for s in range(2):
            grad = back_ref[s * 32 : (s + 1) * 32, which].reshape(TOK, HD)
            total += product(gain_ref, which, slots[3 + s], grad, ref)
        sums.append(lane_sums(total))
    out_ref[...] = jnp.broadcast_to(rows_of(*sums)[None], (8, 8, HD))


def final_body(
    cls_ref,
    band_ref,
    gain_ref,
    inv_ref,
    inner_ref,
    q_ref,
    k_ref,
    back_ref,
    dq_ref,
    fin_ref,
    grad_ref,
    out_q_ref,
    out_k_ref,
    out_v_ref,
):
    slots, _ = head_slots(cls_ref, band_ref)
    inv = inv_ref[...]
    pull = inv * inv * inv * jnp.sum(inner_ref[...], axis=0) / FULL
    for which, (ref, out) in enumerate(((q_ref, out_q_ref), (k_ref, out_k_ref))):
        inverse, pulled = spread(inv, 2 * which), spread(pull, 2 * which)
        for s in range(HEADS_DEV):
            if s >= 3:
                grad = back_ref[(s - 3) * 32 : (s - 2) * 32, which].reshape(TOK, HD)
            elif which == 0:
                grad = dq_ref[s]
            else:
                grad = fin_ref[0] if s == 0 else grad_ref[2 * s - 2]
            gain = gain_ref[which, pl.ds(slots[s], 1), :]
            at = columns(slots[s])
            out[:, at] = (
                inverse * gain * grad.astype(F32) - ref[:, at].astype(F32) * pulled
            ).astype(BF)
    out_v_ref[:, columns(slots[0])] = fin_ref[1]
    for s in (1, 2):
        out_v_ref[:, columns(slots[s])] = grad_ref[2 * s - 1]
    for s in range(2):
        out_v_ref[:, columns(slots[3 + s])] = back_ref[s * 32 : (s + 1) * 32, 2].reshape(TOK, HD)


def per_device(query_pre, key_pre, value, d_out, gain_q, gain_k, head_class, head_band):
    frame = lax.axis_index("seq").astype(jnp.int32).reshape(1)
    core = [(i, i ^ 1) for i in range(FRAMES)]
    chip = [(i, ((i - 1) ^ 1) + 1) for i in range(1, FRAMES - 1)]
    block = (4, TOK, HD)

    sums = pl.pallas_call(
        squares_body,
        out_shape=shape((8, 8, HD), F32),
        in_specs=[ANY] * 2,
        out_specs=VM,
        scratch_shapes=[pltpu.VMEM((TOK, WIDTH), BF)] * 2 + [pltpu.SemaphoreType.DMA((2,))],
        name="squares",
        compiler_params=pltpu.CompilerParams(vmem_limit_bytes=56 << 20),
    )(query_pre, key_pre)
    gains = call(gains_body, shape((2, HEADS_DEV, HD), F32), [VM, VM, ANY, VM], "gains", 1)(
        gain_q.reshape(HEADS_DEV, HD), gain_k.reshape(HEADS_DEV, HD), sums, d_out
    )
    sums = lax.all_to_all(sums, "head", 0, 0, tiled=True)
    send, halo, inv = call(
        norm_body,
        (shape((FRAMES, 4, 8, HD), BF), shape(block, BF), shape((8, HD), F32)),
        [SM, SM] + [VM] * 6,
        "norm",
        2,
    )(head_class, head_band, sums, gains, query_pre, key_pre, value, d_out)
    held = lax.all_to_all(send, "seq", 0, 0, tiled=True)
    near = lax.ppermute(halo, "seq", core)
    far = lax.ppermute(halo, "seq", chip)
    dq, fin, own, to_near, to_far = call(
        spatial_body,
        (
            shape((3, TOK, HD), BF),
            shape((2, TOK, HD), BF),
            shape(block, F32),
            shape(block, BF),
            shape(block, BF),
        ),
        [SM] * 3 + [VM] * 9,
        "spatial",
        6,
    )(
        head_class,
        head_band,
        frame,
        gains,
        inv,
        query_pre,
        key_pre,
        value,
        d_out,
        halo,
        near,
        far,
    )
    from_far = lax.ppermute(to_far, "seq", chip)
    from_near = lax.ppermute(to_near, "seq", core)
    grads = call(temporal_body, shape((FRAMES, 3, 8, HD), BF), [VM], "temporal", 3)(held)
    back = lax.all_to_all(grads, "seq", 0, 0, tiled=True)
    grad, part = call(
        spatial_sums_body,
        (shape(block, BF), shape((2, TOK, HD), F32)),
        [SM, SM] + [VM] * 8,
        "spatial_sums",
        3,
    )(head_class, head_band, gains, query_pre, key_pre, dq, fin, own, from_far, from_near)
    inner = call(inner_body, shape((8, 8, HD), F32), [SM, SM] + [VM] * 5, "inner", 2)(
        head_class, head_band, gains, query_pre, key_pre, back, part
    )
    inner = lax.all_to_all(inner, "head", 0, 0, tiled=True)
    return call(
        final_body,
        (shape((TOK, WIDTH), BF),) * 3,
        [SM, SM] + [VM] * 9,
        "final",
        3,
    )(head_class, head_band, gains, inv, inner, query_pre, key_pre, back, dq, fin, grad)


def solution(mesh):
    whole = P("seq", "head")
    return jax.shard_map(
        per_device,
        mesh=mesh,
        in_specs=(whole,) * 4 + (P("head"),) * 4,
        out_specs=(whole,) * 3,
        check_vma=False,
    )
```

```python
import functools
import math

import jax
import jax.numpy as jnp
from jax import lax
from jax.experimental import pallas as pl
from jax.experimental.pallas import tpu as pltpu
from jax.sharding import PartitionSpec as P

HD = 128
TOK = 256
HEADS_DEV = 5
FRAMES = 64
WIDTH = HEADS_DEV * HD
FULL = 5120
EPSILON = 1e-06
SCALE = 1.0 / math.sqrt(HD)
NEG = -1e30
LOG2E = math.log2(math.e)

BF = jnp.bfloat16
F32 = jnp.float32
VM = pl.BlockSpec(memory_space=pltpu.VMEM)
SM = pl.BlockSpec(memory_space=pltpu.SMEM)
ANY = pl.BlockSpec(memory_space=pl.ANY)


def shape(dims, dtype):
    return jax.ShapeDtypeStruct(dims, dtype)


def call(body, outs, specs, name, micros, mib=24):
    return pl.pallas_call(
        body,
        out_shape=outs,
        in_specs=specs,
        out_specs=jax.tree.map(lambda _: VM, outs),
        name=name,
        compiler_params=pltpu.CompilerParams(vmem_limit_bytes=mib << 20),
        cost_estimate=pl.CostEstimate(
            flops=int(micros * 1e9), bytes_accessed=int(micros * 1e6), transcendentals=0
        ),
    )


def head_slots(cls_ref, band_ref):
    kinds = [cls_ref[i] for i in range(HEADS_DEV)]
    bands = [band_ref[i] for i in range(HEADS_DEV)]
    zero = jnp.int32(0)
    first = zero
    for i in reversed(range(HEADS_DEV)):
        first = jnp.where((kinds[i] == 0) & (bands[i] == 0), i, first)
    second, third, band_2, band_3, temp_0, temp_1 = zero, zero, zero, zero, zero, zero
    for i in reversed(range(HEADS_DEV)):
        other = (kinds[i] == 0) & (first != i)
        second = jnp.where(other, i, second)
        band_2 = jnp.where(other, bands[i], band_2)
        temp_0 = jnp.where(kinds[i] != 0, i, temp_0)
    for i in range(HEADS_DEV):
        other = (kinds[i] == 0) & (first != i)
        third = jnp.where(other, i, third)
        band_3 = jnp.where(other, bands[i], band_3)
        temp_1 = jnp.where(kinds[i] != 0, i, temp_1)
    return (first, second, third, temp_0, temp_1), (band_2, band_3)


def columns(slot):
    return pl.ds(pl.multiple_of(slot * HD, HD), HD)


def dot_nt(a, b, precision=None):
    return lax.dot_general(
        a, b, (((1,), (1,)), ((), ())), preferred_element_type=F32, precision=precision
    )


def dot_tn(a, b):
    return lax.dot_general(a, b, (((0,), (0,)), ((), ())), preferred_element_type=F32)


def dot_nn(a, b):
    return lax.dot_general(a, b, (((1,), (0,)), ((), ())), preferred_element_type=F32)


def rows_of(q_row, k_row):
    at = lax.broadcasted_iota(jnp.int32, (8, HD), 0)
    return jnp.where(
        at == 0,
        q_row[:, :HD],
        jnp.where(at == 1, q_row[:, HD:], jnp.where(at == 2, k_row[:, :HD], k_row[:, HD:])),
    )


def spread(rows, at):
    low = jnp.broadcast_to(rows[at : at + 1], (HD, HD)).T
    high = jnp.broadcast_to(rows[at + 1 : at + 2], (HD, HD)).T
    return jnp.concatenate([low, high], axis=0)


def lane_sums(values):
    return dot_nt(jnp.ones((8, HD), F32), values, lax.Precision.HIGHEST)


def inverses(sums_ref):
    return lax.rsqrt(jnp.sum(sums_ref[...], axis=0) / FULL + EPSILON)


def squares_body(q_hbm, k_hbm, out_ref, q_ref, k_ref, sems):
    copies = [
        pltpu.make_async_copy(source, target, sems.at[i])
        for i, (source, target) in enumerate(((q_hbm, q_ref), (k_hbm, k_ref)))
    ]
    for copy in copies:
        copy.start()
    sums = []
    for copy, ref in zip(copies, (q_ref, k_ref)):
        copy.wait()
        total = jnp.zeros((TOK, HD), F32)
        for head in range(HEADS_DEV):
            wide = ref[:, head * HD : (head + 1) * HD].astype(F32)
            total += wide * wide
        sums.append(lane_sums(total))
    out_ref[...] = jnp.broadcast_to(rows_of(*sums)[None], (8, 8, HD))


def halo_body(cls_ref, band_ref, after_ref, k_ref, v_ref, halo_ref):
    slots, _ = head_slots(cls_ref, band_ref)
    for s in (1, 2):
        halo_ref[2 * s - 2] = k_ref[:, columns(slots[s])]
        halo_ref[2 * s - 1] = v_ref[:, columns(slots[s])]


def gains_body(q_ref, k_ref, after_ref, g_ref, out_ref):
    out_ref[0] = q_ref[...].astype(F32)
    out_ref[1] = k_ref[...].astype(F32)


def normed(values, inverse, gain):
    return (values.astype(F32) * inverse * gain).astype(BF)


def norm_body(
    cls_ref, band_ref, sums_ref, gain_ref, q_ref, k_ref, v_ref, g_ref, send_ref, halo_ref, inv_ref
):
    slots, _ = head_slots(cls_ref, band_ref)
    inv = inverses(sums_ref)
    inv_ref[...] = inv
    q_inv, k_inv = spread(inv, 0), spread(inv, 2)
    for s in range(2):
        slot = slots[3 + s]
        at = columns(slot)
        parts = (
            normed(q_ref[:, at], q_inv, gain_ref[0, pl.ds(slot, 1), :]),
            normed(k_ref[:, at], k_inv, gain_ref[1, pl.ds(slot, 1), :]),
            v_ref[:, at],
            g_ref[:, at],
        )
        for a, part in enumerate(parts):
            send_ref[s * 32 : (s + 1) * 32, a] = part.reshape(32, 8, HD)
    for s in (1, 2):
        at = columns(slots[s])
        halo_ref[2 * s - 2] = normed(k_ref[:, at], k_inv, gain_ref[1, pl.ds(slots[s], 1), :])
        halo_ref[2 * s - 1] = v_ref[:, at]


def attend(q, g, keys, values, allowed):
    scores = []
    for key, ok in zip(keys, allowed):
        score = dot_nt(key, q)
        scores.append(score if ok is None else jnp.where(ok, score, NEG))
    largest = functools.reduce(
        jnp.maximum, [jnp.max(score, axis=0, keepdims=True) for score in scores]
    )
    powers = [jnp.exp2((score - largest) * (SCALE * LOG2E)) for score in scores]
    totals = sum(jnp.sum(power, axis=0, keepdims=True) for power in powers)
    inverse = 1.0 / totals
    probs = [power * inverse for power in powers]
    d_probs = [dot_nt(value, g) for value in values]
    deltas = sum(jnp.sum(p * d, axis=0, keepdims=True) for p, d in zip(probs, d_probs))
    d_scores = [(p * (d - deltas)).astype(BF) for p, d in zip(probs, d_probs)]
    d_q = sum(dot_tn(d, key) for d, key in zip(d_scores, keys)) * SCALE
    d_keys = [dot_nn(d, q) * SCALE for d in d_scores]
    d_values = [dot_nn(p.astype(BF), g) for p in probs]
    return d_q, d_keys, d_values


def own_body(
    cls_ref, band_ref, gain_ref, inv_ref, q_ref, k_ref, v_ref, g_ref, after_ref, dq_ref, fin_ref, done_ref
):
    slots, _ = head_slots(cls_ref, band_ref)
    inv = inv_ref[...]
    done_ref[...] = inv
    cols = columns(slots[0])
    q = normed(q_ref[:, cols], spread(inv, 0), gain_ref[0, pl.ds(slots[0], 1), :])
    k = normed(k_ref[:, cols], spread(inv, 2), gain_ref[1, pl.ds(slots[0], 1), :])
    d_q, d_k, d_v = attend(q, g_ref[:, cols], [k], [v_ref[:, cols]], [None])
    dq_ref[...] = d_q.astype(BF)
    fin_ref[0] = d_k[0].astype(BF)
    fin_ref[1] = d_v[0].astype(BF)


def spatial_body(
    cls_ref,
    band_ref,
    frame_ref,
    gain_ref,
    inv_ref,
    inv_far_ref,
    q_ref,
    g_ref,
    halo_ref,
    near_ref,
    far_ref,
    dq_ref,
    own_ref,
    to_near_ref,
    to_far_ref,
):
    slots, bands = head_slots(cls_ref, band_ref)
    frame = frame_ref[0]
    q_inv = spread(inv_ref[...], 0)
    far_inv = spread(inv_far_ref[...], 2)
    for s in (1, 2):
        cols = columns(slots[s])
        q = normed(q_ref[:, cols], q_inv, gain_ref[0, pl.ds(slots[s], 1), :])
        at = 2 * s - 2
        wide = bands[s - 1] > 0
        far = normed(far_ref[at], far_inv, gain_ref[1, pl.ds(slots[s], 1), :])
        keys = [near_ref[at], halo_ref[at], far]
        values = [near_ref[at + 1], halo_ref[at + 1], far_ref[at + 1]]
        allowed = [wide, None, wide & (frame > 0) & (frame < FRAMES - 1)]
        d_q, d_k, d_v = attend(q, g_ref[:, cols], keys, values, allowed)
        dq_ref[s - 1] = d_q.astype(BF)
        to_near_ref[at] = d_k[0].astype(BF)
        to_near_ref[at + 1] = d_v[0].astype(BF)
        own_ref[at] = d_k[1]
        own_ref[at + 1] = d_v[1]
        to_far_ref[at] = d_k[2].astype(BF)
        to_far_ref[at + 1] = d_v[2].astype(BF)


def temporal_body(in_ref, after_ref, out_ref):
    rows = FRAMES * 8
    q, k, v, g = (in_ref[:, a].reshape(rows, HD) for a in range(4))
    d_k = jnp.zeros((rows, HD), F32)
    d_v = jnp.zeros((rows, HD), F32)
    step = 256
    for part in range(rows // step):
        q_part, g_part = q[part * step : (part + 1) * step], g[part * step : (part + 1) * step]
        key_tile = lax.broadcasted_iota(jnp.int32, (rows, step), 0) & 4
        query_tile = lax.broadcasted_iota(jnp.int32, (rows, step), 1) & 4
        d_q, d_keys, d_values = attend(q_part, g_part, [k], [v], [key_tile == query_tile])
        frames = step // 8
        out_ref[part * frames : (part + 1) * frames, 0] = d_q.astype(BF).reshape(frames, 8, HD)
        d_k += d_keys[0]
        d_v += d_values[0]
    out_ref[:, 1] = d_k.astype(BF).reshape(FRAMES, 8, HD)
    out_ref[:, 2] = d_v.astype(BF).reshape(FRAMES, 8, HD)


def product(gain_ref, which, slot, grad, ref):
    gain = gain_ref[which, pl.ds(slot, 1), :]
    return gain * grad.astype(F32) * ref[:, columns(slot)].astype(F32)


def spatial_sums_body(
    cls_ref,
    band_ref,
    gain_ref,
    q_ref,
    k_ref,
    dq0_ref,
    dq_ref,
    fin_ref,
    own_ref,
    far_ref,
    near_ref,
    grad_ref,
    part_ref,
):
    slots, _ = head_slots(cls_ref, band_ref)
    q_total = product(gain_ref, 0, slots[0], dq0_ref[...], q_ref)
    k_total = product(gain_ref, 1, slots[0], fin_ref[0], k_ref)
    for s in (1, 2):
        for b in range(2):
            at = 2 * s - 2 + b
            grad_ref[at] = (
                own_ref[at] + far_ref[at].astype(F32) + near_ref[at].astype(F32)
            ).astype(BF)
        q_total += product(gain_ref, 0, slots[s], dq_ref[s - 1], q_ref)
        k_total += product(gain_ref, 1, slots[s], grad_ref[2 * s - 2], k_ref)
    part_ref[0] = q_total
    part_ref[1] = k_total


def inner_body(cls_ref, band_ref, gain_ref, q_ref, k_ref, back_ref, part_ref, out_ref):
    slots, _ = head_slots(cls_ref, band_ref)
    sums = []
    for which, ref in enumerate((q_ref, k_ref)):
        total = part_ref[which]
        for s in range(2):
            grad = back_ref[s * 32 : (s + 1) * 32, which].reshape(TOK, HD)
            total += product(gain_ref, which, slots[3 + s], grad, ref)
        sums.append(lane_sums(total))
    out_ref[...] = jnp.broadcast_to(rows_of(*sums)[None], (8, 8, HD))


def final_body(
    cls_ref,
    band_ref,
    gain_ref,
    inv_ref,
    inner_ref,
    q_ref,
    k_ref,
    back_ref,
    dq0_ref,
    dq_ref,
    fin_ref,
    grad_ref,
    out_q_ref,
    out_k_ref,
    out_v_ref,
):
    slots, _ = head_slots(cls_ref, band_ref)
    inv = inv_ref[...]
    pull = inv * inv * inv * jnp.sum(inner_ref[...], axis=0) / FULL
    for which, (ref, out) in enumerate(((q_ref, out_q_ref), (k_ref, out_k_ref))):
        inverse, pulled = spread(inv, 2 * which), spread(pull, 2 * which)
        for s in range(HEADS_DEV):
            if s >= 3:
                grad = back_ref[(s - 3) * 32 : (s - 2) * 32, which].reshape(TOK, HD)
            elif which == 0:
                grad = dq0_ref[...] if s == 0 else dq_ref[s - 1]
            else:
                grad = fin_ref[0] if s == 0 else grad_ref[2 * s - 2]
            gain = gain_ref[which, pl.ds(slots[s], 1), :]
            at = columns(slots[s])
            out[:, at] = (
                inverse * gain * grad.astype(F32) - ref[:, at].astype(F32) * pulled
            ).astype(BF)
    out_v_ref[:, columns(slots[0])] = fin_ref[1]
    for s in (1, 2):
        out_v_ref[:, columns(slots[s])] = grad_ref[2 * s - 1]
    for s in range(2):
        out_v_ref[:, columns(slots[3 + s])] = back_ref[s * 32 : (s + 1) * 32, 2].reshape(TOK, HD)


def per_device(query_pre, key_pre, value, d_out, gain_q, gain_k, head_class, head_band):
    frame = lax.axis_index("seq").astype(jnp.int32).reshape(1)
    core = [(i, i ^ 1) for i in range(FRAMES)]
    chip = [(i, ((i - 1) ^ 1) + 1) for i in range(1, FRAMES - 1)]
    block = (4, TOK, HD)

    sums = pl.pallas_call(
        squares_body,
        out_shape=shape((8, 8, HD), F32),
        in_specs=[ANY] * 2,
        out_specs=VM,
        scratch_shapes=[pltpu.VMEM((TOK, WIDTH), BF)] * 2 + [pltpu.SemaphoreType.DMA((2,))],
        name="squares",
        compiler_params=pltpu.CompilerParams(vmem_limit_bytes=56 << 20),
    )(query_pre, key_pre)
    halo = call(halo_body, shape(block, BF), [SM, SM, ANY, VM, VM], "halo", 2)(
        head_class, head_band, sums, key_pre, value
    )
    far = lax.ppermute(halo, "seq", chip)
    gains = call(gains_body, shape((2, HEADS_DEV, HD), F32), [VM, VM, ANY, VM], "gains", 8)(
        gain_q.reshape(HEADS_DEV, HD), gain_k.reshape(HEADS_DEV, HD), sums, d_out
    )
    sums = lax.all_to_all(sums, "head", 0, 0, tiled=True)
    send, halo, inv = call(
        norm_body,
        (shape((FRAMES, 4, 8, HD), BF), shape(block, BF), shape((8, HD), F32)),
        [SM, SM] + [VM] * 6,
        "norm",
        2,
    )(head_class, head_band, sums, gains, query_pre, key_pre, value, d_out)
    held = lax.all_to_all(send, "seq", 0, 0, tiled=True)
    near = lax.ppermute(halo, "seq", core)
    inv_far = lax.ppermute(inv, "seq", chip)
    dq0, fin, done = call(
        own_body,
        (shape((TOK, HD), BF), shape((2, TOK, HD), BF), shape((8, HD), F32)),
        [SM, SM] + [VM] * 6 + [ANY],
        "own",
        10,
    )(head_class, head_band, gains, inv, query_pre, key_pre, value, d_out, far)
    dq, own, to_near, to_far = call(
        spatial_body,
        (
            shape((2, TOK, HD), BF),
            shape(block, F32),
            shape(block, BF),
            shape(block, BF),
        ),
        [SM] * 3 + [VM] * 8,
        "spatial",
        6,
    )(
        head_class, head_band, frame, gains, inv, inv_far, query_pre, d_out, halo, near, far
    )
    from_far = lax.ppermute(to_far, "seq", chip)
    from_near = lax.ppermute(to_near, "seq", core)
    grads = call(temporal_body, shape((FRAMES, 3, 8, HD), BF), [VM, ANY], "temporal", 3)(held, done)
    back = lax.all_to_all(grads, "seq", 0, 0, tiled=True)
    grad, part = call(
        spatial_sums_body,
        (shape(block, BF), shape((2, TOK, HD), F32)),
        [SM, SM] + [VM] * 9,
        "spatial_sums",
        3,
    )(head_class, head_band, gains, query_pre, key_pre, dq0, dq, fin, own, from_far, from_near)
    inner = call(inner_body, shape((8, 8, HD), F32), [SM, SM] + [VM] * 5, "inner", 2)(
        head_class, head_band, gains, query_pre, key_pre, back, part
    )
    inner = lax.all_to_all(inner, "head", 0, 0, tiled=True)
    return call(
        final_body,
        (shape((TOK, WIDTH), BF),) * 3,
        [SM, SM] + [VM] * 10,
        "final",
        3,
    )(head_class, head_band, gains, inv, inner, query_pre, key_pre, back, dq0, dq, fin, grad)


def solution(mesh):
    whole = P("seq", "head")
    return jax.shard_map(
        per_device,
        mesh=mesh,
        in_specs=(whole,) * 4 + (P("head"),) * 4,
        out_specs=(whole,) * 3,
        check_vma=False,
    )
```

```python
import functools
import math

import jax
import jax.numpy as jnp
from jax import lax
from jax.experimental import pallas as pl
from jax.experimental.pallas import tpu as pltpu
from jax.sharding import PartitionSpec as P

HD = 128
TOK = 256
HEADS_DEV = 5
FRAMES = 64
WIDTH = HEADS_DEV * HD
FULL = 5120
EPSILON = 1e-06
SCALE = 1.0 / math.sqrt(HD)
NEG = -1e30
LOG2E = math.log2(math.e)

BF = jnp.bfloat16
F32 = jnp.float32
VM = pl.BlockSpec(memory_space=pltpu.VMEM)
SM = pl.BlockSpec(memory_space=pltpu.SMEM)
ANY = pl.BlockSpec(memory_space=pl.ANY)


def shape(dims, dtype):
    return jax.ShapeDtypeStruct(dims, dtype)


def call(body, outs, specs, name, micros, mib=24):
    return pl.pallas_call(
        body,
        out_shape=outs,
        in_specs=specs,
        out_specs=jax.tree.map(lambda _: VM, outs),
        name=name,
        compiler_params=pltpu.CompilerParams(vmem_limit_bytes=mib << 20),
        cost_estimate=pl.CostEstimate(
            flops=int(micros * 1e9), bytes_accessed=int(micros * 1e6), transcendentals=0
        ),
    )


def head_slots(cls_ref, band_ref):
    kinds = [cls_ref[i] for i in range(HEADS_DEV)]
    bands = [band_ref[i] for i in range(HEADS_DEV)]
    zero = jnp.int32(0)
    first = zero
    for i in reversed(range(HEADS_DEV)):
        first = jnp.where((kinds[i] == 0) & (bands[i] == 0), i, first)
    second, third, band_2, band_3, temp_0, temp_1 = zero, zero, zero, zero, zero, zero
    for i in reversed(range(HEADS_DEV)):
        other = (kinds[i] == 0) & (first != i)
        second = jnp.where(other, i, second)
        band_2 = jnp.where(other, bands[i], band_2)
        temp_0 = jnp.where(kinds[i] != 0, i, temp_0)
    for i in range(HEADS_DEV):
        other = (kinds[i] == 0) & (first != i)
        third = jnp.where(other, i, third)
        band_3 = jnp.where(other, bands[i], band_3)
        temp_1 = jnp.where(kinds[i] != 0, i, temp_1)
    return (first, second, third, temp_0, temp_1), (band_2, band_3)


def columns(slot):
    return pl.ds(pl.multiple_of(slot * HD, HD), HD)


def dot_nt(a, b, precision=None):
    return lax.dot_general(
        a, b, (((1,), (1,)), ((), ())), preferred_element_type=F32, precision=precision
    )


def dot_tn(a, b):
    return lax.dot_general(a, b, (((0,), (0,)), ((), ())), preferred_element_type=F32)


def dot_nn(a, b):
    return lax.dot_general(a, b, (((1,), (0,)), ((), ())), preferred_element_type=F32)


def rows_of(q_row, k_row):
    at = lax.broadcasted_iota(jnp.int32, (8, HD), 0)
    return jnp.where(
        at == 0,
        q_row[:, :HD],
        jnp.where(at == 1, q_row[:, HD:], jnp.where(at == 2, k_row[:, :HD], k_row[:, HD:])),
    )


def spread(rows, at):
    low = jnp.broadcast_to(rows[at : at + 1], (HD, HD)).T
    high = jnp.broadcast_to(rows[at + 1 : at + 2], (HD, HD)).T
    return jnp.concatenate([low, high], axis=0)


def lane_sums(values):
    return dot_nt(jnp.ones((8, HD), F32), values, lax.Precision.HIGHEST)


def inverses(sums_ref):
    return lax.rsqrt(jnp.sum(sums_ref[...], axis=0) / FULL + EPSILON)


def squares_body(q_hbm, k_hbm, out_ref, q_ref, k_ref, sems):
    copies = [
        pltpu.make_async_copy(source, target, sems.at[i])
        for i, (source, target) in enumerate(((q_hbm, q_ref), (k_hbm, k_ref)))
    ]
    for copy in copies:
        copy.start()
    sums = []
    for copy, ref in zip(copies, (q_ref, k_ref)):
        copy.wait()
        total = jnp.zeros((TOK, HD), F32)
        for head in range(HEADS_DEV):
            wide = ref[:, head * HD : (head + 1) * HD].astype(F32)
            total += wide * wide
        sums.append(lane_sums(total))
    out_ref[...] = jnp.broadcast_to(rows_of(*sums)[None], (8, 8, HD))


def halo_body(cls_ref, band_ref, after_ref, k_ref, v_ref, halo_ref):
    slots, _ = head_slots(cls_ref, band_ref)
    for s in (1, 2):
        halo_ref[2 * s - 2] = k_ref[:, columns(slots[s])]
        halo_ref[2 * s - 1] = v_ref[:, columns(slots[s])]


def gains_body(q_ref, k_ref, after_ref, g_ref, out_ref):
    out_ref[0] = q_ref[...].astype(F32)
    out_ref[1] = k_ref[...].astype(F32)


def normed(values, inverse, gain):
    return (values.astype(F32) * inverse * gain).astype(BF)


def norm_body(
    cls_ref, band_ref, sums_ref, gain_ref, q_ref, k_ref, v_ref, g_ref, send_ref, inv_ref
):
    slots, _ = head_slots(cls_ref, band_ref)
    inv = inverses(sums_ref)
    inv_ref[...] = inv
    q_inv, k_inv = spread(inv, 0), spread(inv, 2)
    for s in range(2):
        slot = slots[3 + s]
        at = columns(slot)
        parts = (
            normed(q_ref[:, at], q_inv, gain_ref[0, pl.ds(slot, 1), :]),
            normed(k_ref[:, at], k_inv, gain_ref[1, pl.ds(slot, 1), :]),
            v_ref[:, at],
            g_ref[:, at],
        )
        for a, part in enumerate(parts):
            send_ref[s * 32 : (s + 1) * 32, a] = part.reshape(32, 8, HD)


def attend(q, g, keys, values, allowed):
    scores = []
    for key, ok in zip(keys, allowed):
        score = dot_nt(key, q)
        scores.append(score if ok is None else jnp.where(ok, score, NEG))
    largest = functools.reduce(
        jnp.maximum, [jnp.max(score, axis=0, keepdims=True) for score in scores]
    )
    powers = [jnp.exp2((score - largest) * (SCALE * LOG2E)) for score in scores]
    totals = sum(jnp.sum(power, axis=0, keepdims=True) for power in powers)
    inverse = 1.0 / totals
    probs = [power * inverse for power in powers]
    d_probs = [dot_nt(value, g) for value in values]
    deltas = sum(jnp.sum(p * d, axis=0, keepdims=True) for p, d in zip(probs, d_probs))
    d_scores = [(p * (d - deltas)).astype(BF) for p, d in zip(probs, d_probs)]
    d_q = sum(dot_tn(d, key) for d, key in zip(d_scores, keys)) * SCALE
    d_keys = [dot_nn(d, q) * SCALE for d in d_scores]
    d_values = [dot_nn(p.astype(BF), g) for p in probs]
    return d_q, d_keys, d_values


def own_body(
    cls_ref, band_ref, gain_ref, inv_ref, q_ref, k_ref, v_ref, g_ref, after_ref, dq_ref, fin_ref, halo_ref, done_ref
):
    slots, _ = head_slots(cls_ref, band_ref)
    inv = inv_ref[...]
    done_ref[...] = inv
    cols = columns(slots[0])
    q = normed(q_ref[:, cols], spread(inv, 0), gain_ref[0, pl.ds(slots[0], 1), :])
    k_inv = spread(inv, 2)
    k = normed(k_ref[:, cols], k_inv, gain_ref[1, pl.ds(slots[0], 1), :])
    d_q, d_k, d_v = attend(q, g_ref[:, cols], [k], [v_ref[:, cols]], [None])
    dq_ref[...] = d_q.astype(BF)
    fin_ref[0] = d_k[0].astype(BF)
    fin_ref[1] = d_v[0].astype(BF)
    for s in (1, 2):
        at = columns(slots[s])
        halo_ref[2 * s - 2] = normed(k_ref[:, at], k_inv, gain_ref[1, pl.ds(slots[s], 1), :])
        halo_ref[2 * s - 1] = v_ref[:, at]


def spatial_body(
    cls_ref,
    band_ref,
    frame_ref,
    gain_ref,
    inv_ref,
    inv_far_ref,
    q_ref,
    g_ref,
    halo_ref,
    near_ref,
    far_ref,
    dq_ref,
    own_ref,
    to_near_ref,
    to_far_ref,
    tick_ref,
):
    slots, bands = head_slots(cls_ref, band_ref)
    frame = frame_ref[0]
    q_inv = spread(inv_ref[...], 0)
    far_inv = spread(inv_far_ref[...], 2)
    far_total = jnp.zeros((TOK, HD), F32)
    for s in (1, 2):
        cols = columns(slots[s])
        q = normed(q_ref[:, cols], q_inv, gain_ref[0, pl.ds(slots[s], 1), :])
        at = 2 * s - 2
        wide = bands[s - 1] > 0
        k_gain = gain_ref[1, pl.ds(slots[s], 1), :]
        far = normed(far_ref[at], far_inv, k_gain)
        keys = [near_ref[at], halo_ref[at], far]
        values = [near_ref[at + 1], halo_ref[at + 1], far_ref[at + 1]]
        allowed = [wide, None, wide & (frame > 0) & (frame < FRAMES - 1)]
        d_q, d_k, d_v = attend(q, g_ref[:, cols], keys, values, allowed)
        dq_ref[s - 1] = d_q.astype(BF)
        to_near_ref[at] = d_k[0].astype(BF)
        to_near_ref[at + 1] = d_v[0].astype(BF)
        own_ref[at] = d_k[1]
        own_ref[at + 1] = d_v[1]
        to_far_ref[at] = d_k[2].astype(BF)
        to_far_ref[at + 1] = d_v[2].astype(BF)
        far_total += k_gain * d_k[2] * far_ref[at].astype(F32)
    tick_ref[...] = lane_sums(far_total)


def temporal_body(in_ref, after_ref, out_ref):
    rows = FRAMES * 8
    q, k, v, g = (in_ref[:, a].reshape(rows, HD) for a in range(4))
    d_k = jnp.zeros((rows, HD), F32)
    d_v = jnp.zeros((rows, HD), F32)
    step = 256
    for part in range(rows // step):
        q_part, g_part = q[part * step : (part + 1) * step], g[part * step : (part + 1) * step]
        key_tile = lax.broadcasted_iota(jnp.int32, (rows, step), 0) & 4
        query_tile = lax.broadcasted_iota(jnp.int32, (rows, step), 1) & 4
        d_q, d_keys, d_values = attend(q_part, g_part, [k], [v], [key_tile == query_tile])
        frames = step // 8
        out_ref[part * frames : (part + 1) * frames, 0] = d_q.astype(BF).reshape(frames, 8, HD)
        d_k += d_keys[0]
        d_v += d_values[0]
    out_ref[:, 1] = d_k.astype(BF).reshape(FRAMES, 8, HD)
    out_ref[:, 2] = d_v.astype(BF).reshape(FRAMES, 8, HD)


def product(gain_ref, which, slot, grad, ref):
    gain = gain_ref[which, pl.ds(slot, 1), :]
    return gain * grad.astype(F32) * ref[:, columns(slot)].astype(F32)


def spatial_sums_body(
    cls_ref, band_ref, gain_ref, q_ref, k_ref, dq0_ref, dq_ref, fin_ref, own_ref, near_ref, part_ref
):
    slots, _ = head_slots(cls_ref, band_ref)
    q_total = product(gain_ref, 0, slots[0], dq0_ref[...], q_ref)
    k_total = product(gain_ref, 1, slots[0], fin_ref[0], k_ref)
    for s in (1, 2):
        at = 2 * s - 2
        q_total += product(gain_ref, 0, slots[s], dq_ref[s - 1], q_ref)
        k_total += product(gain_ref, 1, slots[s], own_ref[at] + near_ref[at].astype(F32), k_ref)
    part_ref[0] = q_total
    part_ref[1] = k_total


def inner_body(cls_ref, band_ref, gain_ref, q_ref, k_ref, back_ref, part_ref, tick_ref, out_ref):
    slots, _ = head_slots(cls_ref, band_ref)
    sums = []
    for which, ref in enumerate((q_ref, k_ref)):
        total = part_ref[which]
        for s in range(2):
            grad = back_ref[s * 32 : (s + 1) * 32, which].reshape(TOK, HD)
            total += product(gain_ref, which, slots[3 + s], grad, ref)
        sums.append(lane_sums(total))
    sums[1] += tick_ref[...]
    out_ref[...] = jnp.broadcast_to(rows_of(*sums)[None], (8, 8, HD))


def final_body(
    cls_ref,
    band_ref,
    gain_ref,
    inv_ref,
    inner_ref,
    q_ref,
    k_ref,
    back_ref,
    dq0_ref,
    dq_ref,
    fin_ref,
    own_ref,
    far_ref,
    near_ref,
    out_q_ref,
    out_k_ref,
    out_v_ref,
):
    slots, _ = head_slots(cls_ref, band_ref)
    inv = inv_ref[...]
    grads = [
        (own_ref[at] + far_ref[at].astype(F32) + near_ref[at].astype(F32)).astype(BF)
        for at in range(4)
    ]
    pull = inv * inv * inv * jnp.sum(inner_ref[...], axis=0) / FULL
    for which, (ref, out) in enumerate(((q_ref, out_q_ref), (k_ref, out_k_ref))):
        inverse, pulled = spread(inv, 2 * which), spread(pull, 2 * which)
        for s in range(HEADS_DEV):
            if s >= 3:
                grad = back_ref[(s - 3) * 32 : (s - 2) * 32, which].reshape(TOK, HD)
            elif which == 0:
                grad = dq0_ref[...] if s == 0 else dq_ref[s - 1]
            else:
                grad = fin_ref[0] if s == 0 else grads[2 * s - 2]
            gain = gain_ref[which, pl.ds(slots[s], 1), :]
            at = columns(slots[s])
            out[:, at] = (
                inverse * gain * grad.astype(F32) - ref[:, at].astype(F32) * pulled
            ).astype(BF)
    out_v_ref[:, columns(slots[0])] = fin_ref[1]
    for s in (1, 2):
        out_v_ref[:, columns(slots[s])] = grads[2 * s - 1]
    for s in range(2):
        out_v_ref[:, columns(slots[3 + s])] = back_ref[s * 32 : (s + 1) * 32, 2].reshape(TOK, HD)


def per_device(query_pre, key_pre, value, d_out, gain_q, gain_k, head_class, head_band):
    frame = lax.axis_index("seq").astype(jnp.int32).reshape(1)
    core = [(i, i ^ 1) for i in range(FRAMES)]
    chip = [(i, ((i - 1) ^ 1) + 1) for i in range(1, FRAMES - 1)]
    block = (4, TOK, HD)

    sums = pl.pallas_call(
        squares_body,
        out_shape=shape((8, 8, HD), F32),
        in_specs=[ANY] * 2,
        out_specs=VM,
        scratch_shapes=[pltpu.VMEM((TOK, WIDTH), BF)] * 2 + [pltpu.SemaphoreType.DMA((2,))],
        name="squares",
        compiler_params=pltpu.CompilerParams(vmem_limit_bytes=56 << 20),
    )(query_pre, key_pre)
    halo = call(halo_body, shape(block, BF), [SM, SM, ANY, VM, VM], "halo", 2)(
        head_class, head_band, sums, key_pre, value
    )
    far = lax.ppermute(halo, "seq", chip)
    gains = call(gains_body, shape((2, HEADS_DEV, HD), F32), [VM, VM, ANY, VM], "gains", 8)(
        gain_q.reshape(HEADS_DEV, HD), gain_k.reshape(HEADS_DEV, HD), sums, d_out
    )
    sums = lax.all_to_all(sums, "head", 0, 0, tiled=True)
    send, inv = call(
        norm_body,
        (shape((FRAMES, 4, 8, HD), BF), shape((8, HD), F32)),
        [SM, SM] + [VM] * 6,
        "norm",
        2,
    )(head_class, head_band, sums, gains, query_pre, key_pre, value, d_out)
    held = lax.all_to_all(send, "seq", 0, 0, tiled=True)
    inv_far = lax.ppermute(inv, "seq", chip)
    dq0, fin, halo, done = call(
        own_body,
        (
            shape((TOK, HD), BF),
            shape((2, TOK, HD), BF),
            shape(block, BF),
            shape((8, HD), F32),
        ),
        [SM, SM] + [VM] * 6 + [ANY],
        "own",
        10,
    )(head_class, head_band, gains, inv, query_pre, key_pre, value, d_out, far)
    near = lax.ppermute(halo, "seq", core)
    dq, own, to_near, to_far, tick = call(
        spatial_body,
        (
            shape((2, TOK, HD), BF),
            shape(block, F32),
            shape(block, BF),
            shape(block, BF),
            shape((8, TOK), F32),
        ),
        [SM] * 3 + [VM] * 8,
        "spatial",
        6,
    )(
        head_class, head_band, frame, gains, inv, inv_far, query_pre, d_out, halo, near, far
    )
    tick = lax.ppermute(tick, "seq", chip)
    from_far = lax.ppermute(to_far, "seq", chip)
    from_near = lax.ppermute(to_near, "seq", core)
    grads = call(temporal_body, shape((FRAMES, 3, 8, HD), BF), [VM, ANY], "temporal", 3)(held, done)
    back = lax.all_to_all(grads, "seq", 0, 0, tiled=True)
    part = call(
        spatial_sums_body, shape((2, TOK, HD), F32), [SM, SM] + [VM] * 8, "spatial_sums", 3
    )(head_class, head_band, gains, query_pre, key_pre, dq0, dq, fin, own, from_near)
    inner = call(inner_body, shape((8, 8, HD), F32), [SM, SM] + [VM] * 6, "inner", 2)(
        head_class, head_band, gains, query_pre, key_pre, back, part, tick
    )
    inner = lax.all_to_all(inner, "head", 0, 0, tiled=True)
    return call(
        final_body,
        (shape((TOK, WIDTH), BF),) * 3,
        [SM, SM] + [VM] * 12,
        "final",
        3,
    )(
        head_class,
        head_band,
        gains,
        inv,
        inner,
        query_pre,
        key_pre,
        back,
        dq0,
        dq,
        fin,
        own,
        from_far,
        from_near,
    )


def solution(mesh):
    whole = P("seq", "head")
    return jax.shard_map(
        per_device,
        mesh=mesh,
        in_specs=(whole,) * 4 + (P("head"),) * 4,
        out_specs=(whole,) * 3,
        check_vma=False,
    )
```

```python
import functools
import math

import jax
import jax.numpy as jnp
from jax import lax
from jax.experimental import pallas as pl
from jax.experimental.pallas import tpu as pltpu
from jax.sharding import PartitionSpec as P

HD = 128
TOK = 256
HEADS_DEV = 5
FRAMES = 64
WIDTH = HEADS_DEV * HD
FULL = 5120
EPSILON = 1e-06
SCALE = 1.0 / math.sqrt(HD)
NEG = -1e30
LOG2E = math.log2(math.e)

BF = jnp.bfloat16
F32 = jnp.float32
VM = pl.BlockSpec(memory_space=pltpu.VMEM)
SM = pl.BlockSpec(memory_space=pltpu.SMEM)
ANY = pl.BlockSpec(memory_space=pl.ANY)


def shape(dims, dtype):
    return jax.ShapeDtypeStruct(dims, dtype)


def call(body, outs, specs, name, micros, mib=24):
    return pl.pallas_call(
        body,
        out_shape=outs,
        in_specs=specs,
        out_specs=jax.tree.map(lambda _: VM, outs),
        name=name,
        compiler_params=pltpu.CompilerParams(vmem_limit_bytes=mib << 20),
        cost_estimate=pl.CostEstimate(
            flops=int(micros * 1e9), bytes_accessed=int(micros * 1e6), transcendentals=0
        ),
    )


def head_slots(cls_ref, band_ref):
    kinds = [cls_ref[i] for i in range(HEADS_DEV)]
    bands = [band_ref[i] for i in range(HEADS_DEV)]
    zero = jnp.int32(0)
    first = zero
    for i in reversed(range(HEADS_DEV)):
        first = jnp.where((kinds[i] == 0) & (bands[i] == 0), i, first)
    second, third, band_2, band_3, temp_0, temp_1 = zero, zero, zero, zero, zero, zero
    for i in reversed(range(HEADS_DEV)):
        other = (kinds[i] == 0) & (first != i)
        second = jnp.where(other, i, second)
        band_2 = jnp.where(other, bands[i], band_2)
        temp_0 = jnp.where(kinds[i] != 0, i, temp_0)
    for i in range(HEADS_DEV):
        other = (kinds[i] == 0) & (first != i)
        third = jnp.where(other, i, third)
        band_3 = jnp.where(other, bands[i], band_3)
        temp_1 = jnp.where(kinds[i] != 0, i, temp_1)
    return (first, second, third, temp_0, temp_1), (band_2, band_3)


def columns(slot):
    return pl.ds(pl.multiple_of(slot * HD, HD), HD)


def dot_nt(a, b):
    return lax.dot_general(a, b, (((1,), (1,)), ((), ())), preferred_element_type=F32)


def dot_tn(a, b):
    return lax.dot_general(a, b, (((0,), (0,)), ((), ())), preferred_element_type=F32)


def dot_nn(a, b):
    return lax.dot_general(a, b, (((1,), (0,)), ((), ())), preferred_element_type=F32)


def rows_of(q_row, k_row):
    at = lax.broadcasted_iota(jnp.int32, (8, HD), 0)
    return jnp.where(
        at == 0,
        q_row[:, :HD],
        jnp.where(at == 1, q_row[:, HD:], jnp.where(at == 2, k_row[:, :HD], k_row[:, HD:])),
    )


def spread(rows, at):
    low = jnp.broadcast_to(rows[at : at + 1], (HD, HD)).T
    high = jnp.broadcast_to(rows[at + 1 : at + 2], (HD, HD)).T
    return jnp.concatenate([low, high], axis=0)


def lane_sums(values):
    return jnp.broadcast_to(jnp.sum(values.T, axis=0, keepdims=True), (8, values.shape[0]))


def inverses(sums_ref):
    return lax.rsqrt(jnp.sum(sums_ref[...], axis=0) / FULL + EPSILON)


def squares_body(q_hbm, k_hbm, out_ref, q_ref, k_ref, sems):
    copies = [
        pltpu.make_async_copy(source, target, sems.at[i])
        for i, (source, target) in enumerate(((q_hbm, q_ref), (k_hbm, k_ref)))
    ]
    for copy in copies:
        copy.start()
    sums = []
    for copy, ref in zip(copies, (q_ref, k_ref)):
        copy.wait()
        total = jnp.zeros((TOK, HD), F32)
        for head in range(HEADS_DEV):
            wide = ref[:, head * HD : (head + 1) * HD].astype(F32)
            total += wide * wide
        sums.append(lane_sums(total))
    out_ref[...] = jnp.broadcast_to(rows_of(*sums)[None], (8, 8, HD))


def halo_body(cls_ref, band_ref, after_ref, k_ref, v_ref, halo_ref):
    slots, _ = head_slots(cls_ref, band_ref)
    for s in (1, 2):
        halo_ref[2 * s - 2] = k_ref[:, columns(slots[s])]
        halo_ref[2 * s - 1] = v_ref[:, columns(slots[s])]


def gains_body(q_ref, k_ref, after_ref, g_ref, out_ref):
    out_ref[0] = q_ref[...].astype(F32)
    out_ref[1] = k_ref[...].astype(F32)


def normed(values, inverse, gain):
    return (values.astype(F32) * inverse * gain).astype(BF)


def norm_body(
    cls_ref, band_ref, sums_ref, gain_ref, q_ref, k_ref, v_ref, g_ref, send_ref, inv_ref
):
    slots, _ = head_slots(cls_ref, band_ref)
    inv = inverses(sums_ref)
    inv_ref[...] = inv
    q_inv, k_inv = spread(inv, 0), spread(inv, 2)
    for s in range(2):
        slot = slots[3 + s]
        at = columns(slot)
        parts = (
            normed(q_ref[:, at], q_inv, gain_ref[0, pl.ds(slot, 1), :]),
            normed(k_ref[:, at], k_inv, gain_ref[1, pl.ds(slot, 1), :]),
            v_ref[:, at],
            g_ref[:, at],
        )
        for a, part in enumerate(parts):
            send_ref[s * 32 : (s + 1) * 32, a] = part.reshape(32, 8, HD)


def attend(q, g, keys, values, allowed):
    scores = []
    for key, ok in zip(keys, allowed):
        score = dot_nt(key, q)
        scores.append(score if ok is None else jnp.where(ok, score, NEG))
    largest = functools.reduce(
        jnp.maximum, [jnp.max(score, axis=0, keepdims=True) for score in scores]
    )
    powers = [jnp.exp2((score - largest) * (SCALE * LOG2E)) for score in scores]
    totals = sum(jnp.sum(power, axis=0, keepdims=True) for power in powers)
    inverse = 1.0 / totals
    probs = [power * inverse for power in powers]
    d_probs = [dot_nt(value, g) for value in values]
    deltas = sum(jnp.sum(p * d, axis=0, keepdims=True) for p, d in zip(probs, d_probs))
    d_scores = [(p * (d - deltas)).astype(BF) for p, d in zip(probs, d_probs)]
    d_q = sum(dot_tn(d, key) for d, key in zip(d_scores, keys)) * SCALE
    d_keys = [dot_nn(d, q) * SCALE for d in d_scores]
    d_values = [dot_nn(p.astype(BF), g) for p in probs]
    return d_q, d_keys, d_values


def own_body(
    cls_ref, band_ref, gain_ref, inv_ref, q_ref, k_ref, v_ref, g_ref, after_ref, dq_ref, fin_ref, halo_ref, done_ref
):
    slots, _ = head_slots(cls_ref, band_ref)
    inv = inv_ref[...]
    done_ref[...] = inv
    cols = columns(slots[0])
    q = normed(q_ref[:, cols], spread(inv, 0), gain_ref[0, pl.ds(slots[0], 1), :])
    k_inv = spread(inv, 2)
    k = normed(k_ref[:, cols], k_inv, gain_ref[1, pl.ds(slots[0], 1), :])
    d_q, d_k, d_v = attend(q, g_ref[:, cols], [k], [v_ref[:, cols]], [None])
    dq_ref[...] = d_q.astype(BF)
    fin_ref[0] = d_k[0].astype(BF)
    fin_ref[1] = d_v[0].astype(BF)
    for s in (1, 2):
        at = columns(slots[s])
        halo_ref[2 * s - 2] = normed(k_ref[:, at], k_inv, gain_ref[1, pl.ds(slots[s], 1), :])
        halo_ref[2 * s - 1] = v_ref[:, at]


def spatial_body(
    cls_ref,
    band_ref,
    frame_ref,
    gain_ref,
    inv_ref,
    inv_far_ref,
    q_ref,
    g_ref,
    halo_ref,
    near_ref,
    far_ref,
    dq_ref,
    own_ref,
    to_near_ref,
    to_far_ref,
    tick_ref,
):
    slots, bands = head_slots(cls_ref, band_ref)
    frame = frame_ref[0]
    q_inv = spread(inv_ref[...], 0)
    far_inv = spread(inv_far_ref[...], 2)
    far_total = jnp.zeros((TOK, HD), F32)
    for s in (1, 2):
        cols = columns(slots[s])
        q = normed(q_ref[:, cols], q_inv, gain_ref[0, pl.ds(slots[s], 1), :])
        at = 2 * s - 2
        wide = bands[s - 1] > 0
        k_gain = gain_ref[1, pl.ds(slots[s], 1), :]
        far = normed(far_ref[at], far_inv, k_gain)
        keys = [near_ref[at], halo_ref[at], far]
        values = [near_ref[at + 1], halo_ref[at + 1], far_ref[at + 1]]
        allowed = [wide, None, wide & (frame > 0) & (frame < FRAMES - 1)]
        d_q, d_k, d_v = attend(q, g_ref[:, cols], keys, values, allowed)
        dq_ref[s - 1] = d_q.astype(BF)
        to_near_ref[at] = d_k[0].astype(BF)
        to_near_ref[at + 1] = d_v[0].astype(BF)
        own_ref[at] = d_k[1]
        own_ref[at + 1] = d_v[1]
        to_far_ref[at] = d_k[2].astype(BF)
        to_far_ref[at + 1] = d_v[2].astype(BF)
        far_total += k_gain * d_k[2] * far_ref[at].astype(F32)
    tick_ref[...] = lane_sums(far_total)


def temporal_body(in_ref, after_ref, out_ref):
    rows = FRAMES * 8
    q, k, v, g = (in_ref[:, a].reshape(rows, HD) for a in range(4))
    d_k = jnp.zeros((rows, HD), F32)
    d_v = jnp.zeros((rows, HD), F32)
    step = 512
    for part in range(rows // step):
        q_part, g_part = q[part * step : (part + 1) * step], g[part * step : (part + 1) * step]
        key_tile = lax.broadcasted_iota(jnp.int32, (rows, step), 0) & 4
        query_tile = lax.broadcasted_iota(jnp.int32, (rows, step), 1) & 4
        d_q, d_keys, d_values = attend(q_part, g_part, [k], [v], [key_tile == query_tile])
        frames = step // 8
        out_ref[part * frames : (part + 1) * frames, 0] = d_q.astype(BF).reshape(frames, 8, HD)
        d_k += d_keys[0]
        d_v += d_values[0]
    out_ref[:, 1] = d_k.astype(BF).reshape(FRAMES, 8, HD)
    out_ref[:, 2] = d_v.astype(BF).reshape(FRAMES, 8, HD)


def product(gain_ref, which, slot, grad, ref):
    gain = gain_ref[which, pl.ds(slot, 1), :]
    return gain * grad.astype(F32) * ref[:, columns(slot)].astype(F32)


def spatial_sums_body(
    cls_ref,
    band_ref,
    gain_ref,
    q_ref,
    k_ref,
    dq0_ref,
    dq_ref,
    fin_ref,
    own_ref,
    tick_ref,
    near_ref,
    part_ref,
):
    slots, _ = head_slots(cls_ref, band_ref)
    q_total = product(gain_ref, 0, slots[0], dq0_ref[...], q_ref)
    k_total = product(gain_ref, 1, slots[0], fin_ref[0], k_ref)
    for s in (1, 2):
        at = 2 * s - 2
        q_total += product(gain_ref, 0, slots[s], dq_ref[s - 1], q_ref)
        k_total += product(gain_ref, 1, slots[s], own_ref[at] + near_ref[at].astype(F32), k_ref)
    part_ref[0] = lane_sums(q_total)
    part_ref[1] = lane_sums(k_total) + tick_ref[...]


def inner_body(cls_ref, band_ref, gain_ref, q_ref, k_ref, back_ref, part_ref, out_ref):
    slots, _ = head_slots(cls_ref, band_ref)
    sums = []
    for which, ref in enumerate((q_ref, k_ref)):
        total = jnp.zeros((TOK, HD), F32)
        for s in range(2):
            grad = back_ref[s * 32 : (s + 1) * 32, which].reshape(TOK, HD)
            total += product(gain_ref, which, slots[3 + s], grad, ref)
        sums.append(lane_sums(total) + part_ref[which])
    out_ref[...] = jnp.broadcast_to(rows_of(*sums)[None], (8, 8, HD))


def final_body(
    cls_ref,
    band_ref,
    gain_ref,
    inv_ref,
    inner_ref,
    q_ref,
    k_ref,
    back_ref,
    dq0_ref,
    dq_ref,
    fin_ref,
    own_ref,
    far_ref,
    near_ref,
    out_q_ref,
    out_k_ref,
    out_v_ref,
):
    slots, _ = head_slots(cls_ref, band_ref)
    inv = inv_ref[...]
    grads = [
        (own_ref[at] + far_ref[at].astype(F32) + near_ref[at].astype(F32)).astype(BF)
        for at in range(4)
    ]
    pull = inv * inv * inv * jnp.sum(inner_ref[...], axis=0) / FULL
    for which, (ref, out) in enumerate(((q_ref, out_q_ref), (k_ref, out_k_ref))):
        inverse, pulled = spread(inv, 2 * which), spread(pull, 2 * which)
        for s in range(HEADS_DEV):
            if s >= 3:
                grad = back_ref[(s - 3) * 32 : (s - 2) * 32, which].reshape(TOK, HD)
            elif which == 0:
                grad = dq0_ref[...] if s == 0 else dq_ref[s - 1]
            else:
                grad = fin_ref[0] if s == 0 else grads[2 * s - 2]
            gain = gain_ref[which, pl.ds(slots[s], 1), :]
            at = columns(slots[s])
            out[:, at] = (
                inverse * gain * grad.astype(F32) - ref[:, at].astype(F32) * pulled
            ).astype(BF)
    out_v_ref[:, columns(slots[0])] = fin_ref[1]
    for s in (1, 2):
        out_v_ref[:, columns(slots[s])] = grads[2 * s - 1]
    for s in range(2):
        out_v_ref[:, columns(slots[3 + s])] = back_ref[s * 32 : (s + 1) * 32, 2].reshape(TOK, HD)


def per_device(query_pre, key_pre, value, d_out, gain_q, gain_k, head_class, head_band):
    frame = lax.axis_index("seq").astype(jnp.int32).reshape(1)
    core = [(i, i ^ 1) for i in range(FRAMES)]
    chip = [(i, ((i - 1) ^ 1) + 1) for i in range(1, FRAMES - 1)]
    block = (4, TOK, HD)

    sums = pl.pallas_call(
        squares_body,
        out_shape=shape((8, 8, HD), F32),
        in_specs=[ANY] * 2,
        out_specs=VM,
        scratch_shapes=[pltpu.VMEM((TOK, WIDTH), BF)] * 2 + [pltpu.SemaphoreType.DMA((2,))],
        name="squares",
        compiler_params=pltpu.CompilerParams(vmem_limit_bytes=56 << 20),
    )(query_pre, key_pre)
    halo = call(halo_body, shape(block, BF), [SM, SM, ANY, VM, VM], "halo", 2)(
        head_class, head_band, sums, key_pre, value
    )
    far = lax.ppermute(halo, "seq", chip)
    gains = call(gains_body, shape((2, HEADS_DEV, HD), F32), [VM, VM, ANY, VM], "gains", 8)(
        gain_q.reshape(HEADS_DEV, HD), gain_k.reshape(HEADS_DEV, HD), sums, d_out
    )
    sums = lax.all_to_all(sums, "head", 0, 0, tiled=True)
    send, inv = call(
        norm_body,
        (shape((FRAMES, 4, 8, HD), BF), shape((8, HD), F32)),
        [SM, SM] + [VM] * 6,
        "norm",
        2,
    )(head_class, head_band, sums, gains, query_pre, key_pre, value, d_out)
    held = lax.all_to_all(send, "seq", 0, 0, tiled=True)
    inv_far = lax.ppermute(inv, "seq", chip)
    dq0, fin, halo, done = call(
        own_body,
        (
            shape((TOK, HD), BF),
            shape((2, TOK, HD), BF),
            shape(block, BF),
            shape((8, HD), F32),
        ),
        [SM, SM] + [VM] * 6 + [ANY],
        "own",
        10,
    )(head_class, head_band, gains, inv, query_pre, key_pre, value, d_out, far)
    near = lax.ppermute(halo, "seq", core)
    dq, own, to_near, to_far, tick = call(
        spatial_body,
        (
            shape((2, TOK, HD), BF),
            shape(block, F32),
            shape(block, BF),
            shape(block, BF),
            shape((8, TOK), F32),
        ),
        [SM] * 3 + [VM] * 8,
        "spatial",
        6,
    )(
        head_class, head_band, frame, gains, inv, inv_far, query_pre, d_out, halo, near, far
    )
    tick = lax.ppermute(tick, "seq", chip)
    from_far = lax.ppermute(to_far, "seq", chip)
    from_near = lax.ppermute(to_near, "seq", core)
    grads = call(temporal_body, shape((FRAMES, 3, 8, HD), BF), [VM, ANY], "temporal", 3)(held, done)
    back = lax.all_to_all(grads, "seq", 0, 0, tiled=True)
    part = call(
        spatial_sums_body, shape((2, 8, TOK), F32), [SM, SM] + [VM] * 9, "spatial_sums", 3
    )(head_class, head_band, gains, query_pre, key_pre, dq0, dq, fin, own, tick, from_near)
    inner = call(inner_body, shape((8, 8, HD), F32), [SM, SM] + [VM] * 5, "inner", 2)(
        head_class, head_band, gains, query_pre, key_pre, back, part
    )
    inner = lax.all_to_all(inner, "head", 0, 0, tiled=True)
    return call(
        final_body,
        (shape((TOK, WIDTH), BF),) * 3,
        [SM, SM] + [VM] * 12,
        "final",
        3,
    )(
        head_class,
        head_band,
        gains,
        inv,
        inner,
        query_pre,
        key_pre,
        back,
        dq0,
        dq,
        fin,
        own,
        from_far,
        from_near,
    )


def solution(mesh):
    whole = P("seq", "head")
    return jax.shard_map(
        per_device,
        mesh=mesh,
        in_specs=(whole,) * 4 + (P("head"),) * 4,
        out_specs=(whole,) * 3,
        check_vma=False,
    )
```

```python
import functools
import math

import jax
import jax.numpy as jnp
from jax import lax
from jax.experimental import pallas as pl
from jax.experimental.pallas import tpu as pltpu
from jax.sharding import PartitionSpec as P

HD = 128
TOK = 256
HEADS_DEV = 5
FRAMES = 64
WIDTH = HEADS_DEV * HD
FULL = 5120
EPSILON = 1e-06
SCALE = 1.0 / math.sqrt(HD)
NEG = -1e30
LOG2E = math.log2(math.e)

BF = jnp.bfloat16
F32 = jnp.float32
VM = pl.BlockSpec(memory_space=pltpu.VMEM)
SM = pl.BlockSpec(memory_space=pltpu.SMEM)
ANY = pl.BlockSpec(memory_space=pl.ANY)


def shape(dims, dtype):
    return jax.ShapeDtypeStruct(dims, dtype)


def call(body, outs, specs, name, micros, mib=24):
    return pl.pallas_call(
        body,
        out_shape=outs,
        in_specs=specs,
        out_specs=jax.tree.map(lambda _: VM, outs),
        name=name,
        compiler_params=pltpu.CompilerParams(vmem_limit_bytes=mib << 20),
        cost_estimate=pl.CostEstimate(
            flops=int(micros * 1e9), bytes_accessed=int(micros * 1e6), transcendentals=0
        ),
    )


def head_slots(cls_ref, band_ref):
    kinds = [cls_ref[i] for i in range(HEADS_DEV)]
    bands = [band_ref[i] for i in range(HEADS_DEV)]
    zero = jnp.int32(0)
    first = zero
    for i in reversed(range(HEADS_DEV)):
        first = jnp.where((kinds[i] == 0) & (bands[i] == 0), i, first)
    second, third, band_2, band_3, temp_0, temp_1 = zero, zero, zero, zero, zero, zero
    for i in reversed(range(HEADS_DEV)):
        other = (kinds[i] == 0) & (first != i)
        second = jnp.where(other, i, second)
        band_2 = jnp.where(other, bands[i], band_2)
        temp_0 = jnp.where(kinds[i] != 0, i, temp_0)
    for i in range(HEADS_DEV):
        other = (kinds[i] == 0) & (first != i)
        third = jnp.where(other, i, third)
        band_3 = jnp.where(other, bands[i], band_3)
        temp_1 = jnp.where(kinds[i] != 0, i, temp_1)
    return (first, second, third, temp_0, temp_1), (band_2, band_3)


def columns(slot):
    return pl.ds(pl.multiple_of(slot * HD, HD), HD)


def dot_nt(a, b):
    return lax.dot_general(a, b, (((1,), (1,)), ((), ())), preferred_element_type=F32)


def dot_tn(a, b):
    return lax.dot_general(a, b, (((0,), (0,)), ((), ())), preferred_element_type=F32)


def dot_nn(a, b):
    return lax.dot_general(a, b, (((1,), (0,)), ((), ())), preferred_element_type=F32)


def rows_of(q_row, k_row):
    at = lax.broadcasted_iota(jnp.int32, (8, HD), 0)
    return jnp.where(
        at == 0,
        q_row[:, :HD],
        jnp.where(at == 1, q_row[:, HD:], jnp.where(at == 2, k_row[:, :HD], k_row[:, HD:])),
    )


def spread(rows, at):
    low = jnp.broadcast_to(rows[at : at + 1], (HD, HD)).T
    high = jnp.broadcast_to(rows[at + 1 : at + 2], (HD, HD)).T
    return jnp.concatenate([low, high], axis=0)


def lane_sums(values):
    return jnp.broadcast_to(jnp.sum(values.T, axis=0, keepdims=True), (8, values.shape[0]))


def inverses(sums_ref):
    return lax.rsqrt(jnp.sum(sums_ref[...], axis=0) / FULL + EPSILON)


def squares_body(q_hbm, k_hbm, out_ref, q_ref, k_ref, sems):
    copies = [
        pltpu.make_async_copy(source, target, sems.at[i])
        for i, (source, target) in enumerate(((q_hbm, q_ref), (k_hbm, k_ref)))
    ]
    for copy in copies:
        copy.start()
    sums = []
    for copy, ref in zip(copies, (q_ref, k_ref)):
        copy.wait()
        total = jnp.zeros((TOK, HD), F32)
        for head in range(HEADS_DEV):
            wide = ref[:, head * HD : (head + 1) * HD].astype(F32)
            total += wide * wide
        sums.append(lane_sums(total))
    out_ref[...] = jnp.broadcast_to(rows_of(*sums)[None], (8, 8, HD))


def halo_body(cls_ref, band_ref, after_ref, k_ref, v_ref, halo_ref):
    slots, _ = head_slots(cls_ref, band_ref)
    for s in (1, 2):
        halo_ref[2 * s - 2] = k_ref[:, columns(slots[s])]
        halo_ref[2 * s - 1] = v_ref[:, columns(slots[s])]


def gains_body(q_ref, k_ref, after_ref, next_ref, g_ref, out_ref):
    out_ref[0] = q_ref[...].astype(F32)
    out_ref[1] = k_ref[...].astype(F32)


def normed(values, inverse, gain):
    return (values.astype(F32) * inverse * gain).astype(BF)


def norm_body(
    cls_ref, band_ref, sums_ref, gain_ref, q_ref, k_ref, v_ref, g_ref, send_ref, inv_ref
):
    slots, _ = head_slots(cls_ref, band_ref)
    inv = inverses(sums_ref)
    inv_ref[...] = inv
    q_inv, k_inv = spread(inv, 0), spread(inv, 2)
    for s in range(2):
        slot = slots[3 + s]
        at = columns(slot)
        parts = (
            normed(q_ref[:, at], q_inv, gain_ref[0, pl.ds(slot, 1), :]),
            normed(k_ref[:, at], k_inv, gain_ref[1, pl.ds(slot, 1), :]),
            v_ref[:, at],
            g_ref[:, at],
        )
        for a, part in enumerate(parts):
            send_ref[s * 32 : (s + 1) * 32, a] = part.reshape(32, 8, HD)


def attend(q, g, keys, values, allowed):
    scores = []
    for key, ok in zip(keys, allowed):
        score = dot_nt(key, q)
        scores.append(score if ok is None else jnp.where(ok, score, NEG))
    largest = functools.reduce(
        jnp.maximum, [jnp.max(score, axis=0, keepdims=True) for score in scores]
    )
    powers = [jnp.exp2((score - largest) * (SCALE * LOG2E)) for score in scores]
    totals = sum(jnp.sum(power, axis=0, keepdims=True) for power in powers)
    inverse = 1.0 / totals
    probs = [power * inverse for power in powers]
    d_probs = [dot_nt(value, g) for value in values]
    deltas = sum(jnp.sum(p * d, axis=0, keepdims=True) for p, d in zip(probs, d_probs))
    d_scores = [(p * (d - deltas)).astype(BF) for p, d in zip(probs, d_probs)]
    d_q = sum(dot_tn(d, key) for d, key in zip(d_scores, keys)) * SCALE
    d_keys = [dot_nn(d, q) * SCALE for d in d_scores]
    d_values = [dot_nn(p.astype(BF), g) for p in probs]
    return d_q, d_keys, d_values


def own_body(
    cls_ref, band_ref, gain_ref, inv_ref, q_ref, k_ref, v_ref, g_ref, after_ref, dq_ref, fin_ref, halo_ref, done_ref
):
    slots, _ = head_slots(cls_ref, band_ref)
    inv = inv_ref[...]
    done_ref[...] = inv
    cols = columns(slots[0])
    q = normed(q_ref[:, cols], spread(inv, 0), gain_ref[0, pl.ds(slots[0], 1), :])
    k_inv = spread(inv, 2)
    k = normed(k_ref[:, cols], k_inv, gain_ref[1, pl.ds(slots[0], 1), :])
    d_q, d_k, d_v = attend(q, g_ref[:, cols], [k], [v_ref[:, cols]], [None])
    dq_ref[...] = d_q.astype(BF)
    fin_ref[0] = d_k[0].astype(BF)
    fin_ref[1] = d_v[0].astype(BF)
    for s in (1, 2):
        at = columns(slots[s])
        halo_ref[2 * s - 2] = normed(k_ref[:, at], k_inv, gain_ref[1, pl.ds(slots[s], 1), :])
        halo_ref[2 * s - 1] = v_ref[:, at]


def spatial_body(
    cls_ref,
    band_ref,
    frame_ref,
    gain_ref,
    inv_ref,
    inv_far_ref,
    q_ref,
    g_ref,
    halo_ref,
    near_ref,
    far_ref,
    dq_ref,
    own_ref,
    to_near_ref,
    to_far_ref,
    tick_ref,
):
    slots, bands = head_slots(cls_ref, band_ref)
    frame = frame_ref[0]
    q_inv = spread(inv_ref[...], 0)
    far_inv = spread(inv_far_ref[...], 2)
    far_total = jnp.zeros((TOK, HD), F32)
    for s in (1, 2):
        cols = columns(slots[s])
        q = normed(q_ref[:, cols], q_inv, gain_ref[0, pl.ds(slots[s], 1), :])
        at = 2 * s - 2
        wide = bands[s - 1] > 0
        k_gain = gain_ref[1, pl.ds(slots[s], 1), :]
        far = normed(far_ref[at], far_inv, k_gain)
        keys = [near_ref[at], halo_ref[at], far]
        values = [near_ref[at + 1], halo_ref[at + 1], far_ref[at + 1]]
        allowed = [wide, None, wide & (frame > 0) & (frame < FRAMES - 1)]
        d_q, d_k, d_v = attend(q, g_ref[:, cols], keys, values, allowed)
        dq_ref[s - 1] = d_q.astype(BF)
        to_near_ref[at] = d_k[0].astype(BF)
        to_near_ref[at + 1] = d_v[0].astype(BF)
        own_ref[at] = d_k[1]
        own_ref[at + 1] = d_v[1]
        to_far_ref[at] = d_k[2].astype(BF)
        to_far_ref[at + 1] = d_v[2].astype(BF)
        far_total += k_gain * d_k[2] * far_ref[at].astype(F32)
    tick_ref[...] = lane_sums(far_total)


def temporal_body(in_ref, after_ref, out_ref):
    rows = FRAMES * 8
    q, k, v, g = (in_ref[:, a].reshape(rows, HD) for a in range(4))
    d_k = jnp.zeros((rows, HD), F32)
    d_v = jnp.zeros((rows, HD), F32)
    step = 512
    for part in range(rows // step):
        q_part, g_part = q[part * step : (part + 1) * step], g[part * step : (part + 1) * step]
        key_tile = lax.broadcasted_iota(jnp.int32, (rows, step), 0) & 4
        query_tile = lax.broadcasted_iota(jnp.int32, (rows, step), 1) & 4
        d_q, d_keys, d_values = attend(q_part, g_part, [k], [v], [key_tile == query_tile])
        frames = step // 8
        out_ref[part * frames : (part + 1) * frames, 0] = d_q.astype(BF).reshape(frames, 8, HD)
        d_k += d_keys[0]
        d_v += d_values[0]
    out_ref[:, 1] = d_k.astype(BF).reshape(FRAMES, 8, HD)
    out_ref[:, 2] = d_v.astype(BF).reshape(FRAMES, 8, HD)


def product(gain_ref, which, slot, grad, ref):
    gain = gain_ref[which, pl.ds(slot, 1), :]
    return gain * grad.astype(F32) * ref[:, columns(slot)].astype(F32)


def spatial_sums_body(
    cls_ref,
    band_ref,
    gain_ref,
    q_ref,
    k_ref,
    dq0_ref,
    dq_ref,
    fin_ref,
    own_ref,
    tick_ref,
    near_ref,
    part_ref,
):
    slots, _ = head_slots(cls_ref, band_ref)
    q_total = product(gain_ref, 0, slots[0], dq0_ref[...], q_ref)
    k_total = product(gain_ref, 1, slots[0], fin_ref[0], k_ref)
    for s in (1, 2):
        at = 2 * s - 2
        q_total += product(gain_ref, 0, slots[s], dq_ref[s - 1], q_ref)
        k_total += product(gain_ref, 1, slots[s], own_ref[at] + near_ref[at].astype(F32), k_ref)
    part_ref[0] = lane_sums(q_total)
    part_ref[1] = lane_sums(k_total) + tick_ref[...]


def inner_body(cls_ref, band_ref, gain_ref, q_ref, k_ref, back_ref, part_ref, out_ref):
    slots, _ = head_slots(cls_ref, band_ref)
    sums = []
    for which, ref in enumerate((q_ref, k_ref)):
        total = jnp.zeros((TOK, HD), F32)
        for s in range(2):
            grad = back_ref[s * 32 : (s + 1) * 32, which].reshape(TOK, HD)
            total += product(gain_ref, which, slots[3 + s], grad, ref)
        sums.append(lane_sums(total) + part_ref[which])
    out_ref[...] = jnp.broadcast_to(rows_of(*sums)[None], (8, 8, HD))


def final_body(
    cls_ref,
    band_ref,
    gain_ref,
    inv_ref,
    inner_ref,
    q_ref,
    k_ref,
    back_ref,
    dq0_ref,
    dq_ref,
    fin_ref,
    own_ref,
    far_ref,
    near_ref,
    out_q_ref,
    out_k_ref,
    out_v_ref,
):
    slots, _ = head_slots(cls_ref, band_ref)
    inv = inv_ref[...]
    grads = [
        (own_ref[at] + far_ref[at].astype(F32) + near_ref[at].astype(F32)).astype(BF)
        for at in range(4)
    ]
    pull = inv * inv * inv * jnp.sum(inner_ref[...], axis=0) / FULL
    for which, (ref, out) in enumerate(((q_ref, out_q_ref), (k_ref, out_k_ref))):
        inverse, pulled = spread(inv, 2 * which), spread(pull, 2 * which)
        for s in range(HEADS_DEV):
            if s >= 3:
                grad = back_ref[(s - 3) * 32 : (s - 2) * 32, which].reshape(TOK, HD)
            elif which == 0:
                grad = dq0_ref[...] if s == 0 else dq_ref[s - 1]
            else:
                grad = fin_ref[0] if s == 0 else grads[2 * s - 2]
            gain = gain_ref[which, pl.ds(slots[s], 1), :]
            at = columns(slots[s])
            out[:, at] = (
                inverse * gain * grad.astype(F32) - ref[:, at].astype(F32) * pulled
            ).astype(BF)
    out_v_ref[:, columns(slots[0])] = fin_ref[1]
    for s in (1, 2):
        out_v_ref[:, columns(slots[s])] = grads[2 * s - 1]
    for s in range(2):
        out_v_ref[:, columns(slots[3 + s])] = back_ref[s * 32 : (s + 1) * 32, 2].reshape(TOK, HD)


def per_device(query_pre, key_pre, value, d_out, gain_q, gain_k, head_class, head_band):
    frame = lax.axis_index("seq").astype(jnp.int32).reshape(1)
    core = [(i, i ^ 1) for i in range(FRAMES)]
    chip = [(i, ((i - 1) ^ 1) + 1) for i in range(1, FRAMES - 1)]
    block = (4, TOK, HD)

    sums = pl.pallas_call(
        squares_body,
        out_shape=shape((8, 8, HD), F32),
        in_specs=[ANY] * 2,
        out_specs=VM,
        scratch_shapes=[pltpu.VMEM((TOK, WIDTH), BF)] * 2 + [pltpu.SemaphoreType.DMA((2,))],
        name="squares",
        compiler_params=pltpu.CompilerParams(vmem_limit_bytes=56 << 20),
    )(query_pre, key_pre)
    halo = call(halo_body, shape(block, BF), [SM, SM, ANY, VM, VM], "halo", 2)(
        head_class, head_band, sums, key_pre, value
    )
    far = lax.ppermute(halo, "seq", chip)
    gains = call(gains_body, shape((2, HEADS_DEV, HD), F32), [VM, VM, ANY, VM, VM], "gains", 8)(
        gain_q.reshape(HEADS_DEV, HD), gain_k.reshape(HEADS_DEV, HD), sums, query_pre, d_out
    )
    sums = lax.all_to_all(sums, "head", 0, 0, tiled=True)
    send, inv = call(
        norm_body,
        (shape((FRAMES, 4, 8, HD), BF), shape((8, HD), F32)),
        [SM, SM] + [VM] * 6,
        "norm",
        2,
    )(head_class, head_band, sums, gains, query_pre, key_pre, value, d_out)
    held = lax.all_to_all(send, "seq", 0, 0, tiled=True)
    inv_far = lax.ppermute(inv, "seq", chip)
    dq0, fin, halo, done = call(
        own_body,
        (
            shape((TOK, HD), BF),
            shape((2, TOK, HD), BF),
            shape(block, BF),
            shape((8, HD), F32),
        ),
        [SM, SM] + [VM] * 6 + [ANY],
        "own",
        10,
    )(head_class, head_band, gains, inv, query_pre, key_pre, value, d_out, far)
    near = lax.ppermute(halo, "seq", core)
    dq, own, to_near, to_far, tick = call(
        spatial_body,
        (
            shape((2, TOK, HD), BF),
            shape(block, F32),
            shape(block, BF),
            shape(block, BF),
            shape((8, TOK), F32),
        ),
        [SM] * 3 + [VM] * 8,
        "spatial",
        6,
    )(
        head_class, head_band, frame, gains, inv, inv_far, query_pre, d_out, halo, near, far
    )
    tick = lax.ppermute(tick, "seq", chip)
    from_far = lax.ppermute(to_far, "seq", chip)
    from_near = lax.ppermute(to_near, "seq", core)
    grads = call(temporal_body, shape((FRAMES, 3, 8, HD), BF), [VM, ANY], "temporal", 3)(held, done)
    back = lax.all_to_all(grads, "seq", 0, 0, tiled=True)
    part = call(
        spatial_sums_body, shape((2, 8, TOK), F32), [SM, SM] + [VM] * 9, "spatial_sums", 3
    )(head_class, head_band, gains, query_pre, key_pre, dq0, dq, fin, own, tick, from_near)
    inner = call(inner_body, shape((8, 8, HD), F32), [SM, SM] + [VM] * 5, "inner", 2)(
        head_class, head_band, gains, query_pre, key_pre, back, part
    )
    inner = lax.all_to_all(inner, "head", 0, 0, tiled=True)
    return call(
        final_body,
        (shape((TOK, WIDTH), BF),) * 3,
        [SM, SM] + [VM] * 12,
        "final",
        3,
    )(
        head_class,
        head_band,
        gains,
        inv,
        inner,
        query_pre,
        key_pre,
        back,
        dq0,
        dq,
        fin,
        own,
        from_far,
        from_near,
    )


def solution(mesh):
    whole = P("seq", "head")
    return jax.shard_map(
        per_device,
        mesh=mesh,
        in_specs=(whole,) * 4 + (P("head"),) * 4,
        out_specs=(whole,) * 3,
        check_vma=False,
    )
```

```python
import functools
import math

import jax
import jax.numpy as jnp
from jax import lax
from jax.experimental import pallas as pl
from jax.experimental.pallas import tpu as pltpu
from jax.sharding import PartitionSpec as P

HD = 128
TOK = 256
HEADS_DEV = 5
FRAMES = 64
WIDTH = HEADS_DEV * HD
FULL = 5120
EPSILON = 1e-06
SCALE = 1.0 / math.sqrt(HD)
NEG = -1e30
LOG2E = math.log2(math.e)

BF = jnp.bfloat16
F32 = jnp.float32
VM = pl.BlockSpec(memory_space=pltpu.VMEM)
SM = pl.BlockSpec(memory_space=pltpu.SMEM)
ANY = pl.BlockSpec(memory_space=pl.ANY)


def shape(dims, dtype):
    return jax.ShapeDtypeStruct(dims, dtype)


def call(body, outs, specs, name, micros, mib=24):
    return pl.pallas_call(
        body,
        out_shape=outs,
        in_specs=specs,
        out_specs=jax.tree.map(lambda _: VM, outs),
        name=name,
        compiler_params=pltpu.CompilerParams(vmem_limit_bytes=mib << 20),
        cost_estimate=pl.CostEstimate(
            flops=int(micros * 1e9), bytes_accessed=int(micros * 1e6), transcendentals=0
        ),
    )


def head_slots(cls_ref, band_ref):
    kinds = [cls_ref[i] for i in range(HEADS_DEV)]
    bands = [band_ref[i] for i in range(HEADS_DEV)]
    zero = jnp.int32(0)
    first = zero
    for i in reversed(range(HEADS_DEV)):
        first = jnp.where((kinds[i] == 0) & (bands[i] == 0), i, first)
    second, third, band_2, band_3, temp_0, temp_1 = zero, zero, zero, zero, zero, zero
    for i in reversed(range(HEADS_DEV)):
        other = (kinds[i] == 0) & (first != i)
        second = jnp.where(other, i, second)
        band_2 = jnp.where(other, bands[i], band_2)
        temp_0 = jnp.where(kinds[i] != 0, i, temp_0)
    for i in range(HEADS_DEV):
        other = (kinds[i] == 0) & (first != i)
        third = jnp.where(other, i, third)
        band_3 = jnp.where(other, bands[i], band_3)
        temp_1 = jnp.where(kinds[i] != 0, i, temp_1)
    return (first, second, third, temp_0, temp_1), (band_2, band_3)


def columns(slot):
    return pl.ds(pl.multiple_of(slot * HD, HD), HD)


def dot_nt(a, b):
    return lax.dot_general(a, b, (((1,), (1,)), ((), ())), preferred_element_type=F32)


def dot_tn(a, b):
    return lax.dot_general(a, b, (((0,), (0,)), ((), ())), preferred_element_type=F32)


def dot_nn(a, b):
    return lax.dot_general(a, b, (((1,), (0,)), ((), ())), preferred_element_type=F32)


def rows_of(q_row, k_row):
    at = lax.broadcasted_iota(jnp.int32, (8, HD), 0)
    return jnp.where(
        at == 0,
        q_row[:, :HD],
        jnp.where(at == 1, q_row[:, HD:], jnp.where(at == 2, k_row[:, :HD], k_row[:, HD:])),
    )


def spread(rows, at):
    low = jnp.broadcast_to(rows[at : at + 1], (HD, HD)).T
    high = jnp.broadcast_to(rows[at + 1 : at + 2], (HD, HD)).T
    return jnp.concatenate([low, high], axis=0)


def lane_sums(values):
    return jnp.broadcast_to(jnp.sum(values.T, axis=0, keepdims=True), (8, values.shape[0]))


def inverses(sums_ref):
    return lax.rsqrt(jnp.sum(sums_ref[...], axis=0) / FULL + EPSILON)


def squares_body(q_hbm, k_hbm, out_ref, q_ref, k_ref, sems):
    copies = [
        pltpu.make_async_copy(source, target, sems.at[i])
        for i, (source, target) in enumerate(((q_hbm, q_ref), (k_hbm, k_ref)))
    ]
    for copy in copies:
        copy.start()
    sums = []
    for copy, ref in zip(copies, (q_ref, k_ref)):
        copy.wait()
        total = jnp.zeros((TOK, HD), F32)
        for head in range(HEADS_DEV):
            wide = ref[:, head * HD : (head + 1) * HD].astype(F32)
            total += wide * wide
        sums.append(lane_sums(total))
    out_ref[...] = jnp.broadcast_to(rows_of(*sums)[None], (8, 8, HD))


def halo_body(cls_ref, band_ref, after_ref, k_ref, v_ref, halo_ref):
    slots, _ = head_slots(cls_ref, band_ref)
    for s in (1, 2):
        halo_ref[2 * s - 2] = k_ref[:, columns(slots[s])]
        halo_ref[2 * s - 1] = v_ref[:, columns(slots[s])]


def gains_body(q_ref, k_ref, after_ref, next_ref, g_ref, out_ref):
    out_ref[0] = q_ref[...].astype(F32)
    out_ref[1] = k_ref[...].astype(F32)


def normed(values, inverse, gain):
    return (values.astype(F32) * inverse * gain).astype(BF)


def norm_body(
    cls_ref,
    band_ref,
    sums_ref,
    gain_ref,
    q_ref,
    k_ref,
    v_ref,
    g_ref,
    send_hbm,
    inv_ref,
    part_ref,
    sems,
):
    slots, _ = head_slots(cls_ref, band_ref)
    copies = []

    def ship(a, s, part):
        part_ref[2 * a + s] = part.reshape(32, 8, HD)
        target = send_hbm.at[s * 32 : (s + 1) * 32, a]
        copy = pltpu.make_async_copy(part_ref.at[2 * a + s], target, sems.at[2 * a + s])
        copy.start()
        copies.append(copy)

    for s in range(2):
        at = columns(slots[3 + s])
        ship(2, s, v_ref[:, at])
        ship(3, s, g_ref[:, at])
    inv = inverses(sums_ref)
    inv_ref[...] = inv
    for a, ref in enumerate((q_ref, k_ref)):
        inverse = spread(inv, 2 * a)
        for s in range(2):
            slot = slots[3 + s]
            ship(a, s, normed(ref[:, columns(slot)], inverse, gain_ref[a, pl.ds(slot, 1), :]))
    for copy in copies:
        copy.wait()


def attend(q, g, keys, values, allowed):
    scores = []
    for key, ok in zip(keys, allowed):
        score = dot_nt(key, q)
        scores.append(score if ok is None else jnp.where(ok, score, NEG))
    largest = functools.reduce(
        jnp.maximum, [jnp.max(score, axis=0, keepdims=True) for score in scores]
    )
    powers = [jnp.exp2((score - largest) * (SCALE * LOG2E)) for score in scores]
    totals = sum(jnp.sum(power, axis=0, keepdims=True) for power in powers)
    inverse = 1.0 / totals
    probs = [power * inverse for power in powers]
    d_probs = [dot_nt(value, g) for value in values]
    deltas = sum(jnp.sum(p * d, axis=0, keepdims=True) for p, d in zip(probs, d_probs))
    d_scores = [(p * (d - deltas)).astype(BF) for p, d in zip(probs, d_probs)]
    d_q = sum(dot_tn(d, key) for d, key in zip(d_scores, keys)) * SCALE
    d_keys = [dot_nn(d, q) * SCALE for d in d_scores]
    d_values = [dot_nn(p.astype(BF), g) for p in probs]
    return d_q, d_keys, d_values


def own_body(
    cls_ref, band_ref, gain_ref, inv_ref, q_ref, k_ref, v_ref, g_ref, after_ref, dq_ref, fin_ref, halo_ref, done_ref
):
    slots, _ = head_slots(cls_ref, band_ref)
    inv = inv_ref[...]
    done_ref[...] = inv
    cols = columns(slots[0])
    q = normed(q_ref[:, cols], spread(inv, 0), gain_ref[0, pl.ds(slots[0], 1), :])
    k_inv = spread(inv, 2)
    k = normed(k_ref[:, cols], k_inv, gain_ref[1, pl.ds(slots[0], 1), :])
    d_q, d_k, d_v = attend(q, g_ref[:, cols], [k], [v_ref[:, cols]], [None])
    dq_ref[...] = d_q.astype(BF)
    fin_ref[0] = d_k[0].astype(BF)
    fin_ref[1] = d_v[0].astype(BF)
    for s in (1, 2):
        at = columns(slots[s])
        halo_ref[2 * s - 2] = normed(k_ref[:, at], k_inv, gain_ref[1, pl.ds(slots[s], 1), :])
        halo_ref[2 * s - 1] = v_ref[:, at]


def spatial_body(
    cls_ref,
    band_ref,
    frame_ref,
    gain_ref,
    inv_ref,
    inv_far_ref,
    q_ref,
    g_ref,
    halo_ref,
    near_ref,
    far_ref,
    dq_ref,
    own_ref,
    to_near_ref,
    to_far_ref,
    tick_ref,
):
    slots, bands = head_slots(cls_ref, band_ref)
    frame = frame_ref[0]
    q_inv = spread(inv_ref[...], 0)
    far_inv = spread(inv_far_ref[...], 2)
    far_total = jnp.zeros((TOK, HD), F32)
    for s in (1, 2):
        cols = columns(slots[s])
        q = normed(q_ref[:, cols], q_inv, gain_ref[0, pl.ds(slots[s], 1), :])
        at = 2 * s - 2
        wide = bands[s - 1] > 0
        k_gain = gain_ref[1, pl.ds(slots[s], 1), :]
        far = normed(far_ref[at], far_inv, k_gain)
        keys = [near_ref[at], halo_ref[at], far]
        values = [near_ref[at + 1], halo_ref[at + 1], far_ref[at + 1]]
        allowed = [wide, None, wide & (frame > 0) & (frame < FRAMES - 1)]
        d_q, d_k, d_v = attend(q, g_ref[:, cols], keys, values, allowed)
        dq_ref[s - 1] = d_q.astype(BF)
        to_near_ref[at] = d_k[0].astype(BF)
        to_near_ref[at + 1] = d_v[0].astype(BF)
        own_ref[at] = d_k[1]
        own_ref[at + 1] = d_v[1]
        to_far_ref[at] = d_k[2].astype(BF)
        to_far_ref[at + 1] = d_v[2].astype(BF)
        far_total += k_gain * d_k[2] * far_ref[at].astype(F32)
    tick_ref[...] = lane_sums(far_total)


def temporal_body(in_ref, after_ref, out_hbm, part_ref, sems):
    rows = FRAMES * 8
    q, k, v, g = (in_ref[:, a].reshape(rows, HD) for a in range(4))
    key_tile = lax.broadcasted_iota(jnp.int32, (rows, rows), 0) & 4
    query_tile = lax.broadcasted_iota(jnp.int32, (rows, rows), 1) & 4
    d_q, d_k, d_v = attend(q, g, [k], [v], [key_tile == query_tile])
    copies = []
    for a, part in ((2, d_v[0]), (1, d_k[0]), (0, d_q)):
        part_ref[a] = part.astype(BF).reshape(FRAMES, 8, HD)
        copy = pltpu.make_async_copy(part_ref.at[a], out_hbm.at[:, a], sems.at[a])
        copy.start()
        copies.append(copy)
    for copy in copies:
        copy.wait()


def product(gain_ref, which, slot, grad, ref):
    gain = gain_ref[which, pl.ds(slot, 1), :]
    return gain * grad.astype(F32) * ref[:, columns(slot)].astype(F32)


def spatial_sums_body(
    cls_ref,
    band_ref,
    gain_ref,
    q_ref,
    k_ref,
    dq0_ref,
    dq_ref,
    fin_ref,
    own_ref,
    tick_ref,
    near_ref,
    part_ref,
):
    slots, _ = head_slots(cls_ref, band_ref)
    q_total = product(gain_ref, 0, slots[0], dq0_ref[...], q_ref)
    k_total = product(gain_ref, 1, slots[0], fin_ref[0], k_ref)
    for s in (1, 2):
        at = 2 * s - 2
        q_total += product(gain_ref, 0, slots[s], dq_ref[s - 1], q_ref)
        k_total += product(gain_ref, 1, slots[s], own_ref[at] + near_ref[at].astype(F32), k_ref)
    part_ref[0] = lane_sums(q_total)
    part_ref[1] = lane_sums(k_total) + tick_ref[...]


def inner_body(cls_ref, band_ref, gain_ref, q_ref, k_ref, back_ref, part_ref, out_ref):
    slots, _ = head_slots(cls_ref, band_ref)
    sums = []
    for which, ref in enumerate((q_ref, k_ref)):
        total = jnp.zeros((TOK, HD), F32)
        for s in range(2):
            grad = back_ref[s * 32 : (s + 1) * 32, which].reshape(TOK, HD)
            total += product(gain_ref, which, slots[3 + s], grad, ref)
        sums.append(lane_sums(total) + part_ref[which])
    out_ref[...] = jnp.broadcast_to(rows_of(*sums)[None], (8, 8, HD))


def final_body(
    cls_ref,
    band_ref,
    gain_ref,
    inv_ref,
    inner_ref,
    q_ref,
    k_ref,
    back_ref,
    dq0_ref,
    dq_ref,
    fin_ref,
    own_ref,
    far_ref,
    near_ref,
    out_q_ref,
    out_k_ref,
    out_v_ref,
):
    slots, _ = head_slots(cls_ref, band_ref)
    inv = inv_ref[...]
    grads = [
        (own_ref[at] + far_ref[at].astype(F32) + near_ref[at].astype(F32)).astype(BF)
        for at in range(4)
    ]
    pull = inv * inv * inv * jnp.sum(inner_ref[...], axis=0) / FULL
    for which, (ref, out) in enumerate(((q_ref, out_q_ref), (k_ref, out_k_ref))):
        inverse, pulled = spread(inv, 2 * which), spread(pull, 2 * which)
        for s in range(HEADS_DEV):
            if s >= 3:
                grad = back_ref[(s - 3) * 32 : (s - 2) * 32, which].reshape(TOK, HD)
            elif which == 0:
                grad = dq0_ref[...] if s == 0 else dq_ref[s - 1]
            else:
                grad = fin_ref[0] if s == 0 else grads[2 * s - 2]
            gain = gain_ref[which, pl.ds(slots[s], 1), :]
            at = columns(slots[s])
            out[:, at] = (
                inverse * gain * grad.astype(F32) - ref[:, at].astype(F32) * pulled
            ).astype(BF)
    out_v_ref[:, columns(slots[0])] = fin_ref[1]
    for s in (1, 2):
        out_v_ref[:, columns(slots[s])] = grads[2 * s - 1]
    for s in range(2):
        out_v_ref[:, columns(slots[3 + s])] = back_ref[s * 32 : (s + 1) * 32, 2].reshape(TOK, HD)


def per_device(query_pre, key_pre, value, d_out, gain_q, gain_k, head_class, head_band):
    frame = lax.axis_index("seq").astype(jnp.int32).reshape(1)
    core = [(i, i ^ 1) for i in range(FRAMES)]
    chip = [(i, ((i - 1) ^ 1) + 1) for i in range(1, FRAMES - 1)]
    block = (4, TOK, HD)

    sums = pl.pallas_call(
        squares_body,
        out_shape=shape((8, 8, HD), F32),
        in_specs=[ANY] * 2,
        out_specs=VM,
        scratch_shapes=[pltpu.VMEM((TOK, WIDTH), BF)] * 2 + [pltpu.SemaphoreType.DMA((2,))],
        name="squares",
        compiler_params=pltpu.CompilerParams(vmem_limit_bytes=56 << 20),
    )(query_pre, key_pre)
    halo = call(halo_body, shape(block, BF), [SM, SM, ANY, VM, VM], "halo", 2)(
        head_class, head_band, sums, key_pre, value
    )
    far = lax.ppermute(halo, "seq", chip)
    gains = call(gains_body, shape((2, HEADS_DEV, HD), F32), [VM, VM, ANY, VM, VM], "gains", 8)(
        gain_q.reshape(HEADS_DEV, HD), gain_k.reshape(HEADS_DEV, HD), sums, query_pre, d_out
    )
    sums = lax.all_to_all(sums, "head", 0, 0, tiled=True)
    send, inv = pl.pallas_call(
        norm_body,
        out_shape=(shape((FRAMES, 4, 8, HD), BF), shape((8, HD), F32)),
        in_specs=[SM, SM] + [VM] * 6,
        out_specs=(ANY, VM),
        scratch_shapes=[pltpu.VMEM((8, 32, 8, HD), BF), pltpu.SemaphoreType.DMA((8,))],
        name="norm",
        compiler_params=pltpu.CompilerParams(vmem_limit_bytes=24 << 20),
        cost_estimate=pl.CostEstimate(
            flops=int(2e9), bytes_accessed=int(2e6), transcendentals=0
        ),
    )(head_class, head_band, sums, gains, query_pre, key_pre, value, d_out)
    held = lax.all_to_all(send, "seq", 0, 0, tiled=True)
    inv_far = lax.ppermute(inv, "seq", chip)
    dq0, fin, halo, done = call(
        own_body,
        (
            shape((TOK, HD), BF),
            shape((2, TOK, HD), BF),
            shape(block, BF),
            shape((8, HD), F32),
        ),
        [SM, SM] + [VM] * 6 + [ANY],
        "own",
        10,
    )(head_class, head_band, gains, inv, query_pre, key_pre, value, d_out, far)
    near = lax.ppermute(halo, "seq", core)
    dq, own, to_near, to_far, tick = call(
        spatial_body,
        (
            shape((2, TOK, HD), BF),
            shape(block, F32),
            shape(block, BF),
            shape(block, BF),
            shape((8, TOK), F32),
        ),
        [SM] * 3 + [VM] * 8,
        "spatial",
        6,
    )(
        head_class, head_band, frame, gains, inv, inv_far, query_pre, d_out, halo, near, far
    )
    tick = lax.ppermute(tick, "seq", chip)
    from_far = lax.ppermute(to_far, "seq", chip)
    from_near = lax.ppermute(to_near, "seq", core)
    grads = pl.pallas_call(
        temporal_body,
        out_shape=shape((FRAMES, 3, 8, HD), BF),
        in_specs=[VM, ANY],
        out_specs=ANY,
        scratch_shapes=[pltpu.VMEM((3, FRAMES, 8, HD), BF), pltpu.SemaphoreType.DMA((3,))],
        name="temporal",
        compiler_params=pltpu.CompilerParams(vmem_limit_bytes=24 << 20),
        cost_estimate=pl.CostEstimate(
            flops=int(3e9), bytes_accessed=int(3e6), transcendentals=0
        ),
    )(held, done)
    back = lax.all_to_all(grads, "seq", 0, 0, tiled=True)
    part = call(
        spatial_sums_body, shape((2, 8, TOK), F32), [SM, SM] + [VM] * 9, "spatial_sums", 3
    )(head_class, head_band, gains, query_pre, key_pre, dq0, dq, fin, own, tick, from_near)
    inner = call(inner_body, shape((8, 8, HD), F32), [SM, SM] + [VM] * 5, "inner", 2)(
        head_class, head_band, gains, query_pre, key_pre, back, part
    )
    inner = lax.all_to_all(inner, "head", 0, 0, tiled=True)
    return call(
        final_body,
        (shape((TOK, WIDTH), BF),) * 3,
        [SM, SM] + [VM] * 12,
        "final",
        3,
    )(
        head_class,
        head_band,
        gains,
        inv,
        inner,
        query_pre,
        key_pre,
        back,
        dq0,
        dq,
        fin,
        own,
        from_far,
        from_near,
    )


def solution(mesh):
    whole = P("seq", "head")
    return jax.shard_map(
        per_device,
        mesh=mesh,
        in_specs=(whole,) * 4 + (P("head"),) * 4,
        out_specs=(whole,) * 3,
        check_vma=False,
    )
```

```python
import functools
import math

import jax
import jax.numpy as jnp
from jax import lax
from jax.experimental import pallas as pl
from jax.experimental.pallas import tpu as pltpu
from jax.sharding import PartitionSpec as P

HD = 128
TOK = 256
HEADS_DEV = 5
FRAMES = 64
WIDTH = HEADS_DEV * HD
FULL = 5120
EPSILON = 1e-06
SCALE = 1.0 / math.sqrt(HD)
NEG = -1e30
LOG2E = math.log2(math.e)

BF = jnp.bfloat16
F32 = jnp.float32
VM = pl.BlockSpec(memory_space=pltpu.VMEM)
SM = pl.BlockSpec(memory_space=pltpu.SMEM)
ANY = pl.BlockSpec(memory_space=pl.ANY)


def shape(dims, dtype):
    return jax.ShapeDtypeStruct(dims, dtype)


def call(body, outs, specs, name, micros, mib=24):
    return pl.pallas_call(
        body,
        out_shape=outs,
        in_specs=specs,
        out_specs=jax.tree.map(lambda _: VM, outs),
        name=name,
        compiler_params=pltpu.CompilerParams(vmem_limit_bytes=mib << 20),
        cost_estimate=pl.CostEstimate(
            flops=int(micros * 1e9), bytes_accessed=int(micros * 1e6), transcendentals=0
        ),
    )


def head_slots(cls_ref, band_ref):
    kinds = [cls_ref[i] for i in range(HEADS_DEV)]
    bands = [band_ref[i] for i in range(HEADS_DEV)]
    zero = jnp.int32(0)
    first = zero
    for i in reversed(range(HEADS_DEV)):
        first = jnp.where((kinds[i] == 0) & (bands[i] == 0), i, first)
    second, third, band_2, band_3, temp_0, temp_1 = zero, zero, zero, zero, zero, zero
    for i in reversed(range(HEADS_DEV)):
        other = (kinds[i] == 0) & (first != i)
        second = jnp.where(other, i, second)
        band_2 = jnp.where(other, bands[i], band_2)
        temp_0 = jnp.where(kinds[i] != 0, i, temp_0)
    for i in range(HEADS_DEV):
        other = (kinds[i] == 0) & (first != i)
        third = jnp.where(other, i, third)
        band_3 = jnp.where(other, bands[i], band_3)
        temp_1 = jnp.where(kinds[i] != 0, i, temp_1)
    return (first, second, third, temp_0, temp_1), (band_2, band_3)


def columns(slot):
    return pl.ds(pl.multiple_of(slot * HD, HD), HD)


def dot_nt(a, b):
    return lax.dot_general(a, b, (((1,), (1,)), ((), ())), preferred_element_type=F32)


def dot_tn(a, b):
    return lax.dot_general(a, b, (((0,), (0,)), ((), ())), preferred_element_type=F32)


def dot_nn(a, b):
    return lax.dot_general(a, b, (((1,), (0,)), ((), ())), preferred_element_type=F32)


def rows_of(q_row, k_row):
    at = lax.broadcasted_iota(jnp.int32, (8, HD), 0)
    return jnp.where(
        at == 0,
        q_row[:, :HD],
        jnp.where(at == 1, q_row[:, HD:], jnp.where(at == 2, k_row[:, :HD], k_row[:, HD:])),
    )


def spread(rows, at):
    low = jnp.broadcast_to(rows[at : at + 1], (HD, HD)).T
    high = jnp.broadcast_to(rows[at + 1 : at + 2], (HD, HD)).T
    return jnp.concatenate([low, high], axis=0)


def lane_sums(values):
    return jnp.broadcast_to(jnp.sum(values.T, axis=0, keepdims=True), (8, values.shape[0]))


def inverses(sums_ref):
    return lax.rsqrt(jnp.sum(sums_ref[...], axis=0) / FULL + EPSILON)


def squares_body(q_hbm, k_hbm, out_ref, q_ref, k_ref, sems):
    copies = [
        pltpu.make_async_copy(source, target, sems.at[i])
        for i, (source, target) in enumerate(((q_hbm, q_ref), (k_hbm, k_ref)))
    ]
    for copy in copies:
        copy.start()
    sums = []
    for copy, ref in zip(copies, (q_ref, k_ref)):
        copy.wait()
        total = jnp.zeros((TOK, HD), F32)
        for head in range(HEADS_DEV):
            wide = ref[:, head * HD : (head + 1) * HD].astype(F32)
            total += wide * wide
        sums.append(lane_sums(total))
    out_ref[...] = jnp.broadcast_to(rows_of(*sums)[None], (8, 8, HD))


def halo_body(cls_ref, band_ref, after_ref, k_ref, v_ref, halo_ref):
    slots, _ = head_slots(cls_ref, band_ref)
    for s in (1, 2):
        halo_ref[2 * s - 2] = k_ref[:, columns(slots[s])]
        halo_ref[2 * s - 1] = v_ref[:, columns(slots[s])]


def gains_body(q_ref, k_ref, after_ref, next_ref, g_ref, out_ref):
    out_ref[0] = q_ref[...].astype(F32)
    out_ref[1] = k_ref[...].astype(F32)


def normed(values, inverse, gain):
    return (values.astype(F32) * inverse * gain).astype(BF)


def norm_body(
    cls_ref, band_ref, sums_ref, gain_ref, q_ref, k_ref, v_ref, g_ref, send_ref, inv_ref
):
    slots, _ = head_slots(cls_ref, band_ref)
    inv = inverses(sums_ref)
    inv_ref[...] = inv
    q_inv, k_inv = spread(inv, 0), spread(inv, 2)
    for s in range(2):
        slot = slots[3 + s]
        at = columns(slot)
        parts = (
            normed(q_ref[:, at], q_inv, gain_ref[0, pl.ds(slot, 1), :]),
            normed(k_ref[:, at], k_inv, gain_ref[1, pl.ds(slot, 1), :]),
            v_ref[:, at],
            g_ref[:, at],
        )
        for a, part in enumerate(parts):
            send_ref[s * 32 : (s + 1) * 32, a] = part.reshape(32, 8, HD)


def attend(q, g, keys, values, allowed):
    scores = []
    for key, ok in zip(keys, allowed):
        score = dot_nt(key, q)
        scores.append(score if ok is None else jnp.where(ok, score, NEG))
    largest = functools.reduce(
        jnp.maximum, [jnp.max(score, axis=0, keepdims=True) for score in scores]
    )
    powers = [jnp.exp2((score - largest) * (SCALE * LOG2E)) for score in scores]
    totals = sum(jnp.sum(power, axis=0, keepdims=True) for power in powers)
    inverse = 1.0 / totals
    probs = [power * inverse for power in powers]
    d_probs = [dot_nt(value, g) for value in values]
    deltas = sum(jnp.sum(p * d, axis=0, keepdims=True) for p, d in zip(probs, d_probs))
    d_scores = [(p * (d - deltas)).astype(BF) for p, d in zip(probs, d_probs)]
    d_q = sum(dot_tn(d, key) for d, key in zip(d_scores, keys)) * SCALE
    d_keys = [dot_nn(d, q) * SCALE for d in d_scores]
    d_values = [dot_nn(p.astype(BF), g) for p in probs]
    return d_q, d_keys, d_values


def own_body(
    cls_ref, band_ref, gain_ref, inv_ref, q_ref, k_ref, v_ref, g_ref, after_ref, dq_ref, fin_ref, halo_ref, done_ref
):
    slots, _ = head_slots(cls_ref, band_ref)
    inv = inv_ref[...]
    done_ref[...] = inv
    cols = columns(slots[0])
    q = normed(q_ref[:, cols], spread(inv, 0), gain_ref[0, pl.ds(slots[0], 1), :])
    k_inv = spread(inv, 2)
    k = normed(k_ref[:, cols], k_inv, gain_ref[1, pl.ds(slots[0], 1), :])
    d_q, d_k, d_v = attend(q, g_ref[:, cols], [k], [v_ref[:, cols]], [None])
    dq_ref[...] = d_q.astype(BF)
    fin_ref[0] = d_k[0].astype(BF)
    fin_ref[1] = d_v[0].astype(BF)
    for s in (1, 2):
        at = columns(slots[s])
        halo_ref[2 * s - 2] = normed(k_ref[:, at], k_inv, gain_ref[1, pl.ds(slots[s], 1), :])
        halo_ref[2 * s - 1] = v_ref[:, at]


def spatial_body(
    cls_ref,
    band_ref,
    frame_ref,
    gain_ref,
    inv_ref,
    inv_far_ref,
    q_ref,
    g_ref,
    halo_ref,
    near_ref,
    far_ref,
    dq_ref,
    own_ref,
    to_near_ref,
    to_far_ref,
    tick_ref,
    sum_ref,
):
    slots, bands = head_slots(cls_ref, band_ref)
    frame = frame_ref[0]
    q_inv = spread(inv_ref[...], 0)
    far_inv = spread(inv_far_ref[...], 2)
    far_total = jnp.zeros((TOK, HD), F32)
    q_total = jnp.zeros((TOK, HD), F32)
    for s in (1, 2):
        cols = columns(slots[s])
        q = normed(q_ref[:, cols], q_inv, gain_ref[0, pl.ds(slots[s], 1), :])
        at = 2 * s - 2
        wide = bands[s - 1] > 0
        k_gain = gain_ref[1, pl.ds(slots[s], 1), :]
        far = normed(far_ref[at], far_inv, k_gain)
        keys = [near_ref[at], halo_ref[at], far]
        values = [near_ref[at + 1], halo_ref[at + 1], far_ref[at + 1]]
        allowed = [wide, None, wide & (frame > 0) & (frame < FRAMES - 1)]
        d_q, d_k, d_v = attend(q, g_ref[:, cols], keys, values, allowed)
        d_q = d_q.astype(BF)
        dq_ref[s - 1] = d_q
        q_total += product(gain_ref, 0, slots[s], d_q, q_ref)
        to_near_ref[at] = d_k[0].astype(BF)
        to_near_ref[at + 1] = d_v[0].astype(BF)
        own_ref[at] = d_k[1]
        own_ref[at + 1] = d_v[1]
        to_far_ref[at] = d_k[2].astype(BF)
        to_far_ref[at + 1] = d_v[2].astype(BF)
        far_total += k_gain * d_k[2] * far_ref[at].astype(F32)
    tick_ref[...] = lane_sums(far_total)
    sum_ref[...] = lane_sums(q_total)


def temporal_body(in_ref, after_ref, out_ref):
    rows = FRAMES * 8
    q, k, v, g = (in_ref[:, a].reshape(rows, HD) for a in range(4))
    d_k = jnp.zeros((rows, HD), F32)
    d_v = jnp.zeros((rows, HD), F32)
    step = 512
    for part in range(rows // step):
        q_part, g_part = q[part * step : (part + 1) * step], g[part * step : (part + 1) * step]
        key_tile = lax.broadcasted_iota(jnp.int32, (rows, step), 0) & 4
        query_tile = lax.broadcasted_iota(jnp.int32, (rows, step), 1) & 4
        d_q, d_keys, d_values = attend(q_part, g_part, [k], [v], [key_tile == query_tile])
        frames = step // 8
        out_ref[part * frames : (part + 1) * frames, 0] = d_q.astype(BF).reshape(frames, 8, HD)
        d_k += d_keys[0]
        d_v += d_values[0]
    out_ref[:, 1] = d_k.astype(BF).reshape(FRAMES, 8, HD)
    out_ref[:, 2] = d_v.astype(BF).reshape(FRAMES, 8, HD)


def product(gain_ref, which, slot, grad, ref):
    gain = gain_ref[which, pl.ds(slot, 1), :]
    return gain * grad.astype(F32) * ref[:, columns(slot)].astype(F32)


def spatial_sums_body(
    cls_ref,
    band_ref,
    gain_ref,
    q_ref,
    k_ref,
    dq0_ref,
    q_part_ref,
    fin_ref,
    own_ref,
    tick_ref,
    near_ref,
    part_ref,
):
    slots, _ = head_slots(cls_ref, band_ref)
    q_total = product(gain_ref, 0, slots[0], dq0_ref[...], q_ref)
    k_total = product(gain_ref, 1, slots[0], fin_ref[0], k_ref)
    for s in (1, 2):
        at = 2 * s - 2
        k_total += product(gain_ref, 1, slots[s], own_ref[at] + near_ref[at].astype(F32), k_ref)
    part_ref[0] = lane_sums(q_total) + q_part_ref[...]
    part_ref[1] = lane_sums(k_total) + tick_ref[...]


def inner_body(cls_ref, band_ref, gain_ref, q_ref, k_ref, back_ref, part_ref, out_ref):
    slots, _ = head_slots(cls_ref, band_ref)
    sums = []
    for which, ref in enumerate((q_ref, k_ref)):
        total = jnp.zeros((TOK, HD), F32)
        for s in range(2):
            grad = back_ref[s * 32 : (s + 1) * 32, which].reshape(TOK, HD)
            total += product(gain_ref, which, slots[3 + s], grad, ref)
        sums.append(lane_sums(total) + part_ref[which])
    out_ref[...] = jnp.broadcast_to(rows_of(*sums)[None], (8, 8, HD))


def final_body(
    cls_ref,
    band_ref,
    gain_ref,
    inv_ref,
    inner_ref,
    q_ref,
    k_ref,
    back_ref,
    dq0_ref,
    dq_ref,
    fin_ref,
    own_ref,
    far_ref,
    near_ref,
    out_q_ref,
    out_k_ref,
    out_v_ref,
):
    slots, _ = head_slots(cls_ref, band_ref)
    inv = inv_ref[...]
    grads = [
        (own_ref[at] + far_ref[at].astype(F32) + near_ref[at].astype(F32)).astype(BF)
        for at in range(4)
    ]
    pull = inv * inv * inv * jnp.sum(inner_ref[...], axis=0) / FULL
    for which, (ref, out) in enumerate(((q_ref, out_q_ref), (k_ref, out_k_ref))):
        inverse, pulled = spread(inv, 2 * which), spread(pull, 2 * which)
        for s in range(HEADS_DEV):
            if s >= 3:
                grad = back_ref[(s - 3) * 32 : (s - 2) * 32, which].reshape(TOK, HD)
            elif which == 0:
                grad = dq0_ref[...] if s == 0 else dq_ref[s - 1]
            else:
                grad = fin_ref[0] if s == 0 else grads[2 * s - 2]
            gain = gain_ref[which, pl.ds(slots[s], 1), :]
            at = columns(slots[s])
            out[:, at] = (
                inverse * gain * grad.astype(F32) - ref[:, at].astype(F32) * pulled
            ).astype(BF)
    out_v_ref[:, columns(slots[0])] = fin_ref[1]
    for s in (1, 2):
        out_v_ref[:, columns(slots[s])] = grads[2 * s - 1]
    for s in range(2):
        out_v_ref[:, columns(slots[3 + s])] = back_ref[s * 32 : (s + 1) * 32, 2].reshape(TOK, HD)


def per_device(query_pre, key_pre, value, d_out, gain_q, gain_k, head_class, head_band):
    frame = lax.axis_index("seq").astype(jnp.int32).reshape(1)
    core = [(i, i ^ 1) for i in range(FRAMES)]
    chip = [(i, ((i - 1) ^ 1) + 1) for i in range(1, FRAMES - 1)]
    block = (4, TOK, HD)

    sums = pl.pallas_call(
        squares_body,
        out_shape=shape((8, 8, HD), F32),
        in_specs=[ANY] * 2,
        out_specs=VM,
        scratch_shapes=[pltpu.VMEM((TOK, WIDTH), BF)] * 2 + [pltpu.SemaphoreType.DMA((2,))],
        name="squares",
        compiler_params=pltpu.CompilerParams(vmem_limit_bytes=56 << 20),
    )(query_pre, key_pre)
    halo = call(halo_body, shape(block, BF), [SM, SM, ANY, VM, VM], "halo", 2)(
        head_class, head_band, sums, key_pre, value
    )
    far = lax.ppermute(halo, "seq", chip)
    gains = call(gains_body, shape((2, HEADS_DEV, HD), F32), [VM, VM, ANY, VM, VM], "gains", 8)(
        gain_q.reshape(HEADS_DEV, HD), gain_k.reshape(HEADS_DEV, HD), sums, query_pre, d_out
    )
    sums = lax.all_to_all(sums, "head", 0, 0, tiled=True)
    send, inv = call(
        norm_body,
        (shape((FRAMES, 4, 8, HD), BF), shape((8, HD), F32)),
        [SM, SM] + [VM] * 6,
        "norm",
        2,
    )(head_class, head_band, sums, gains, query_pre, key_pre, value, d_out)
    held = lax.all_to_all(send, "seq", 0, 0, tiled=True)
    inv_far = lax.ppermute(inv, "seq", chip)
    dq0, fin, halo, done = call(
        own_body,
        (
            shape((TOK, HD), BF),
            shape((2, TOK, HD), BF),
            shape(block, BF),
            shape((8, HD), F32),
        ),
        [SM, SM] + [VM] * 6 + [ANY],
        "own",
        10,
    )(head_class, head_band, gains, inv, query_pre, key_pre, value, d_out, far)
    near = lax.ppermute(halo, "seq", core)
    dq, own, to_near, to_far, tick, q_part = call(
        spatial_body,
        (
            shape((2, TOK, HD), BF),
            shape(block, F32),
            shape(block, BF),
            shape(block, BF),
            shape((8, TOK), F32),
            shape((8, TOK), F32),
        ),
        [SM] * 3 + [VM] * 8,
        "spatial",
        6,
    )(
        head_class, head_band, frame, gains, inv, inv_far, query_pre, d_out, halo, near, far
    )
    tick = lax.ppermute(tick, "seq", chip)
    from_far = lax.ppermute(to_far, "seq", chip)
    from_near = lax.ppermute(to_near, "seq", core)
    grads = call(temporal_body, shape((FRAMES, 3, 8, HD), BF), [VM, ANY], "temporal", 3)(held, done)
    back = lax.all_to_all(grads, "seq", 0, 0, tiled=True)
    part = call(
        spatial_sums_body, shape((2, 8, TOK), F32), [SM, SM] + [VM] * 9, "spatial_sums", 3
    )(head_class, head_band, gains, query_pre, key_pre, dq0, q_part, fin, own, tick, from_near)
    inner = call(inner_body, shape((8, 8, HD), F32), [SM, SM] + [VM] * 5, "inner", 2)(
        head_class, head_band, gains, query_pre, key_pre, back, part
    )
    inner = lax.all_to_all(inner, "head", 0, 0, tiled=True)
    return call(
        final_body,
        (shape((TOK, WIDTH), BF),) * 3,
        [SM, SM] + [VM] * 12,
        "final",
        3,
    )(
        head_class,
        head_band,
        gains,
        inv,
        inner,
        query_pre,
        key_pre,
        back,
        dq0,
        dq,
        fin,
        own,
        from_far,
        from_near,
    )


def solution(mesh):
    whole = P("seq", "head")
    return jax.shard_map(
        per_device,
        mesh=mesh,
        in_specs=(whole,) * 4 + (P("head"),) * 4,
        out_specs=(whole,) * 3,
        check_vma=False,
    )
```
